128 devices in a mesh: dp: 128 (over z, y, x, core).
Axes of the slice: x: 4, y: 4, z: 4, core: 2. Of those that a mesh axis runs over, the one named last changes fastest.
Arguments:
- tokens: bfloat16 [16384, 2048], P('dp'), may hold values from -6 to 6
- seq_lengths: int32 [128, 3], P('dp'), may hold values from 1 to 96, 128 in all within a row
- attn_norm: bfloat16 [2048], P('dp'), may hold values from 0.5 to 1.5
- w_query: bfloat16 [2048, 2048], P('dp'), may hold values from -0.125 to 0.125
- w_key: bfloat16 [2048, 256], P('dp'), may hold values from -0.125 to 0.125
- w_value: bfloat16 [2048, 256], P('dp'), may hold values from -0.125 to 0.125
- w_out: bfloat16 [2048, 2048], P('dp'), may hold values from -0.5 to 0.5
- mlp_norm: bfloat16 [2048], P('dp'), may hold values from 0.5 to 1.5
- w_gate: bfloat16 [2048, 5632], P('dp'), may hold values from -0.125 to 0.125
- w_up: bfloat16 [2048, 5632], P('dp'), may hold values from -0.125 to 0.125
- w_down: bfloat16 [5632, 2048], P('dp'), may hold values from -0.15625 to 0.15625
- cotangent: bfloat16 [16384, 2048], P('dp'), may hold values from -6 to 6
Outputs:
- mixed_out: bfloat16 [16384, 2048], P('dp')
- grad_tokens: float32 [16384, 2048], P('dp')
- grad_attn_norm: float32 [2048], P('dp')
- grad_query: float32 [2048, 2048], P('dp')
- grad_key: float32 [2048, 256], P('dp')
- grad_value: float32 [2048, 256], P('dp')
- grad_out: float32 [2048, 2048], P('dp')
- grad_mlp_norm: float32 [2048], P('dp')
- grad_gate: float32 [2048, 5632], P('dp')
- grad_up: float32 [2048, 5632], P('dp')
- grad_down: float32 [5632, 2048], P('dp')
The draws below stay inside these ranges and needn't reach their ends.
Inputs may be any that keep to these rules, and one draw needn't show every extreme that they name: `seq_lengths`: each row holds 3 sequence lengths that sum to 128; the largest of each row is exactly 96.
All inputs are finite; a program needn't handle non-finite values.
Results may differ from the reference program's by a relative error of at most 0.015.
Values may be sent and summed in bfloat16 or wider, within the bound.
A program may use at most 448 MiB of HBM per device.

```python
import math
import jax
import jax.numpy as jnp
import numpy as np
from jax import lax

D = 2048
HEADS = 32
KV_HEADS = 4
HEAD = 64
FF = 5632
TOK_DEV = 128
SEQS = 3
MOST = 96
TOKENS = 16384
N_DP = 128


def steps_of(rng, dims, shards, smallest, high):
    loudness, own = 1.0, jax.random.fold_in(rng, 6)
    for dim, blocks in shards:
        steps = jnp.exp(jax.random.uniform(jax.random.fold_in(own, dim), (blocks,), jnp.float32, smallest / len(shards), high / len(shards)))
        loudness = loudness * jnp.repeat(steps, dims[dim] // blocks).reshape([-1 if axis == dim else 1 for axis in range(len(dims))])
    return loudness


def split_up(amount, total, reach, lean):
    portions = [(1 << 20) // math.isqrt(rank ** lean) + 1 for rank in range(2, amount + 1)]
    surplus, counts = total - reach - (amount - 1), [1] * (amount - 1)
    while surplus > 0:
        free = [i for i in range(amount - 1) if counts[i] < reach]
        mass, left = sum([portions[i] for i in free]), surplus
        for i in free:
            addition = min(reach - counts[i], max(1, left * portions[i] // mass), surplus)
            counts[i] = counts[i] + addition
            surplus = surplus - addition
    return np.array([reach] + counts)


def uneven(stream_key, number_of, total, bound, lean):
    if number_of == 2:
        one = jax.random.randint(stream_key, (), max(1, total - bound), min(bound, total - 1) + 1)
        return jnp.stack([one, total - one])
    sizes = jnp.asarray(split_up(number_of, total, bound, lean), jnp.int32)
    pairs = (number_of - 1) // 2
    source_of, sink = sizes[1:1 + 2 * pairs:2], sizes[2:2 + 2 * pairs:2]
    margin = jnp.minimum(source_of - 1, bound - sink)
    passed = jax.random.randint(jax.random.fold_in(stream_key, 1), (pairs,), 0, 1 << 20) % (margin + 1)
    sizes = sizes.at[1:1 + 2 * pairs:2].set(source_of - passed).at[2:2 + 2 * pairs:2].set(sink + passed)
    return sizes[jax.random.permutation(jax.random.fold_in(stream_key, 2), number_of)]


def bell_draw(stream_key, dims, scale, most, split=(), kind=jnp.bfloat16):
    entries = jax.random.normal(stream_key, dims, jnp.float32) * scale
    if len(split) > 0:
        entries = steps_of(stream_key, dims, split, -0.22, 0.18) * entries
    return jnp.clip(entries, min=-most, max=most).astype(kind)


def setup_inputs(seed: int = 0) -> dict:
    key_of = jax.random.split(jax.random.key(seed), 13)
    return {
        "tokens": bell_draw(key_of[0], (TOKENS, D), 1.0, 6.0, ((0, 128),)),
        "seq_lengths": jax.vmap(lambda own: uneven(own, SEQS, TOK_DEV, MOST, 2))(jax.random.split(key_of[1], N_DP)).reshape((N_DP, SEQS)).astype(jnp.int32),
        "attn_norm": jnp.clip(1.0 + 0.1 * jax.random.normal(key_of[2], (D,), jnp.float32), 0.5, 1.5).astype(jnp.bfloat16),
        "w_query": bell_draw(key_of[3], (D, HEADS * HEAD), D ** -0.5, 0.125, ((0, 128),)),
        "w_key": bell_draw(key_of[4], (D, KV_HEADS * HEAD), D ** -0.5, 0.125, ((0, 128),)),
        "w_value": bell_draw(key_of[5], (D, KV_HEADS * HEAD), D ** -0.5, 0.125, ((0, 128),)),
        "w_out": bell_draw(key_of[6], (HEADS * HEAD, D), (D // 16) ** -0.5, 0.5, ((0, 128),)),
        "mlp_norm": jnp.clip(1.0 + 0.1 * jax.random.normal(key_of[7], (D,), jnp.float32), 0.5, 1.5).astype(jnp.bfloat16),
        "w_gate": bell_draw(key_of[8], (D, FF), D ** -0.5, 0.125, ((0, 128),)),
        "w_up": bell_draw(key_of[9], (D, FF), D ** -0.5, 0.125, ((0, 128),)),
        "w_down": bell_draw(key_of[10], (FF, D), (FF // 4) ** -0.5, 0.15625, ((0, 128),)),
        "cotangent": bell_draw(key_of[11], (TOKENS, D), 1.0, 6.0, ((0, 128),)),
    }


@jax.custom_vjp
def low(v):
    return lax.optimization_barrier(v.astype(jnp.bfloat16)).astype(jnp.float32)

@jax.custom_vjp
def low_back(v):
    return v

def low_keep(v):
    return (low(v), None)

def low_pass(kept, grad):
    return (grad,)

def back_keep(v):
    return (v, None)

def back_low(kept, grad):
    return (low(grad),)
low.defvjp(low_keep, low_pass)
low_back.defvjp(back_keep, back_low)
EPSILON = 1e-05
THETA = 10000.0
SCALE = 0.125
MASKED = -1e+30

def layout(lengths, tok_count):
    ends = jnp.cumsum(lengths).astype(jnp.int32)
    places = jnp.arange(tok_count, dtype=jnp.int32)
    segment = lax.optimization_barrier(jnp.sum((places[:, None] >= ends[None, :]).astype(jnp.int32), axis=-1))
    starts = ends - lengths
    labels = jnp.arange(lengths.shape[0], dtype=jnp.int32)
    begins = lax.optimization_barrier(jnp.sum(jnp.where(segment[:, None] == labels[None, :], starts[None, :], 0), axis=-1))
    return (segment, (places - begins).astype(jnp.int32))

def angles(position):
    inverse = jnp.exp(jnp.arange(HEAD // 2, dtype=jnp.float32) * (-2.0 * math.log(THETA) / HEAD))
    angle = position.astype(jnp.float32)[:, None] * inverse[None, :]
    return (jnp.cos(angle), jnp.sin(angle))

def rotate(values, cosine, sine_table):
    half_size = values.shape[-1] // 2
    front_half = values[..., :half_size]
    back_half = values[..., half_size:]
    return jnp.concatenate([front_half * cosine - back_half * sine_table, back_half * cosine + front_half * sine_table], axis=-1)

def product(left, right):
    return jnp.dot(left, right, precision=lax.Precision.HIGHEST)

def rms_norm(values, gain):
    square = lax.optimization_barrier(jnp.mean(values * values, axis=-1, keepdims=True))
    return values * lax.rsqrt(square + EPSILON) * gain

def reference(tokens, seq_lengths, attn_norm, w_query, w_key, w_value, w_out, mlp_norm, w_gate, w_up, w_down, cotangent):
    group_size = HEADS // KV_HEADS
    segment, position = jax.vmap(lambda lengths: layout(lengths, TOK_DEV))(seq_lengths)
    cosine, sine_table = angles(position.reshape(TOKENS))
    cosine = cosine[:, None, :]
    sine_table = sine_table[:, None, :]
    places = jnp.arange(TOK_DEV, dtype=jnp.int32)
    causal = places[:, None] >= places[None, :]
    allowed = (segment[:, :, None] == segment[:, None, :]) & causal[None]
    allowed = allowed[:, None, None]

    def attend(queries, key_rows, values):
        query_heads = queries.reshape(N_DP, TOK_DEV, KV_HEADS, group_size, HEAD)
        key_heads = key_rows.reshape(N_DP, TOK_DEV, KV_HEADS, HEAD)
        value_heads = values.reshape(N_DP, TOK_DEV, KV_HEADS, HEAD)
        scores = low_back(jnp.einsum('ntkgd,nskd->nkgts', query_heads, key_heads, precision=lax.Precision.HIGHEST) * SCALE)
        scores = jnp.where(allowed, scores, MASKED)
        weights = low(jax.nn.softmax(scores, axis=-1))
        result = jnp.einsum('nkgts,nskd->ntkgd', weights, value_heads, precision=lax.Precision.HIGHEST)
        return result.reshape(TOKENS, HEADS * HEAD)

    def forward(inputs, attn_gain, query_w, key_w, value_w, out_w, mlp_gain, gate_w, up_w, down_w):
        normed = low(rms_norm(inputs, attn_gain))
        queries = low(rotate(low_back(product(normed, query_w)).reshape(TOKENS, HEADS, HEAD), cosine, sine_table))
        key_rows = low(rotate(low_back(product(normed, key_w)).reshape(TOKENS, KV_HEADS, HEAD), cosine, sine_table))
        values = low(low_back(product(normed, value_w)))
        attended = low_back(low(attend(queries, key_rows, values)))
        residual = inputs + low_back(product(attended, out_w))
        normed_two = low(rms_norm(residual, mlp_gain))
        gate_val = low_back(product(normed_two, gate_w))
        up_val = low_back(product(normed_two, up_w))
        active = low(jax.nn.silu(gate_val) * up_val)
        return residual + product(active, down_w)
    inputs = (tokens.astype(jnp.float32), attn_norm.astype(jnp.float32), w_query.astype(jnp.float32), w_key.astype(jnp.float32), w_value.astype(jnp.float32), w_out.astype(jnp.float32), mlp_norm.astype(jnp.float32), w_gate.astype(jnp.float32), w_up.astype(jnp.float32), w_down.astype(jnp.float32))
    result, pull = jax.vjp(forward, *inputs)
    grads = pull(cotangent.astype(jnp.float32))
    return (result.astype(jnp.bfloat16), grads[0], grads[1], grads[2], grads[3], grads[4], grads[5], grads[6], grads[7], grads[8], grads[9])
```

```python
import functools
import math

import jax
import jax.numpy as jnp
from jax import lax
from jax.experimental import pallas as pl
from jax.experimental.pallas import tpu as pltpu
from jax.sharding import PartitionSpec as P


HEADS = 32
KV_HEADS = 4
HEAD = 64
EPSILON = 1e-05
THETA = 10000.0
SCALE = 0.125
MASKED = -1e30

GROUP = 8
TOK = 128
TOKENS = GROUP * TOK
D = 2048
MY_HEADS = HEADS // GROUP
COLS = D // GROUP
FF_ROWS = 44
FF_PAD = 48
FF_COLS = 16 * FF_PAD
KV_COLS = 2 * HEAD
QKV = COLS + KV_COLS
ATT = QKV + COLS
PACK = ATT + 2 * FF_COLS

MESH = pl.DeviceIdType.MESH
BF16 = jnp.bfloat16
F32 = jnp.float32
ANY = pl.BlockSpec(memory_space=pl.ANY)
VMEM = pl.BlockSpec(memory_space=pltpu.VMEM)


def place():
    me = lax.axis_index("dp")
    return me // 32, (me // 8) % 4, (me // 2) % 4, me % 2


def index(z, y, x, c):
    return ((z * 4 + y) * 4 + x) * 2 + c


def shifted(here, axis, step):
    spot = list(here)
    spot[axis] = (spot[axis] + step) % 4
    return index(*spot)


def group_peers(here):
    z, y, x, c = here
    return [
        ((x + dx) % 4 * 2 + (c + dc) % 2, index(z, y, (x + dx) % 4, (c + dc) % 2))
        for dx in (2, 1, 3, 0)
        for dc in (0, 1)
        if (dx, dc) != (0, 0)
    ]


def plane_peers(here):
    z, y, x, c = here
    return [
        (((z + dz) % 4, (y + dy) % 4), index((z + dz) % 4, (y + dy) % 4, x, c))
        for dz in range(4)
        for dy in range(4)
        if (dz, dy) != (0, 0)
    ]


def greet(partners):
    barrier = pltpu.get_barrier_semaphore()
    for partner in partners:
        pl.semaphore_signal(barrier, inc=1, device_id=(partner,), device_id_type=MESH)
    pl.semaphore_wait(barrier, len(partners))


class Net:
    def __init__(self, send_sem, recv_sem, local_sem):
        self.sems = (send_sem, recv_sem, local_sem)
        self.sent, self.moved = 0, 0
        self.open = []

    def send(self, src, dst, device):
        copy = pltpu.make_async_remote_copy(
            src_ref=src,
            dst_ref=dst,
            send_sem=self.sems[0].at[self.sent],
            recv_sem=self.sems[1].at[self.sent],
            device_id=(device,),
            device_id_type=MESH,
        )
        copy.start()
        self.sent += 1
        self.open.append(copy)
        return copy

    def move(self, src, dst):
        copy = pltpu.make_async_copy(src, dst, self.sems[2].at[self.moved])
        copy.start()
        self.moved += 1
        return copy

    def finish(self):
        for copy in self.open:
            copy.wait_send()


def run(*programs):
    left = list(programs)
    while left:
        for program in list(left):
            if next(program, "end") == "end":
                left.remove(program)


def chain(*programs):
    for program in programs:
        yield from program


def together(*programs):
    left = list(programs)
    while left:
        for program in list(left):
            if next(program, "end") == "end":
                left.remove(program)
        yield


def ring_gather(net, here, axis, at):
    spot = here[axis]
    before, after = (spot + 3) % 4, (spot + 1) % 4
    up, down = shifted(here, axis, 1), shifted(here, axis, -1)
    first = net.send(at(spot, None), at(spot, None), up)
    second = net.send(at(spot, None), at(spot, None), down)
    yield
    first.wait_recv()
    third = net.send(at(before, 0), at(before, 0), up)
    second.wait_recv()
    fourth = net.send(at(after, 1), at(after, 1), down)
    yield
    third.wait_recv()
    fourth.wait_recv()


def plane_gather(net, here, region, half):
    z, y = here[0], here[1]
    if half == 0:
        yield from ring_gather(net, here, 1, lambda p, s: region(z, p, 0, s))
        yield from ring_gather(net, here, 0, lambda p, s: region(p, None, 0, s))
    else:
        yield from ring_gather(net, here, 0, lambda p, s: region(p, y, 1, s))
        yield from ring_gather(net, here, 1, lambda p, s: region(None, p, 1, s))


def group_gather(net, here, own, at):
    z, y, x, c = here
    right, left = shifted(here, 2, 1), shifted(here, 2, -1)
    peer = index(z, y, x, 1 - c)
    before, after, far = (x + 3) % 4 * 2 + c, (x + 1) % 4 * 2 + c, (x + 2) % 4 * 2 + c
    mine = x * 2 + c
    first = net.send(own, at(mine, None), right)
    second = net.send(own, at(mine, None), left)
    across = [net.send(own, at(mine, None), peer)]
    kept = net.move(own, at(mine, None))
    yield
    first.wait_recv()
    third = net.send(at(before, 0), at(before, 0), right)
    across.append(net.send(at(before, None), at(before, None), peer))
    yield
    second.wait_recv()
    fourth = net.send(at(after, 1), at(after, 1), left)
    across.append(net.send(at(after, None), at(after, None), peer))
    yield
    third.wait_recv()
    across.append(net.send(at(far, 0), at(far, 0), peer))
    yield
    fourth.wait_recv()
    across.append(net.send(at(far, 1), at(far, 1), peer))
    yield
    for copy in across:
        copy.wait_recv()
    kept.wait()


def group_exchange(net, here, src, dst):
    mine = here[2] * 2 + here[3]
    copies = [net.send(src(g), dst(mine), device) for g, device in group_peers(here)]
    kept = net.move(src(mine), dst(mine))
    yield
    for copy in copies:
        copy.wait_recv()
    kept.wait()


def strips(rows, work, step=16):
    def body(i, carry):
        work(pl.ds(pl.multiple_of(i * step, step), step))
        return carry

    lax.fori_loop(0, rows // step, body, 0)


def add_into(total, term):
    if len(total.shape) == 3:
        for i in range(total.shape[0]):
            add_into(total.at[i], term.at[i])
        return

    def work(rows):
        total[rows] = (total[rows].astype(F32) + term[rows].astype(F32)).astype(total.dtype)

    strips(total.shape[0], work)


def add_up(out, *terms):
    if len(out.shape) == 3:
        for i in range(out.shape[0]):
            add_up(out.at[i], *[term.at[i] for term in terms])
        return

    def work(rows):
        total = terms[0][rows].astype(F32)
        for term in terms[1:]:
            total = total + term[rows].astype(F32)
        out[rows] = total.astype(out.dtype)

    strips(out.shape[0], work)


def group_reduce_scratch(rows, cols):
    return [
        pltpu.VMEM((4, rows, cols), BF16),
        pltpu.VMEM((4, rows, cols), BF16),
        pltpu.VMEM((2, rows // 2, cols), BF16),
        pltpu.VMEM((2, rows, cols), BF16),
    ]


def group_reduce(net, here, src, out, scratch):
    crossed, held, relay, landed = scratch
    z, y, x, c = here
    right, left = shifted(here, 2, 1), shifted(here, 2, -1)
    peer = index(z, y, x, 1 - c)
    half = held.shape[1] // 2
    upper, lower = pl.ds(0, half), pl.ds(half, half)
    cross, own = [], []
    for slot, step in enumerate((2, 1, 3, 0)):
        there = (x + step) % 4
        cross.append(net.send(src(there * 2 + 1 - c), crossed.at[slot], peer))
        own.append(net.move(src(there * 2 + c), held.at[slot]))
    yield
    cross[0].wait_recv()
    own[0].wait()
    add_into(held.at[0], crossed.at[0])
    one = net.send(held.at[0, upper], relay.at[0], right)
    two = net.send(held.at[0, lower], relay.at[1], left)
    yield
    cross[1].wait_recv()
    own[1].wait()
    add_into(held.at[1], crossed.at[1])
    three = net.send(held.at[1, lower], landed.at[0, lower], right)
    cross[2].wait_recv()
    own[2].wait()
    add_into(held.at[2], crossed.at[2])
    four = net.send(held.at[2, upper], landed.at[1, upper], left)
    yield
    one.wait_recv()
    add_into(held.at[1, upper], relay.at[0])
    five = net.send(held.at[1, upper], landed.at[0, upper], right)
    two.wait_recv()
    add_into(held.at[2, lower], relay.at[1])
    six = net.send(held.at[2, lower], landed.at[1, lower], left)
    yield
    cross[3].wait_recv()
    own[3].wait()
    for copy in (three, four, five, six):
        copy.wait_recv()
    add_up(out, held.at[3], crossed.at[3], landed.at[0], landed.at[1])


def plane_reduce_scratch(rows, cols):
    return [
        pltpu.VMEM((2, 4, rows, cols), BF16),
        pltpu.VMEM((2, 4, rows, cols), BF16),
        pltpu.VMEM((2, 2, 4, rows, cols), BF16),
        pltpu.VMEM((2, 4, rows, cols), BF16),
        pltpu.VMEM((2, rows, cols), BF16),
        pltpu.VMEM((2, 2, rows, cols), BF16),
    ]


def plane_reduce(net, here, region, half, out, scratch):
    relay, passing, landed, total, relay_two, landed_two = scratch
    axis, other = (0, 1) if half == 0 else (1, 0)

    def at(position, part):
        return region(position, None, half, part) if half == 0 else region(None, position, half, part)

    spot = here[axis]
    up, down = shifted(here, axis, 1), shifted(here, axis, -1)
    after, before, far = (spot + 1) % 4, (spot + 3) % 4, (spot + 2) % 4
    one = net.send(at(far, 0), relay.at[0], up)
    two = net.send(at(far, 1), relay.at[1], down)
    three = net.send(at(after, 1), landed.at[0, 1], up)
    four = net.send(at(before, 0), landed.at[1, 0], down)
    moves = [
        net.move(at(after, 0), passing.at[0]),
        net.move(at(before, 1), passing.at[1]),
        net.move(at(spot, 0), total.at[0]),
        net.move(at(spot, 1), total.at[1]),
    ]
    yield
    one.wait_recv()
    moves[0].wait()
    add_into(passing.at[0], relay.at[0])
    five = net.send(passing.at[0], landed.at[0, 0], up)
    two.wait_recv()
    moves[1].wait()
    add_into(passing.at[1], relay.at[1])
    six = net.send(passing.at[1], landed.at[1, 1], down)
    yield
    moves[2].wait()
    four.wait_recv()
    five.wait_recv()
    add_up(total.at[0], total.at[0], landed.at[0, 0], landed.at[1, 0])
    moves[3].wait()
    three.wait_recv()
    six.wait_recv()
    add_up(total.at[1], total.at[1], landed.at[0, 1], landed.at[1, 1])
    spot = here[other]
    up, down = shifted(here, other, 1), shifted(here, other, -1)
    after, before, far = (spot + 1) % 4, (spot + 3) % 4, (spot + 2) % 4
    one = net.send(total.at[0, far], relay_two.at[0], up)
    two = net.send(total.at[1, far], relay_two.at[1], down)
    three = net.send(total.at[1, after], landed_two.at[0, 1], up)
    four = net.send(total.at[0, before], landed_two.at[1, 0], down)
    yield
    one.wait_recv()
    add_into(total.at[0, after], relay_two.at[0])
    five = net.send(total.at[0, after], landed_two.at[0, 0], up)
    two.wait_recv()
    add_into(total.at[1, before], relay_two.at[1])
    six = net.send(total.at[1, before], landed_two.at[1, 1], down)
    yield
    four.wait_recv()
    five.wait_recv()
    add_up(out(0), total.at[0, spot], landed_two.at[0, 0], landed_two.at[1, 0])
    three.wait_recv()
    six.wait_recv()
    add_up(out(1), total.at[1, spot], landed_two.at[0, 1], landed_two.at[1, 1])


def by_rows(ref, rows, cols):
    def region(z, y, half, part):
        size = rows // 2 if part is None else rows // 4
        start = half * (rows // 2) + (0 if part is None else part * (rows // 4))
        return ref.at[
            slice(None) if z is None else z, slice(None) if y is None else y, pl.ds(start, size), cols
        ]

    return region


def by_cols(ref, cols):
    def region(z, y, half, part):
        size = cols // 2 if part is None else cols // 4
        start = half * (cols // 2) + (0 if part is None else part * (cols // 4))
        return ref.at[
            slice(None) if z is None else z, slice(None) if y is None else y, :, pl.ds(start, size)
        ]

    return region


def row_block(ref, rows):
    def at(g, part=None):
        size = rows if part is None else rows // 2
        start = g * rows + (0 if part is None else part * (rows // 2))
        return ref.at[pl.ds(pl.multiple_of(start, rows // 2), size)]

    return at


def col_block(ref, rows, cols):
    def at(g, part=None):
        size = rows if part is None else rows // 2
        start = 0 if part is None else part * (rows // 2)
        return ref.at[pl.ds(start, size), pl.ds(pl.multiple_of(g * cols, cols), cols)]

    return at


def ring_partners(here, axes):
    return [shifted(here, axis, step) for axis in axes for step in (1, -1)]


def core_peer(here):
    return index(here[0], here[1], here[2], 1 - here[3])


def communicate(kernel, collective_id, outs, scratch, n_sends, n_moves, name):
    def call(*args):
        def body(*refs):
            n_in, n_out = len(args), len(outs)
            send_sem, recv_sem, local_sem = refs[-3:]
            net = Net(send_sem, recv_sem, local_sem)
            kernel(net, place(), refs[:n_in], refs[n_in : n_in + n_out], refs[n_in + n_out : -3])
            net.finish()

        return pl.pallas_call(
            body,
            out_shape=[jax.ShapeDtypeStruct(shape, dtype) for shape, dtype, _ in outs],
            in_specs=[ANY] * len(args),
            out_specs=[VMEM if inside else ANY for _, _, inside in outs],
            scratch_shapes=list(scratch)
            + [
                pltpu.SemaphoreType.DMA((n_sends,)),
                pltpu.SemaphoreType.DMA((n_sends,)),
                pltpu.SemaphoreType.DMA((max(n_moves, 1),)),
            ],
            compiler_params=pltpu.CompilerParams(
                collective_id=collective_id, has_side_effects=True, vmem_limit_bytes=56 << 20
            ),
            name=name,
        )(*args)

    return call


def gather_all(net, here, inputs, outputs, scratch):
    packed, down, tokens, upstream, meta = inputs
    wide, narrow, all_tokens, all_upstream, all_meta = outputs
    seen, mine_meta = scratch
    z, y, x, c = here
    mine = x * 2 + c
    greet([device for _, device in group_peers(here)] + [device for _, device in plane_peers(here)])

    def small():
        copies = [net.send(meta, seen.at[mine], device) for _, device in group_peers(here)]
        kept = net.move(meta, seen.at[mine])
        yield
        for copy in copies:
            copy.wait_recv()
        kept.wait()
        mine_meta[...] = jnp.sum(seen[...], axis=0)
        spots = all_meta.at[z * 4 + y]
        copies = [net.send(mine_meta, spots, device) for _, device in plane_peers(here)]
        all_meta[z * 4 + y] = mine_meta[...]
        yield
        yield
        for copy in copies:
            copy.wait_recv()

    def weights():
        rows = pl.ds(pl.multiple_of(mine * 16, 16), 16)
        yield from group_exchange(
            net, here, lambda g: packed.at[g], lambda g: wide.at[z, y, pl.ds(pl.multiple_of(g * 16, 16), 16)]
        )
        edges = [(0, QKV), (QKV, COLS), (ATT, FF_COLS), (ATT + FF_COLS, FF_COLS)]
        pieces = [by_rows(wide, TOK, pl.ds(start, size)) for start, size in edges]
        running = []
        for region in pieces:
            running += [plane_gather(net, here, region, 0), plane_gather(net, here, region, 1)]
        yield from together(*running)

    def feed():
        kept = net.move(down, narrow.at[z, y])
        kept.wait()
        region = by_cols(narrow, D)
        yield
        yield from together(plane_gather(net, here, region, 0), plane_gather(net, here, region, 1))

    run(
        small(),
        weights(),
        group_gather(net, here, tokens, row_block(all_tokens, TOK)),
        group_gather(net, here, upstream, row_block(all_upstream, TOK)),
        feed(),
    )


def gather_columns(net, here, inputs, outputs, scratch):
    greet(ring_partners(here, (2,)) + [core_peer(here)])
    run(group_gather(net, here, inputs[0], col_block(outputs[0], TOKENS, COLS)))


def reduce_feed(net, here, inputs, outputs, scratch):
    grad_rows, mixed_rows, wide, narrow = inputs
    grad_out, mixed_out, wide_out, narrow_out = outputs
    greet(ring_partners(here, (0, 1, 2)) + [core_peer(here)])
    wide_region = by_rows(wide, TOK, slice(None))
    narrow_region = by_cols(narrow, D)
    quarter = D // 4

    def wide_part(half):
        return lambda part: wide_out.at[pl.ds((half * 2 + part) * (TOK // 4), TOK // 4)]

    def narrow_part(half):
        return lambda part: narrow_out.at[:, pl.ds((half * 2 + part) * quarter, quarter)]

    run(
        group_reduce(net, here, row_block(grad_rows, TOK), grad_out, scratch[0:4]),
        plane_reduce(net, here, wide_region, 0, wide_part(0), scratch[8:14]),
        plane_reduce(net, here, wide_region, 1, wide_part(1), scratch[14:20]),
        plane_reduce(net, here, narrow_region, 0, narrow_part(0), scratch[20:26]),
        plane_reduce(net, here, narrow_region, 1, narrow_part(1), scratch[26:32]),
        group_reduce(net, here, row_block(mixed_rows, TOK), mixed_out, scratch[4:8]),
    )


def exchange_columns(net, here, inputs, outputs, scratch):
    greet([device for _, device in group_peers(here)])
    run(group_exchange(net, here, col_block(inputs[0], TOK, COLS), row_block(outputs[0], TOK)))


def reduce_heads(net, here, inputs, outputs, scratch):
    greet(ring_partners(here, (2,)) + [core_peer(here)])
    run(group_reduce(net, here, col_block(inputs[0], TOKENS, COLS), outputs[0], scratch))


def reduce_attention(net, here, inputs, outputs, scratch):
    grad_rows, wide = inputs
    grad_out, wide_out = outputs
    greet(ring_partners(here, (0, 1, 2)) + [core_peer(here)])
    region = by_rows(wide, TOK, slice(None))

    def part_of(half):
        return lambda part: wide_out.at[pl.ds((half * 2 + part) * (TOK // 4), TOK // 4)]

    run(
        group_reduce(net, here, row_block(grad_rows, TOK), grad_out, scratch[0:4]),
        plane_reduce(net, here, region, 0, part_of(0), scratch[4:10]),
        plane_reduce(net, here, region, 1, part_of(1), scratch[10:16]),
    )


def hand_out(net, here, inputs, outputs, scratch):
    wide, narrow, norms = inputs
    wide_out, narrow_out, norms_out = outputs
    seen, kept_norms, again = scratch
    z, y, x, c = here
    mine = x * 2 + c
    greet([device for _, device in group_peers(here)] + [device for _, device in plane_peers(here)])

    def rows_of(ref):
        return lambda g: ref.at[pl.ds(pl.multiple_of(g * 16, 16), 16)]

    def small():
        spot = z * 4 + y
        copies = [
            net.send(norms.at[to[0] * 4 + to[1]], seen.at[spot], device) for to, device in plane_peers(here)
        ]
        kept = net.move(norms.at[spot], seen.at[spot])
        yield
        for copy in copies:
            copy.wait_recv()
        kept.wait()
        kept_norms[...] = jnp.sum(seen[...], axis=0)
        again[mine] = kept_norms[...]
        copies = [net.send(kept_norms, again.at[mine], device) for _, device in group_peers(here)]
        yield
        for copy in copies:
            copy.wait_recv()
        norms_out[...] = jnp.sum(again[...], axis=0)

    run(
        small(),
        group_exchange(net, here, rows_of(wide), lambda g: wide_out.at[g]),
        group_exchange(net, here, rows_of(narrow), lambda g: narrow_out.at[g]),
    )


def angles(position):
    inverse = jnp.exp(jnp.arange(HEAD // 2, dtype=F32) * (-2.0 * math.log(THETA) / HEAD))
    angle = position.astype(F32)[:, None] * inverse[None, :]
    return (jnp.cos(angle), jnp.sin(angle))


def rotate(values, cosine, sine_table):
    half_size = values.shape[-1] // 2
    front_half = values[..., :half_size]
    back_half = values[..., half_size:]
    return jnp.concatenate(
        [
            front_half * cosine - back_half * sine_table,
            back_half * cosine + front_half * sine_table,
        ],
        axis=-1,
    )


def matmul(left, right):
    return jnp.dot(left, right, preferred_element_type=F32)


def dot_last(left, right):
    return lax.dot_general(left, right, (((1,), (1,)), ((), ())), preferred_element_type=F32)


def dot_first(left, right):
    return lax.dot_general(left, right, (((0,), (0,)), ((), ())), preferred_element_type=F32)


def norm_back(grad_unit, unit_vals, inv_scale):
    return inv_scale * (
        grad_unit - unit_vals * jnp.mean(grad_unit * unit_vals, axis=-1, keepdims=True)
    )


def inverse_rms(values):
    return lax.rsqrt(jnp.mean(values * values, axis=-1, keepdims=True) + EPSILON)


def pack_columns(w_query, w_key, w_value, w_out, w_gate, w_up):
    def even(w):
        return w.reshape(16, GROUP, COLS).transpose(1, 0, 2)

    def feed(w):
        parts = w.reshape(16, 16, GROUP, FF_ROWS).transpose(2, 0, 1, 3)
        parts = jnp.pad(parts, ((0, 0), (0, 0), (0, 0), (0, FF_PAD - FF_ROWS)))
        return parts.reshape(GROUP, 16, FF_COLS)

    keyed = jnp.concatenate(
        [w_key.reshape(16, KV_HEADS, HEAD), w_value.reshape(16, KV_HEADS, HEAD)], axis=-1
    )
    keyed = jnp.repeat(keyed.transpose(1, 0, 2), 2, axis=0)
    return jnp.concatenate([even(w_query), keyed, even(w_out), feed(w_gate), feed(w_up)], axis=-1)


def on_device(
    tokens,
    seq_lengths,
    attn_norm,
    w_query,
    w_key,
    w_value,
    w_out,
    mlp_norm,
    w_gate,
    w_up,
    w_down,
    cotangent,
):
    me = lax.axis_index("dp")
    member = me % GROUP
    blocks = GROUP
    meta = jnp.stack(
        [
            attn_norm.astype(F32),
            mlp_norm.astype(F32),
            jnp.pad(seq_lengths[0].astype(F32), (0, 13)),
        ]
    )
    meta = lax.dynamic_update_slice(jnp.zeros((8, 128), F32), meta, (0, member * 16))
    packed = pack_columns(w_query, w_key, w_value, w_out, w_gate, w_up)
    down_rows = jnp.pad(w_down, ((0, FF_PAD - FF_ROWS), (0, 0)))
    wide, narrow, all_tokens, all_upstream, all_meta = communicate(
        gather_all,
        0,
        [
            ((4, 4, TOK, PACK), BF16, False),
            ((4, 4, FF_PAD, D), BF16, False),
            ((TOKENS, D), BF16, False),
            ((TOKENS, D), BF16, False),
            ((16, 8, 128), F32, True),
        ],
        [pltpu.VMEM((8, 8, 128), F32), pltpu.VMEM((8, 128), F32)],
        140,
        16,
        "gather_all",
    )(packed, down_rows, tokens, cotangent, meta)
    wide = wide.reshape(D, PACK)
    narrow = narrow.reshape(FF_COLS, D)
    attn_gain = all_meta[:, 0, :].reshape(D)
    mlp_gain = all_meta[:, 1, :].reshape(D)
    plane = lax.dynamic_index_in_dim(all_meta, me // GROUP, 0, keepdims=False)
    lengths = plane[2].reshape(GROUP, 16)[:, :3].astype(jnp.int32)

    ends = jnp.cumsum(lengths, axis=-1)
    places = jnp.arange(TOK, dtype=jnp.int32)
    segment = jnp.sum((places[None, :, None] >= ends[:, None, :]).astype(jnp.int32), axis=-1)
    starts = ends - lengths
    labels = jnp.arange(3, dtype=jnp.int32)
    begins = jnp.sum(
        jnp.where(segment[:, :, None] == labels, starts[:, None, :], 0), axis=-1
    )
    position = (places[None, :] - begins).reshape(TOKENS)
    cosine, sine_table = angles(position)
    cosine, sine_table = cosine[:, None, :], sine_table[:, None, :]
    allowed = (
        (segment[:, :, None] == segment[:, None, :]) & (places[:, None] >= places[None, :])
    )[:, None]

    inputs = all_tokens.astype(F32)
    unit = inputs * inverse_rms(inputs)
    normed = (unit * attn_gain).astype(BF16)
    linear = matmul(normed, wide[:, :QKV])
    queries = rotate(linear[:, :COLS].reshape(TOKENS, MY_HEADS, HEAD), cosine, sine_table)
    queries = queries.astype(BF16).reshape(blocks, TOK, MY_HEADS, HEAD)
    key_rows = rotate(linear[:, COLS : COLS + HEAD].reshape(TOKENS, 1, HEAD), cosine, sine_table)
    key_rows = key_rows.astype(BF16).reshape(blocks, TOK, HEAD)
    values = linear[:, COLS + HEAD :].astype(BF16).reshape(blocks, TOK, HEAD)
    raw = jnp.einsum("nthd,nsd->nhts", queries, key_rows, preferred_element_type=F32) * SCALE
    scores = jnp.where(allowed, raw, MASKED)
    probs = jax.nn.softmax(scores, axis=-1)
    weights_low = probs.astype(BF16)
    attended = jnp.einsum("nhts,nsd->nthd", weights_low, values, preferred_element_type=F32)
    attended = attended.astype(BF16).reshape(TOKENS, COLS)

    (all_attended,) = communicate(
        gather_columns, 1, [((TOKENS, D), BF16, False)], [], 10, 1, "gather_attended"
    )(attended)
    out_cols = wide[:, QKV:ATT]
    my_inputs = lax.dynamic_slice(all_tokens, (0, member * COLS), (TOKENS, COLS))
    my_residual = (my_inputs.astype(F32) + matmul(all_attended, out_cols)).astype(BF16)
    (all_residual,) = communicate(
        gather_columns, 2, [((TOKENS, D), BF16, False)], [], 10, 1, "gather_residual"
    )(my_residual)

    residual = all_residual.astype(F32)
    normed_two = (residual * inverse_rms(residual) * mlp_gain).astype(BF16)
    feed_cols = wide[:, ATT:]
    both = matmul(normed_two, feed_cols)
    gate_val, up_val = both[:, :FF_COLS], both[:, FF_COLS:]
    sigmoid_gate = jax.nn.sigmoid(gate_val)
    silu_gate = gate_val * sigmoid_gate
    active = (silu_gate * up_val).astype(BF16)
    mixed_partial = matmul(active, narrow).astype(BF16)
    grad_active = dot_last(all_upstream, narrow)
    grad_up_lin = (grad_active * silu_gate).astype(BF16)
    grad_gate_lin = (
        grad_active * up_val * sigmoid_gate * (1.0 + gate_val * (1.0 - sigmoid_gate))
    ).astype(BF16)
    grad_both = jnp.concatenate([grad_gate_lin, grad_up_lin], axis=1)
    grad_normed_partial = dot_last(grad_both, feed_cols).astype(BF16)
    grad_feed = dot_first(normed_two, grad_both).astype(BF16).reshape(4, 4, TOK, 2 * FF_COLS)
    grad_narrow = dot_first(active, all_upstream).astype(BF16).reshape(4, 4, FF_PAD, D)
    grad_normed_two, mixed, feed_sum, down_sum = communicate(
        reduce_feed,
        3,
        [
            ((TOK, D), F32, True),
            ((TOK, D), F32, True),
            ((TOK, 2 * FF_COLS), BF16, True),
            ((FF_PAD, D), F32, True),
        ],
        group_reduce_scratch(TOK, D) * 2
        + plane_reduce_scratch(TOK // 4, 2 * FF_COLS) * 2
        + plane_reduce_scratch(FF_PAD, D // 4) * 2,
        80,
        40,
        "reduce_feed",
    )(grad_normed_partial, mixed_partial, grad_feed, grad_narrow)

    start = member * TOK
    own_residual = lax.dynamic_slice(all_residual, (start, 0), (TOK, D)).astype(F32)
    mixed_out = (own_residual + mixed).astype(BF16)
    scale_two = inverse_rms(own_residual)
    unit_two = own_residual * scale_two
    mlp_gain_term = jnp.sum(grad_normed_two * unit_two, axis=0)
    grad_resid = cotangent.astype(F32) + norm_back(grad_normed_two * mlp_gain, unit_two, scale_two)
    (grad_attn_cols,) = communicate(
        exchange_columns, 4, [((TOKENS, COLS), BF16, False)], [], 8, 1, "exchange_residual"
    )(grad_resid.astype(BF16))

    grad_heads_partial = dot_last(grad_attn_cols, out_cols).astype(BF16)
    (grad_heads,) = communicate(
        reduce_heads,
        5,
        [((TOKENS, COLS), BF16, True)],
        group_reduce_scratch(TOKENS, COLS),
        12,
        4,
        "reduce_heads",
    )(grad_heads_partial)
    grad_out_cols = dot_first(all_attended, grad_attn_cols)
    grad_heads = grad_heads.reshape(blocks, TOK, MY_HEADS, HEAD)
    grad_probs = jnp.einsum("nthd,nsd->nhts", grad_heads, values, preferred_element_type=F32)
    grad_scores = (
        probs * (grad_probs - jnp.sum(probs * grad_probs, axis=-1, keepdims=True))
    ).astype(BF16)
    grad_queries = jnp.einsum("nhts,nsd->nthd", grad_scores, key_rows, preferred_element_type=F32)
    grad_keys = jnp.einsum("nhts,nthd->nsd", grad_scores, queries, preferred_element_type=F32)
    grad_values = jnp.einsum("nhts,nthd->nsd", weights_low, grad_heads, preferred_element_type=F32)
    grad_query_lin = rotate(
        (grad_queries * SCALE).reshape(TOKENS, MY_HEADS, HEAD), cosine, -sine_table
    ).reshape(TOKENS, COLS)
    grad_key_lin = rotate(
        (grad_keys * SCALE).reshape(TOKENS, 1, HEAD), cosine, -sine_table
    ).reshape(TOKENS, HEAD)
    grad_lin = jnp.concatenate(
        [grad_query_lin, grad_key_lin, grad_values.reshape(TOKENS, HEAD)], axis=1
    ).astype(BF16)
    grad_normed_partial = dot_last(grad_lin, wide[:, :QKV]).astype(BF16)
    grad_qkv_cols = dot_first(normed, grad_lin)
    grad_att = jnp.concatenate([grad_qkv_cols, grad_out_cols], axis=1).astype(BF16)
    grad_normed, att_sum = communicate(
        reduce_attention,
        6,
        [((TOK, D), F32, True), ((TOK, ATT), BF16, True)],
        group_reduce_scratch(TOK, D) + plane_reduce_scratch(TOK // 4, ATT) * 2,
        50,
        20,
        "reduce_attention",
    )(grad_normed_partial, grad_att.reshape(4, 4, TOK, ATT))

    own_inputs = tokens.astype(F32)
    scale_one = inverse_rms(own_inputs)
    unit_one = own_inputs * scale_one
    attn_gain_term = jnp.sum(grad_normed * unit_one, axis=0)
    grad_tokens = grad_resid + norm_back(grad_normed * attn_gain, unit_one, scale_one)
    norms = jnp.stack([attn_gain_term.reshape(16, 128), mlp_gain_term.reshape(16, 128)], axis=1)
    norms = jnp.pad(norms, ((0, 0), (0, 6), (0, 0)))
    feed_rows, att_rows, norm_sums = communicate(
        hand_out,
        7,
        [
            ((GROUP, 16, 2 * FF_COLS), BF16, False),
            ((GROUP, 16, ATT), BF16, False),
            ((8, 128), F32, True),
        ],
        [pltpu.VMEM((16, 8, 128), F32), pltpu.VMEM((8, 128), F32), pltpu.VMEM((8, 8, 128), F32)],
        40,
        4,
        "hand_out",
    )(feed_sum, att_sum, norms)

    def even(part):
        return part.transpose(1, 0, 2).reshape(16, D).astype(F32)

    def feed(part):
        part = part.reshape(GROUP, 16, 16, FF_PAD)[..., :FF_ROWS]
        return part.transpose(1, 2, 0, 3).reshape(16, 16 * GROUP * FF_ROWS).astype(F32)

    keyed = att_rows[:, :, COLS:QKV].astype(F32).reshape(KV_HEADS, 2, 16, KV_COLS).sum(axis=1)
    keyed = keyed.transpose(1, 0, 2)
    own_norms = lax.dynamic_slice(norm_sums, (0, member * 16), (2, 16))
    return (
        mixed_out,
        grad_tokens,
        own_norms[0],
        even(att_rows[:, :, :COLS]),
        keyed[:, :, :HEAD].reshape(16, KV_HEADS * HEAD),
        keyed[:, :, HEAD:].reshape(16, KV_HEADS * HEAD),
        even(att_rows[:, :, QKV:]),
        own_norms[1],
        feed(feed_rows[:, :, :FF_COLS]),
        feed(feed_rows[:, :, FF_COLS:]),
        down_sum[:FF_ROWS],
    )


def solution(mesh):
    matrix, vector = P("dp", None), P("dp")
    return jax.shard_map(
        on_device,
        mesh=mesh,
        in_specs=(
            matrix,
            matrix,
            vector,
            matrix,
            matrix,
            matrix,
            matrix,
            vector,
            matrix,
            matrix,
            matrix,
            matrix,
        ),
        out_specs=(
            matrix,
            matrix,
            vector,
            matrix,
            matrix,
            matrix,
            matrix,
            vector,
            matrix,
            matrix,
            matrix,
        ),
        check_vma=False,
    )
```

```python
import functools
import math

import jax
import jax.numpy as jnp
from jax import lax
from jax.experimental import pallas as pl
from jax.experimental.pallas import tpu as pltpu
from jax.sharding import PartitionSpec as P


HEADS = 32
KV_HEADS = 4
HEAD = 64
EPSILON = 1e-05
THETA = 10000.0
SCALE = 0.125
MASKED = -1e30

GROUP = 8
TOK = 128
TOKENS = GROUP * TOK
D = 2048
MY_HEADS = HEADS // GROUP
COLS = D // GROUP
FF_ROWS = 44
FF_PAD = 48
FF_COLS = 16 * FF_PAD
KV_COLS = 2 * HEAD
QKV = COLS + KV_COLS
ATT = QKV + COLS
PACK = ATT + 2 * FF_COLS

MESH = pl.DeviceIdType.MESH
BF16 = jnp.bfloat16
F32 = jnp.float32
ANY = pl.BlockSpec(memory_space=pl.ANY)
VMEM = pl.BlockSpec(memory_space=pltpu.VMEM)


def place():
    me = lax.axis_index("dp")
    return me // 32, (me // 8) % 4, (me // 2) % 4, me % 2


def index(z, y, x, c):
    return ((z * 4 + y) * 4 + x) * 2 + c


def shifted(here, axis, step):
    spot = list(here)
    spot[axis] = (spot[axis] + step) % 4
    return index(*spot)


def group_peers(here):
    z, y, x, c = here
    return [
        ((x + dx) % 4 * 2 + (c + dc) % 2, index(z, y, (x + dx) % 4, (c + dc) % 2))
        for dx in (2, 1, 3, 0)
        for dc in (0, 1)
        if (dx, dc) != (0, 0)
    ]


GROUP_LINKS = [[(2, 1), (2, -1)]] * 2 + [[(2, 1)]] * 2 + [[(2, -1)]] * 2 + [["core"]]


def plane_peers(here):
    z, y, x, c = here
    return [
        (((z + dz) % 4, (y + dy) % 4), index((z + dz) % 4, (y + dy) % 4, x, c))
        for dz in range(4)
        for dy in range(4)
        if (dz, dy) != (0, 0)
    ]


def greet(partners):
    barrier = pltpu.get_barrier_semaphore()
    for partner in partners:
        pl.semaphore_signal(barrier, inc=1, device_id=(partner,), device_id_type=MESH)
    pl.semaphore_wait(barrier, len(partners))


HOP = 1.5
RATE = 46000.0
CORE_RATE = 450000.0


class Net:
    def __init__(self, send_sem, recv_sem, local_sem):
        self.sems = (send_sem, recv_sem, local_sem)
        self.sent, self.moved = 0, 0
        self.open = []
        self.now = 0.0
        self.free = {}
        self.due = {}
        self.tasks = []
        self.late = []

    def start(self, program, rank=0):
        task = Task(program, rank)
        self.tasks.append(task)
        self.tasks.sort(key=lambda t: t.rank)
        return task

    def queue(self, copy, ref, links):
        size = math.prod(ref.shape) * jnp.dtype(ref.dtype).itemsize
        done = self.now
        for link in links:
            rate = CORE_RATE if link == "core" else RATE
            self.free[link] = max(self.free.get(link, 0.0), self.now) + size / rate
            done = max(done, self.free[link])
        self.due[id(copy)] = done + HOP
        self.open.append(copy)

    def send(self, src, dst, device, *links):
        copy = pltpu.make_async_remote_copy(
            src_ref=src,
            dst_ref=dst,
            send_sem=self.sems[0].at[self.sent],
            recv_sem=self.sems[1].at[self.sent],
            device_id=(device,),
            device_id_type=MESH,
        )
        copy.start()
        self.sent += 1
        self.queue(copy, src, links)
        return copy

    def move(self, src, dst):
        copy = pltpu.make_async_copy(src, dst, self.sems[2].at[self.moved])
        copy.start()
        self.moved += 1
        self.due[id(copy)] = self.now + 1.0
        return copy

    def spend(self, time):
        self.now += time

    def ready(self, needs):
        times = [0.0]
        for need in needs:
            if isinstance(need, Task):
                times.append(0.0 if need.done else math.inf)
            else:
                times.append(self.due[id(need)])
        return max(times)

    def leave(self, src, dst):
        self.late.append(self.move(src, dst))

    def finish(self):
        for copy in self.open:
            copy.wait_send()
        for copy in self.late:
            copy.wait()


class Task:
    def __init__(self, program, rank):
        self.program, self.rank, self.needs, self.done = program, rank, [], False


def run(net, *programs):
    for program in programs:
        net.start(program)
    while net.tasks:
        times = [net.ready(task.needs) for task in net.tasks]
        at = next((i for i, time in enumerate(times) if time <= net.now), times.index(min(times)))
        net.now = max(net.now, times[at])
        task = net.tasks[at]
        needs = next(task.program, None)
        if needs is None:
            task.done = True
            net.tasks.remove(task)
        else:
            task.needs = needs


def ring_gather(net, here, axis, at, own=None):
    spot = here[axis]
    before, after = (spot + 3) % 4, (spot + 1) % 4
    up, down = shifted(here, axis, 1), shifted(here, axis, -1)
    source = (lambda part: at(spot, part)) if own is None else own
    one = net.send(source(0), at(spot, 0), up, (axis, 1))
    two = net.send(source(1), at(spot, 1), down, (axis, -1))
    three = net.send(source(1), at(spot, 1), up, (axis, 1))
    four = net.send(source(0), at(spot, 0), down, (axis, -1))
    kept = [] if own is None else [net.move(own(None), at(spot, None))]
    yield [one]
    one.wait_recv()
    five = net.send(at(before, 0), at(before, 0), up, (axis, 1))
    yield [two]
    two.wait_recv()
    six = net.send(at(after, 1), at(after, 1), down, (axis, -1))
    yield [three, four, five, six, *kept]
    for copy in (three, four, five, six):
        copy.wait_recv()
    for copy in kept:
        copy.wait()


def plane_gather(net, here, region, half, own, then=None):
    z, y = here[0], here[1]
    mine = functools.partial(own, half)
    if half == 0:
        yield from ring_gather(net, here, 1, lambda p, s: region(z, p, 0, s), mine)
        second = ring_gather(net, here, 0, lambda p, s: region(p, None, 0, s))
    else:
        yield from ring_gather(net, here, 0, lambda p, s: region(p, y, 1, s), mine)
        second = ring_gather(net, here, 1, lambda p, s: region(None, p, 1, s))
    needs = next(second)
    if then is not None:
        then()
    yield needs
    yield from second


def half_rows(ref, cols):
    def own(half, part):
        size = TOK // 2 if part is None else TOK // 4
        return ref.at[pl.ds(half * (TOK // 2) + (part or 0) * (TOK // 4), size), cols]

    return own


def half_cols(ref, width):
    def own(half, part):
        size = width // 2 if part is None else width // 4
        return ref.at[:, pl.ds(half * (width // 2) + (part or 0) * (width // 4), size)]

    return own


def group_gather(net, here, own, at):
    z, y, x, c = here
    right, left = shifted(here, 2, 1), shifted(here, 2, -1)
    peer = index(z, y, x, 1 - c)
    before, after, far = (x + 3) % 4 * 2 + c, (x + 1) % 4 * 2 + c, (x + 2) % 4 * 2 + c
    mine = x * 2 + c
    one = net.send(own(0), at(mine, 0), right, (2, 1))
    two = net.send(own(1), at(mine, 1), left, (2, -1))
    three = net.send(own(1), at(mine, 1), right, (2, 1))
    four = net.send(own(0), at(mine, 0), left, (2, -1))
    across = [net.send(own(None), at(mine, None), peer, "core")]
    kept = net.move(own(None), at(mine, None))
    yield [one]
    one.wait_recv()
    five = net.send(at(before, 0), at(before, 0), right, (2, 1))
    yield [two]
    two.wait_recv()
    six = net.send(at(after, 1), at(after, 1), left, (2, -1))
    yield [three]
    three.wait_recv()
    across.append(net.send(at(before, None), at(before, None), peer, "core"))
    yield [four]
    four.wait_recv()
    across.append(net.send(at(after, None), at(after, None), peer, "core"))
    yield [five]
    five.wait_recv()
    across.append(net.send(at(far, 0), at(far, 0), peer, "core"))
    yield [six]
    six.wait_recv()
    across.append(net.send(at(far, 1), at(far, 1), peer, "core"))
    yield [*across, kept]
    for copy in across:
        copy.wait_recv()
    kept.wait()


def group_exchange(net, here, src, dst):
    mine = here[2] * 2 + here[3]
    copies = [
        net.send(src(g), dst(mine), device, *links)
        for (g, device), links in zip(group_peers(here), GROUP_LINKS, strict=True)
    ]
    kept = net.move(src(mine), dst(mine))
    yield [*copies, kept]
    for copy in copies:
        copy.wait_recv()
    kept.wait()


def strips(rows, work, step=16):
    def body(i, carry):
        work(pl.ds(pl.multiple_of(i * step, step), step))
        return carry

    lax.fori_loop(0, rows // step, body, 0)


def add_into(total, term):
    if len(total.shape) == 3:
        for i in range(total.shape[0]):
            add_into(total.at[i], term.at[i])
        return

    def work(rows):
        total[rows] = (total[rows].astype(F32) + term[rows].astype(F32)).astype(total.dtype)

    strips(total.shape[0], work)


def add_up(out, *terms):
    if len(out.shape) == 3:
        for i in range(out.shape[0]):
            add_up(out.at[i], *[term.at[i] for term in terms])
        return

    def work(rows):
        total = terms[0][rows].astype(F32)
        for term in terms[1:]:
            total = total + term[rows].astype(F32)
        out[rows] = total.astype(out.dtype)

    strips(out.shape[0], work)


def group_reduce_scratch(rows, cols):
    return [
        pltpu.VMEM((4, rows, cols), BF16),
        pltpu.VMEM((2, rows // 2, cols), BF16),
        pltpu.VMEM((2, rows, cols), BF16),
    ]


class GroupReduce:
    ORDER = (2, 1, 3, 0)

    def __init__(self, net, here, src, out, scratch, extra=()):
        self.net, self.here, self.src, self.out, self.extra = net, here, src, out, extra
        self.crossed, self.relay, self.landed = scratch
        self.cross_copies = []

    def cross(self, slot):
        z, y, x, c = self.here
        there = (x + self.ORDER[slot]) % 4
        self.cross_copies.append(
            self.net.send(
                self.src(there * 2 + 1 - c), self.crossed.at[slot], index(z, y, x, 1 - c), "core"
            )
        )

    def steps(self):
        z, y, x, c = self.here
        net, cross = self.net, self.cross_copies
        crossed, relay, landed = self.crossed, self.relay, self.landed
        right, left = shifted(self.here, 2, 1), shifted(self.here, 2, -1)
        held = [self.src((x + step) % 4 * 2 + c) for step in self.ORDER]
        part = [
            [self.src((x + step) % 4 * 2 + c, half) for half in (0, 1)] for step in self.ORDER
        ]
        half = relay.shape[1]
        upper, lower = pl.ds(0, half), pl.ds(half, half)
        yield [cross[0]]
        cross[0].wait_recv()
        add_into(held[0], crossed.at[0])
        net.spend(1.0)
        one = net.send(part[0][0], relay.at[0], right, (2, 1))
        two = net.send(part[0][1], relay.at[1], left, (2, -1))
        yield [cross[1]]
        cross[1].wait_recv()
        add_into(held[1], crossed.at[1])
        net.spend(1.0)
        three = net.send(part[1][1], landed.at[0, lower], right, (2, 1))
        yield [cross[2]]
        cross[2].wait_recv()
        add_into(held[2], crossed.at[2])
        net.spend(1.0)
        four = net.send(part[2][0], landed.at[1, upper], left, (2, -1))
        yield [one]
        one.wait_recv()
        add_into(part[1][0], relay.at[0])
        net.spend(0.5)
        five = net.send(part[1][0], landed.at[0, upper], right, (2, 1))
        yield [two]
        two.wait_recv()
        add_into(part[2][1], relay.at[1])
        net.spend(0.5)
        six = net.send(part[2][1], landed.at[1, lower], left, (2, -1))
        yield [cross[3]]
        cross[3].wait_recv()
        add_into(held[3], crossed.at[3])
        net.spend(1.0)
        yield [three, four, five, six]
        for copy in (three, four, five, six):
            copy.wait_recv()
        add_up(self.out, held[3], landed.at[0], landed.at[1], *self.extra)
        net.spend(1.0)


def plane_reduce_scratch(rows, cols):
    return [
        pltpu.VMEM((2, 4, rows, cols), BF16),
        pltpu.VMEM((2, 4, rows, cols), BF16),
        pltpu.VMEM((2, 2, 4, rows, cols), BF16),
        pltpu.VMEM((2, 4, rows, cols), BF16),
        pltpu.VMEM((2, rows, cols), BF16),
        pltpu.VMEM((2, 2, rows, cols), BF16),
    ]


def plane_reduce(net, here, region, half, out, scratch):
    relay, passing, landed, total, relay_two, landed_two = scratch
    axis, other = (0, 1) if half == 0 else (1, 0)

    def at(position, part):
        return region(position, None, half, part) if half == 0 else region(None, position, half, part)

    spot = here[axis]
    up, down = shifted(here, axis, 1), shifted(here, axis, -1)
    after, before, far = (spot + 1) % 4, (spot + 3) % 4, (spot + 2) % 4
    one = net.send(at(far, 0), relay.at[0], up, (axis, 1))
    two = net.send(at(far, 1), relay.at[1], down, (axis, -1))
    three = net.send(at(after, 1), landed.at[0, 1], up, (axis, 1))
    four = net.send(at(before, 0), landed.at[1, 0], down, (axis, -1))
    moves = [
        net.move(at(after, 0), passing.at[0]),
        net.move(at(before, 1), passing.at[1]),
        net.move(at(spot, 0), total.at[0]),
        net.move(at(spot, 1), total.at[1]),
    ]
    cost = math.prod(relay.shape[1:]) / 250000
    yield [one, moves[0]]
    one.wait_recv()
    moves[0].wait()
    add_into(passing.at[0], relay.at[0])
    net.spend(cost)
    five = net.send(passing.at[0], landed.at[0, 0], up, (axis, 1))
    yield [two, moves[1]]
    two.wait_recv()
    moves[1].wait()
    add_into(passing.at[1], relay.at[1])
    net.spend(cost)
    six = net.send(passing.at[1], landed.at[1, 1], down, (axis, -1))
    yield [four, five, moves[2]]
    moves[2].wait()
    four.wait_recv()
    five.wait_recv()
    add_up(total.at[0], total.at[0], landed.at[0, 0], landed.at[1, 0])
    net.spend(cost)
    spot = here[other]
    up, down = shifted(here, other, 1), shifted(here, other, -1)
    after, before, far = (spot + 1) % 4, (spot + 3) % 4, (spot + 2) % 4
    seven = net.send(total.at[0, far], relay_two.at[0], up, (other, 1))
    eight = net.send(total.at[0, before], landed_two.at[1, 0], down, (other, -1))
    yield [three, six, moves[3]]
    moves[3].wait()
    three.wait_recv()
    six.wait_recv()
    add_up(total.at[1], total.at[1], landed.at[0, 1], landed.at[1, 1])
    net.spend(cost)
    nine = net.send(total.at[1, far], relay_two.at[1], down, (other, -1))
    ten = net.send(total.at[1, after], landed_two.at[0, 1], up, (other, 1))
    yield [seven]
    seven.wait_recv()
    add_into(total.at[0, after], relay_two.at[0])
    net.spend(cost / 4)
    eleven = net.send(total.at[0, after], landed_two.at[0, 0], up, (other, 1))
    yield [nine]
    nine.wait_recv()
    add_into(total.at[1, before], relay_two.at[1])
    net.spend(cost / 4)
    twelve = net.send(total.at[1, before], landed_two.at[1, 1], down, (other, -1))
    yield [eight, eleven]
    eight.wait_recv()
    eleven.wait_recv()
    add_up(out(0), total.at[0, spot], landed_two.at[0, 0], landed_two.at[1, 0])
    net.spend(cost / 4)
    yield [ten, twelve]
    ten.wait_recv()
    twelve.wait_recv()
    add_up(out(1), total.at[1, spot], landed_two.at[0, 1], landed_two.at[1, 1])
    net.spend(cost / 4)


def by_rows(ref, rows, cols):
    def region(z, y, half, part):
        size = rows // 2 if part is None else rows // 4
        start = half * (rows // 2) + (0 if part is None else part * (rows // 4))
        return ref.at[
            slice(None) if z is None else z, slice(None) if y is None else y, pl.ds(start, size), cols
        ]

    return region


def by_cols(ref, cols):
    def region(z, y, half, part):
        size = cols // 2 if part is None else cols // 4
        start = half * (cols // 2) + (0 if part is None else part * (cols // 4))
        return ref.at[
            slice(None) if z is None else z, slice(None) if y is None else y, :, pl.ds(start, size)
        ]

    return region


def row_block(ref, rows):
    def at(g, part=None):
        size = rows if part is None else rows // 2
        start = g * rows + (0 if part is None else part * (rows // 2))
        return ref.at[pl.ds(pl.multiple_of(start, rows // 2), size)]

    return at


def col_block(ref, rows, cols, first=0):
    def at(g, part=None):
        size = rows if part is None else rows // 2
        start = first + (0 if part is None else part * (rows // 2))
        return ref.at[pl.ds(start, size), pl.ds(pl.multiple_of(g * cols, cols), cols)]

    return at


def halves(ref, rows, first=0):
    def own(part):
        size = rows if part is None else rows // 2
        return ref.at[pl.ds(first + (0 if part is None else part * (rows // 2)), size)]

    return own


def ring_partners(here, axes):
    return [shifted(here, axis, step) for axis in axes for step in (1, -1)]


def core_peer(here):
    return index(here[0], here[1], here[2], 1 - here[3])


def communicate(kernel, collective_id, outs, scratch, n_sends, n_moves, name, inside=()):
    def call(*args):
        def body(*refs):
            n_in, n_out = len(args), len(outs)
            send_sem, recv_sem, local_sem = refs[-3:]
            net = Net(send_sem, recv_sem, local_sem)
            kernel(net, place(), refs[:n_in], refs[n_in : n_in + n_out], refs[n_in + n_out : -3])
            net.finish()

        return pl.pallas_call(
            body,
            out_shape=[jax.ShapeDtypeStruct(shape, dtype) for shape, dtype, _ in outs],
            in_specs=[VMEM if i in inside else ANY for i in range(len(args))],
            out_specs=[VMEM if near else ANY for _, _, near in outs],
            scratch_shapes=list(scratch)
            + [
                pltpu.SemaphoreType.DMA((n_sends,)),
                pltpu.SemaphoreType.DMA((n_sends,)),
                pltpu.SemaphoreType.DMA((max(n_moves, 1),)),
            ],
            compiler_params=pltpu.CompilerParams(
                collective_id=collective_id, has_side_effects=True, vmem_limit_bytes=60 << 20
            ),
            name=name,
        )(*args)

    return call


def chunk(i, size):
    return pl.ds(pl.multiple_of(i * size, size), size)


def loop(count, work):
    def body(i, carry):
        work(i)
        return carry

    lax.fori_loop(0, count, body, 0)


def lanes(shape):
    return lax.broadcasted_iota(jnp.int32, shape, 1)


def tables(aux):
    lane = lanes(aux.shape)
    by = [aux] + [pltpu.roll(aux, 32 * k, 1) for k in (1, 2, 3)]
    cosine = jnp.where(lane < 32, by[0], jnp.where(lane < 64, by[1], jnp.where(lane < 96, by[2], by[3])))
    sine = jnp.where(lane < 32, by[3], jnp.where(lane < 64, by[0], jnp.where(lane < 96, by[1], by[2])))
    sine = jnp.where(lane % 64 < 32, -sine, sine)
    begin = jnp.where(lane < 64, by[2], by[0])
    return cosine, sine, begin


def turn(values, cosine, sine):
    width = values.shape[1]
    if width > 128:
        cosine, sine = (jnp.concatenate([t] * (width // 128), axis=1) for t in (cosine, sine))
    partner = jnp.where(
        lanes(values.shape) % 64 < 32,
        pltpu.roll(values, width - 32, 1),
        pltpu.roll(values, 32, 1),
    )
    return values * cosine + partner * sine


def allowed_keys(begin):
    key = lanes(begin.shape).astype(F32)
    query = lax.broadcasted_iota(jnp.int32, begin.shape, 0).astype(F32)
    return (key >= begin) & (key <= query)


def doubled(keyed):
    lane, other = lanes(keyed.shape), pltpu.roll(keyed, 64, 1)
    keys = jnp.where(lane < 64, keyed, other).astype(BF16)
    values = jnp.where(lane < 64, other, keyed).astype(BF16)
    return keys, values


def only_half(pair, side):
    lane = lanes(pair.shape)
    keep = lane < 64 if side == 0 else lane >= 64
    return jnp.where(keep, pair, jnp.zeros_like(pair))


def probabilities(query, keys, allowed):
    scores = jnp.where(allowed, dot_last(query, keys) * SCALE, MASKED)
    powers = jnp.exp(scores - jnp.max(scores, axis=-1, keepdims=True))
    return powers / jnp.sum(powers, axis=-1, keepdims=True)


def forward(net, here, inputs, outputs, scratch):
    packed, tokens, aux, meta, down = inputs
    wide_out, gate_out, up_out, narrow_out, normed_out, qkv_out, attended_out, residual_out = outputs[:8]
    all_aux, all_meta = outputs[8:]
    (
        all_tokens,
        normed,
        own,
        wide,
        gate,
        up,
        narrow,
        linear,
        qkv,
        mine_attended,
        attended,
        mine_residual,
        residual,
        seen,
        mine_meta,
        gain,
    ) = scratch
    z, y, x, c = here
    mine = x * 2 + c
    greet([device for _, device in group_peers(here)] + [device for _, device in plane_peers(here)])

    def small():
        copies = [net.send(meta, seen.at[mine], device) for _, device in group_peers(here)]
        kept = net.move(meta, seen.at[mine])
        yield [*copies, kept]
        for copy in copies:
            copy.wait_recv()
        kept.wait()
        mine_meta[...] = jnp.sum(seen[...], axis=0)
        spots = all_meta.at[z * 4 + y]
        copies = [net.send(mine_meta, spots, device) for _, device in plane_peers(here)]
        all_meta[z * 4 + y] = mine_meta[...]
        net.spend(1.0)
        yield copies
        for copy in copies:
            copy.wait_recv()
        for spot in range(16):
            gain[:, pl.ds(spot * 128, 128)] = all_meta[spot, 0:1, :]

    def rows_of(ref):
        return lambda g: ref.at[pl.ds(pl.multiple_of(g * 16, 16), 16)]

    parts = [
        (by_rows(wide, TOK, slice(None)), half_rows(own, pl.ds(0, ATT))),
        (by_rows(gate, TOK, slice(None)), half_rows(own, pl.ds(ATT, FF_COLS))),
        (by_rows(up, TOK, slice(None)), half_rows(own, pl.ds(ATT + FF_COLS, FF_COLS))),
        (by_cols(narrow, D), half_cols(down, D)),
    ]
    tasks = {}

    def gather_part(i):
        region, source = parts[i]
        for half in (0, 1):
            follow = functools.partial(gather_part, i + 1) if half == 1 and i + 1 < len(parts) else None
            tasks[i, half] = net.start(plane_gather(net, here, region, half, source, follow))

    def exchange():
        yield from group_exchange(net, here, lambda g: packed.at[g], rows_of(own))
        gather_part(0)

    def attend(i):
        rows = chunk(i, TOK)
        cosine, sine, begin = tables(all_aux[rows])
        allowed = allowed_keys(begin)
        turned = turn(linear[rows, :COLS], cosine, sine).astype(BF16)
        keyed = linear[rows, COLS:]
        keyed = jnp.where(lanes(keyed.shape) < 64, turn(keyed, cosine, sine), keyed)
        keys, values = doubled(keyed)
        qkv[rows, :COLS] = turned
        qkv[rows, COLS:] = keyed.astype(BF16)
        for pair in range(MY_HEADS // 2):
            both = turned[:, pair * 128 : pair * 128 + 128]
            sides = []
            for side in (0, 1):
                probs = probabilities(only_half(both, side), keys, allowed)
                sides.append(matmul(probs.astype(BF16), values))
            out = jnp.where(lanes(sides[0].shape) < 64, sides[0], sides[1])
            mine_attended[rows, pair * 128 : pair * 128 + 128] = out.astype(BF16)

    def normalise(strip):
        values = all_tokens[strip].astype(F32)
        scale = lax.rsqrt(jnp.mean(values * values, axis=-1, keepdims=True) + EPSILON)
        normed[strip] = (values * scale * gain[...]).astype(BF16)

    half_tokens = TOKENS // 2

    def work():
        yield [gains, took]
        strips(TOKENS, normalise)
        net.spend(3.0)
        net.leave(normed, normed_out)
        yield [exchanged, placed]
        yield [tasks[0, 0], tasks[0, 1]]
        net.leave(wide, wide_out)

        def project(i):
            rows = chunk(i, 256)
            linear[rows] = matmul(normed[rows], wide[:, :, :, :QKV].reshape(D, QKV))

        sent = []
        for half in (0, 1):
            loop(2, lambda i, half=half: project(i + 2 * half))
            loop(4, lambda i, half=half: attend(i + 4 * half))
            net.spend(5.0)
            first = half * half_tokens
            at = col_block(attended, half_tokens, COLS, first)
            sent.append(net.start(group_gather(net, here, halves(mine_attended, half_tokens, first), at)))
            yield []
        net.leave(qkv, qkv_out)
        my_cols = pl.ds(pl.multiple_of(mine * COLS, COLS), COLS)

        def add_attended(i):
            rows = chunk(i, 256)
            out = matmul(attended[rows], wide[:, :, :, QKV:].reshape(D, COLS))
            mine_residual[rows] = (all_tokens[rows, my_cols].astype(F32) + out).astype(BF16)

        last = []
        for half in (0, 1):
            yield [sent[half]]
            loop(2, lambda i, half=half: add_attended(i + 2 * half))
            net.spend(1.0)
            first = half * half_tokens
            at = col_block(residual, half_tokens, COLS, first)
            last.append(net.start(group_gather(net, here, halves(mine_residual, half_tokens, first), at)))
        net.leave(attended, attended_out)
        for i, (ref, out) in enumerate(((gate, gate_out), (up, up_out), (narrow, narrow_out))):
            yield [tasks[i + 1, 0], tasks[i + 1, 1]]
            net.leave(ref, out)
        yield last
        net.leave(residual, residual_out)

    exchanged = net.start(exchange())
    gains = net.start(small())
    took = net.start(group_gather(net, here, halves(tokens, TOK), row_block(all_tokens, TOK)))
    placed = net.start(group_gather(net, here, halves(aux, TOK), row_block(all_aux, TOK)))
    net.start(work(), rank=1)
    run(net)


def forward_call(*args):
    outs = [
        ((4, 4, TOK, ATT), BF16, False),
        ((4, 4, TOK, FF_COLS), BF16, False),
        ((4, 4, TOK, FF_COLS), BF16, False),
        ((4, 4, FF_PAD, D), BF16, False),
        ((TOKENS, D), BF16, False),
        ((TOKENS, QKV), BF16, False),
        ((TOKENS, D), BF16, False),
        ((TOKENS, D), BF16, False),
        ((TOKENS, 128), F32, True),
        ((16, 8, 128), F32, True),
    ]
    scratch = [
        pltpu.VMEM((TOKENS, D), BF16),
        pltpu.VMEM((TOKENS, D), BF16),
        pltpu.VMEM((TOK, PACK), BF16),
        pltpu.VMEM((4, 4, TOK, ATT), BF16),
        pltpu.VMEM((4, 4, TOK, FF_COLS), BF16),
        pltpu.VMEM((4, 4, TOK, FF_COLS), BF16),
        pltpu.VMEM((4, 4, FF_PAD, D), BF16),
        pltpu.VMEM((TOKENS, QKV), F32),
        pltpu.VMEM((TOKENS, QKV), BF16),
        pltpu.VMEM((TOKENS, COLS), BF16),
        pltpu.VMEM((TOKENS, D), BF16),
        pltpu.VMEM((TOKENS, COLS), BF16),
        pltpu.VMEM((TOKENS, D), BF16),
        pltpu.VMEM((8, 8, 128), F32),
        pltpu.VMEM((8, 128), F32),
        pltpu.VMEM((1, D), F32),
    ]
    return communicate(forward, 0, outs, scratch, 200, 40, "forward")(*args)


def feed_forward(net, here, inputs, outputs, scratch):
    residual, gate_w, up_w, down_w, upstream, gain = inputs
    grad_out, mixed_out, down_out, grad_gate, grad_up = outputs
    (
        normed,
        weight,
        narrow,
        all_upstream,
        gate,
        up,
        active,
        grad_gate_lin,
        grad_up_lin,
        mixed_part,
        grad_part,
        grad_down,
        stage,
    ) = scratch[:13]
    own_residual = scratch[-1]
    x = here[2]
    member = x * 2 + here[3]
    loads = [
        net.move(residual, grad_part),
        net.move(gate_w, weight.at[0]),
        net.move(up_w, weight.at[1]),
        net.move(down_w, narrow),
        net.move(row_block(residual, TOK)(member), own_residual),
    ]
    greet(ring_partners(here, (0, 1, 2)) + [core_peer(here)])
    rows = TOKENS // 4
    gather = net.start(group_gather(net, here, halves(upstream, TOK), row_block(all_upstream, TOK)))

    def normalise(strip):
        values = grad_part[strip].astype(F32)
        scale = lax.rsqrt(jnp.mean(values * values, axis=-1, keepdims=True) + EPSILON)
        normed[strip] = (values * scale * gain[...]).astype(BF16)

    def expand(i):
        here_rows = chunk(i, rows)
        for j in range(FF_COLS // 256):
            cols = pl.ds(j * 256, 256)
            gate_val = matmul(normed[here_rows], weight[0, :, cols])
            up_val = matmul(normed[here_rows], weight[1, :, cols])
            sigmoid_gate = 1.0 / (1.0 + jnp.exp(-gate_val))
            silu_gate = gate_val * sigmoid_gate
            active[here_rows, cols] = (silu_gate * up_val).astype(BF16)
            gate[here_rows, cols] = silu_gate.astype(BF16)
            up[here_rows, cols] = (
                up_val * sigmoid_gate * (1.0 + gate_val * (1.0 - sigmoid_gate))
            ).astype(BF16)

    def down(j):
        cols = chunk(j, 256)
        for p in range(2):
            part = dot_first(active[:, pl.ds(p * 384, 384)], all_upstream[:, cols])
            grad_down[2 * p : 2 * p + 2, :, :, cols] = part.astype(BF16).reshape(2, 4, FF_PAD, 256)

    def backward(i):
        here_rows = chunk(i, rows)
        for j in range(FF_COLS // 256):
            cols = pl.ds(j * 256, 256)
            grad_active = dot_last(all_upstream[here_rows], narrow[cols])
            grad_up_lin[here_rows, cols] = (grad_active * gate[here_rows, cols].astype(F32)).astype(BF16)
            grad_gate_lin[here_rows, cols] = (grad_active * up[here_rows, cols].astype(F32)).astype(BF16)

    quarter = D // 4
    region = by_cols(grad_down, D)

    def narrow_part(half):
        return lambda part: down_out.at[:, pl.ds((half * 2 + part) * quarter, quarter)]

    mix = GroupReduce(net, here, row_block(mixed_part, TOK), mixed_out, scratch[13:16], [own_residual])
    back = GroupReduce(net, here, row_block(grad_part, TOK), grad_out, scratch[16:19])

    def work():
        loads[0].wait()
        strips(TOKENS, normalise)
        net.spend(3.0)
        loads[1].wait()
        loads[2].wait()
        loop(2, expand)
        net.spend(6.0)
        yield []
        loop(2, lambda i: expand(i + 2))
        net.spend(6.0)
        yield []
        loads[3].wait()
        loads[4].wait()
        for slot, step in enumerate(GroupReduce.ORDER):
            there = chunk((x + step) % 4, rows)

            def mixed(j):
                cols = chunk(j, 512)
                mixed_part[there, cols] = matmul(active[there], narrow[:, cols]).astype(BF16)

            loop(D // 512, mixed)
            net.spend(1.2)
            mix.cross(slot)
            yield []
        net.start(mix.steps())
        yield [gather]
        loop(D // 256, down)
        net.spend(4.5)
        for half in (0, 1):
            room = scratch[19 + 6 * half : 25 + 6 * half]
            net.start(plane_reduce(net, here, region, half, narrow_part(half), room))
        yield []
        loop(2, backward)
        net.spend(3.0)
        yield []
        loop(2, lambda i: backward(i + 2))
        net.spend(3.0)
        yield []
        for slot, step in enumerate(GroupReduce.ORDER):
            there = chunk((x + step) % 4, rows)

            def to_input(j):
                cols = chunk(j, 512)
                total = dot_last(grad_gate_lin[there], weight[0, cols])
                total = total + dot_last(grad_up_lin[there], weight[1, cols])
                grad_part[there, cols] = total.astype(BF16)

            loop(D // 512, to_input)
            net.spend(2.3)
            back.cross(slot)
            yield []
        net.start(back.steps())
        yield []
        outs = [None, None]
        for m in range(D // 256):
            slot = m % 2
            if outs[slot] is not None:
                for copy in outs[slot]:
                    copy.wait()
            rows_of = normed[:, pl.ds(m * 256, 256)]
            stage[slot, 0] = dot_first(rows_of, grad_gate_lin[...]).astype(BF16)
            stage[slot, 1] = dot_first(rows_of, grad_up_lin[...]).astype(BF16)
            outs[slot] = [
                net.move(stage.at[slot, 0], grad_gate.at[pl.ds(m * 256, 256)]),
                net.move(stage.at[slot, 1], grad_up.at[pl.ds(m * 256, 256)]),
            ]
            net.spend(1.2)
            yield []
        for pair in outs:
            for copy in pair:
                copy.wait()

    net.start(work(), rank=1)
    run(net)


def feed_scratch():
    return (
        [
            pltpu.VMEM((TOKENS, D), BF16),
            pltpu.VMEM((2, D, FF_COLS), BF16),
            pltpu.VMEM((FF_COLS, D), BF16),
            pltpu.VMEM((TOKENS, D), BF16),
        ]
        + [pltpu.VMEM((TOKENS, FF_COLS), BF16)] * 5
        + [
            pltpu.VMEM((TOKENS, D), BF16),
            pltpu.VMEM((TOKENS, D), BF16),
            pltpu.VMEM((4, 4, FF_PAD, D), BF16),
            pltpu.VMEM((2, 2, 256, FF_COLS), BF16),
        ]
        + group_reduce_scratch(TOK, D) * 2
        + plane_reduce_scratch(FF_PAD, D // 4) * 2
        + [pltpu.VMEM((TOK, D), BF16)]
    )


def quarter_rows(ref):
    return lambda half: lambda part: ref.at[pl.ds((half * 2 + part) * (TOK // 4), TOK // 4)]


def backward(net, here, inputs, outputs, scratch):
    (
        grad_normed_two,
        all_residual,
        upstream,
        tokens,
        all_meta,
        all_aux,
        qkv_in,
        wide_in,
        normed_in,
        attended_in,
        gate_in,
        up_in,
    ) = inputs
    grad_tokens, norms_out, gate_rows, up_rows, att_rows = outputs
    (
        grad_two,
        residual,
        own_upstream,
        own_tokens,
        grad_residual,
        grad_rounded,
        gains,
        terms,
        grad_cols,
        wide,
        heads_part,
        heads,
        qkv,
        grad_lin,
        normed,
        attended,
        input_part,
        grad_one,
        grad_gate,
        grad_up,
        grad_att,
        gate_sum,
        up_sum,
        att_sum,
        norms,
        seen,
        kept_norms,
        again,
    ) = scratch[:28]
    rest = scratch[28:]
    z, y, x, c = here
    mine = x * 2 + c
    loads = {
        "grad_two": net.move(grad_normed_two, grad_two),
        "residual": net.move(row_block(all_residual, TOK)(mine), residual),
        "upstream": net.move(upstream, own_upstream),
        "gate": net.move(gate_in, grad_gate),
        "wide": net.move(wide_in, wide),
        "up": net.move(up_in, grad_up),
        "qkv": net.move(qkv_in, qkv),
        "attended": net.move(attended_in, attended),
        "normed": net.move(normed_in, normed),
        "tokens": net.move(tokens, own_tokens),
    }
    greet([device for _, device in group_peers(here)] + [device for _, device in plane_peers(here)])

    def rows_of(ref):
        return lambda g: ref.at[pl.ds(pl.multiple_of(g * 16, 16), 16)]

    def feed_gradients():
        for name, source, total, out, room in (
            ("gate", grad_gate, gate_sum, gate_rows, rest[0:12]),
            ("up", grad_up, up_sum, up_rows, rest[12:24]),
        ):
            yield [loads[name]]
            loads[name].wait()
            yield [give_back(source, total, out, room)]

    def give_back(source, total, out, room):
        region, part = by_rows(source, TOK, slice(None)), quarter_rows(total)
        tasks = [
            net.start(plane_reduce(net, here, region, half, part(half), room[6 * half : 6 * half + 6]))
            for half in (0, 1)
        ]

        def hand_out():
            yield tasks
            yield from group_exchange(net, here, rows_of(total), lambda g: out.at[g])

        net.start(hand_out())
        return tasks[1]

    def residual_back(strip):
        values = residual[strip].astype(F32)
        scale = lax.rsqrt(jnp.mean(values * values, axis=-1, keepdims=True) + EPSILON)
        unit = values * scale
        grad = grad_two[strip]
        terms[1:2] += jnp.sum(grad * unit, axis=0, keepdims=True)
        grad = grad * gains[1:2]
        grad = scale * (grad - unit * jnp.mean(grad * unit, axis=-1, keepdims=True))
        grad = own_upstream[strip].astype(F32) + grad
        grad_residual[strip] = grad
        grad_rounded[strip] = grad.astype(BF16)

    def input_back(strip):
        values = own_tokens[strip].astype(F32)
        scale = lax.rsqrt(jnp.mean(values * values, axis=-1, keepdims=True) + EPSILON)
        unit = values * scale
        grad = grad_one[strip]
        terms[0:1] += jnp.sum(grad * unit, axis=0, keepdims=True)
        grad = grad * gains[0:1]
        grad = scale * (grad - unit * jnp.mean(grad * unit, axis=-1, keepdims=True))
        grad_tokens[strip] = grad_residual[strip] + grad

    def attend_back(i):
        rows = chunk(i, TOK)
        cosine, sine, begin = tables(all_aux[rows])
        allowed = allowed_keys(begin)
        keys, values = doubled(qkv[rows, COLS:].astype(F32))
        grad_queries = []
        grad_keys = jnp.zeros((TOK, 128), F32)
        grad_values = jnp.zeros((TOK, 128), F32)
        for pair in range(MY_HEADS // 2):
            cols = pl.ds(pair * 128, 128)
            queries, grads = qkv[rows, cols], heads[rows, cols]
            sides = []
            for side in (0, 1):
                query, grad = only_half(queries, side), only_half(grads, side)
                probs = probabilities(query, keys, allowed)
                grad_probs = dot_last(grad, values)
                grad_scores = probs * (grad_probs - jnp.sum(probs * grad_probs, axis=-1, keepdims=True))
                grad_scores = grad_scores.astype(BF16)
                sides.append(matmul(grad_scores, keys))
                grad_keys = grad_keys + dot_first(grad_scores, query)
                grad_values = grad_values + dot_first(probs.astype(BF16), grad)
            grad_queries.append(jnp.where(lanes(sides[0].shape) < 64, sides[0], sides[1]))
        grad_query = jnp.concatenate(grad_queries, axis=1) * SCALE
        grad_lin[rows, :COLS] = turn(grad_query, cosine, -sine).astype(BF16)
        grad_keys = turn((grad_keys + pltpu.roll(grad_keys, 64, 1)) * SCALE, cosine, -sine)
        grad_values = grad_values + pltpu.roll(grad_values, 64, 1)
        grad_lin[rows, COLS:] = jnp.where(lanes(grad_keys.shape) < 64, grad_keys, grad_values).astype(BF16)

    half_tokens = TOKENS // 2

    def work():
        for name in ("grad_two", "residual", "upstream"):
            loads[name].wait()
        for spot in range(16):
            gains[:, pl.ds(spot * 128, 128)] = all_meta[spot]
        terms[...] = jnp.zeros_like(terms)
        strips(TOK, residual_back)
        net.spend(2.0)
        spread = net.start(
            group_exchange(net, here, col_block(grad_rounded, TOK, COLS), row_block(grad_cols, TOK))
        )
        yield []
        loads["wide"].wait()
        yield [spread]
        reduced = []
        for half in (0, 1):
            first = half * half_tokens
            rows = pl.ds(first, half_tokens)
            room = rest[36 + 3 * half : 39 + 3 * half]
            reduce = GroupReduce(
                net, here, col_block(heads_part, half_tokens, COLS, first), heads.at[rows], room
            )
            for slot, step in enumerate(GroupReduce.ORDER):
                cols = chunk((x + step) % 4, 2 * COLS)
                part = dot_last(grad_cols[rows], wide[cols, QKV:])
                heads_part[rows, cols] = part.astype(BF16)
                net.spend(0.6)
                reduce.cross(slot)
            reduced.append(net.start(reduce.steps()))
        yield []
        loads["attended"].wait()

        def out_gradient(m):
            part = dot_first(attended[:, chunk(m, 256)], grad_cols[...]).astype(BF16)
            grad_att[m // 2, pl.ds(m % 2 * 2, 2), :, QKV:] = part.reshape(2, TOK, COLS)

        for half in (0, 1):
            loop(4, lambda m, half=half: out_gradient(m + 4 * half))
            net.spend(2.3)
            yield []
        loads["qkv"].wait()
        for half in (0, 1):
            yield [reduced[half]]
            loop(4, lambda i, half=half: attend_back(i + 4 * half))
            net.spend(6.0)
        reduce = GroupReduce(net, here, row_block(input_part, TOK), grad_one, rest[42:45])
        for slot, step in enumerate(GroupReduce.ORDER):
            there = chunk((x + step) % 4, 256)

            def to_input(j):
                cols = chunk(j, 512)
                part = dot_last(grad_lin[there], wide[cols, :QKV])
                input_part[there, cols] = part.astype(BF16)

            loop(D // 512, to_input)
            net.spend(1.3)
            reduce.cross(slot)
            yield []
        reduced = net.start(reduce.steps())
        loads["normed"].wait()

        def in_gradient(m):
            part = dot_first(normed[:, chunk(m, 256)], grad_lin[...]).astype(BF16)
            grad_att[m // 2, pl.ds(m % 2 * 2, 2), :, :QKV] = part.reshape(2, TOK, QKV)

        loop(8, in_gradient)
        net.spend(3.5)
        give_back(grad_att, att_sum, att_rows, rest[24:36])
        loads["tokens"].wait()
        yield [reduced]
        strips(TOK, input_back)
        net.spend(2.0)
        norms[...] = jnp.zeros_like(norms)
        for spot in range(16):
            norms[spot, 0:2] = terms[0:2, pl.ds(spot * 128, 128)]
        here_spot = z * 4 + y
        copies = [
            net.send(norms.at[to[0] * 4 + to[1]], seen.at[here_spot], device)
            for to, device in plane_peers(here)
        ]
        seen[here_spot] = norms[here_spot]
        yield copies
        for copy in copies:
            copy.wait_recv()
        kept_norms[...] = jnp.sum(seen[...], axis=0)
        again[mine] = kept_norms[...]
        copies = [net.send(kept_norms, again.at[mine], device) for _, device in group_peers(here)]
        yield copies
        for copy in copies:
            copy.wait_recv()
        norms_out[...] = jnp.sum(again[...], axis=0)

    net.start(feed_gradients())
    net.start(work(), rank=1)
    run(net)


def backward_call(*args):
    outs = [
        ((TOK, D), F32, True),
        ((8, 128), F32, True),
        ((GROUP, 16, FF_COLS), BF16, False),
        ((GROUP, 16, FF_COLS), BF16, False),
        ((GROUP, 16, ATT), BF16, False),
    ]
    scratch = [
        pltpu.VMEM((TOK, D), F32),
        pltpu.VMEM((TOK, D), BF16),
        pltpu.VMEM((TOK, D), BF16),
        pltpu.VMEM((TOK, D), BF16),
        pltpu.VMEM((TOK, D), F32),
        pltpu.VMEM((TOK, D), BF16),
        pltpu.VMEM((8, D), F32),
        pltpu.VMEM((8, D), F32),
        pltpu.VMEM((TOKENS, COLS), BF16),
        pltpu.VMEM((D, ATT), BF16),
        pltpu.VMEM((TOKENS, D), BF16),
        pltpu.VMEM((TOKENS, COLS), BF16),
        pltpu.VMEM((TOKENS, QKV), BF16),
        pltpu.VMEM((TOKENS, QKV), BF16),
        pltpu.VMEM((TOKENS, D), BF16),
        pltpu.VMEM((TOKENS, D), BF16),
        pltpu.VMEM((TOKENS, D), BF16),
        pltpu.VMEM((TOK, D), F32),
        pltpu.VMEM((4, 4, TOK, FF_COLS), BF16),
        pltpu.VMEM((4, 4, TOK, FF_COLS), BF16),
        pltpu.VMEM((4, 4, TOK, ATT), BF16),
        pltpu.VMEM((TOK, FF_COLS), BF16),
        pltpu.VMEM((TOK, FF_COLS), BF16),
        pltpu.VMEM((TOK, ATT), BF16),
        pltpu.VMEM((16, 8, 128), F32),
        pltpu.VMEM((16, 8, 128), F32),
        pltpu.VMEM((8, 128), F32),
        pltpu.VMEM((8, 8, 128), F32),
    ]
    scratch += plane_reduce_scratch(TOK // 4, FF_COLS) * 4 + plane_reduce_scratch(TOK // 4, ATT) * 2
    scratch += group_reduce_scratch(TOKENS // 2, COLS) * 2 + group_reduce_scratch(TOK, D)
    return communicate(backward, 1, outs, scratch, 180, 60, "backward", inside=(4, 5))(*args)


def sequence_table(lengths):
    ends = jnp.cumsum(lengths)
    places = jnp.arange(TOK, dtype=jnp.int32)
    begins = jnp.max(jnp.where(places[:, None] >= ends[None, :], ends[None, :], 0), axis=-1)
    inverse = jnp.exp(jnp.arange(HEAD // 2, dtype=F32) * (-2.0 * math.log(THETA) / HEAD))
    angle = (places - begins).astype(F32)[:, None] * inverse[None, :]
    start = jnp.broadcast_to(begins.astype(F32)[:, None], (TOK, 64))
    return jnp.concatenate([jnp.cos(angle), jnp.sin(angle), start], axis=1)


def matmul(left, right):
    return jnp.dot(left, right, preferred_element_type=F32)


def dot_last(left, right):
    return lax.dot_general(left, right, (((1,), (1,)), ((), ())), preferred_element_type=F32)


def dot_first(left, right):
    return lax.dot_general(left, right, (((0,), (0,)), ((), ())), preferred_element_type=F32)


def pack_columns(w_query, w_key, w_value, w_out, w_gate, w_up):
    def even(w):
        return w.reshape(16, GROUP, COLS).transpose(1, 0, 2)

    def feed(w):
        parts = w.reshape(16, 16, GROUP, FF_ROWS).transpose(2, 0, 1, 3)
        parts = jnp.pad(parts, ((0, 0), (0, 0), (0, 0), (0, FF_PAD - FF_ROWS)))
        return parts.reshape(GROUP, 16, FF_COLS)

    keyed = jnp.concatenate(
        [w_key.reshape(16, KV_HEADS, HEAD), w_value.reshape(16, KV_HEADS, HEAD)], axis=-1
    )
    keyed = jnp.repeat(keyed.transpose(1, 0, 2), 2, axis=0)
    return jnp.concatenate([even(w_query), keyed, even(w_out), feed(w_gate), feed(w_up)], axis=-1)


def on_device(
    tokens,
    seq_lengths,
    attn_norm,
    w_query,
    w_key,
    w_value,
    w_out,
    mlp_norm,
    w_gate,
    w_up,
    w_down,
    cotangent,
):
    me = lax.axis_index("dp")
    member = me % GROUP
    meta = jnp.stack([attn_norm.astype(F32), mlp_norm.astype(F32)])
    meta = lax.dynamic_update_slice(jnp.zeros((8, 128), F32), meta, (0, member * 16))
    packed = pack_columns(w_query, w_key, w_value, w_out, w_gate, w_up)
    down_rows = jnp.pad(w_down, ((0, FF_PAD - FF_ROWS), (0, 0)))
    (
        wide,
        gate_w,
        up_w,
        narrow,
        normed,
        qkv,
        all_attended,
        all_residual,
        all_aux,
        all_meta,
    ) = forward_call(packed, tokens, sequence_table(seq_lengths[0]), meta, down_rows)
    wide = wide.reshape(D, ATT)
    mlp_gain = all_meta[:, 1, :].reshape(1, D)

    grad_normed_two, mixed_out, down_sum, grad_gate, grad_up = communicate(
        feed_forward,
        3,
        [
            ((TOK, D), F32, True),
            ((TOK, D), BF16, True),
            ((FF_PAD, D), F32, True),
            ((D, FF_COLS), BF16, False),
            ((D, FF_COLS), BF16, False),
        ],
        feed_scratch(),
        80,
        40,
        "feed_forward",
        inside=(5,),
    )(
        all_residual,
        gate_w.reshape(D, FF_COLS),
        up_w.reshape(D, FF_COLS),
        narrow.reshape(FF_COLS, D),
        cotangent,
        mlp_gain,
    )

    grad_tokens, norm_sums, gate_rows, up_rows, att_rows = backward_call(
        grad_normed_two,
        all_residual,
        cotangent,
        tokens,
        all_meta,
        all_aux,
        qkv,
        wide,
        normed,
        all_attended,
        grad_gate.reshape(4, 4, TOK, FF_COLS),
        grad_up.reshape(4, 4, TOK, FF_COLS),
    )

    def even(part):
        return part.transpose(1, 0, 2).reshape(16, D).astype(F32)

    def feed(part):
        part = part.reshape(GROUP, 16, 16, FF_PAD)[..., :FF_ROWS]
        return part.transpose(1, 2, 0, 3).reshape(16, 16 * GROUP * FF_ROWS).astype(F32)

    keyed = att_rows[:, :, COLS:QKV].astype(F32).reshape(KV_HEADS, 2, 16, KV_COLS).sum(axis=1)
    keyed = keyed.transpose(1, 0, 2)
    own_norms = lax.dynamic_slice(norm_sums, (0, member * 16), (2, 16))
    return (
        mixed_out,
        grad_tokens,
        own_norms[0],
        even(att_rows[:, :, :COLS]),
        keyed[:, :, :HEAD].reshape(16, KV_HEADS * HEAD),
        keyed[:, :, HEAD:].reshape(16, KV_HEADS * HEAD),
        even(att_rows[:, :, QKV:]),
        own_norms[1],
        feed(gate_rows),
        feed(up_rows),
        down_sum[:FF_ROWS],
    )


def solution(mesh):
    matrix, vector = P("dp", None), P("dp")
    return jax.shard_map(
        on_device,
        mesh=mesh,
        in_specs=(
            matrix,
            matrix,
            vector,
            matrix,
            matrix,
            matrix,
            matrix,
            vector,
            matrix,
            matrix,
            matrix,
            matrix,
        ),
        out_specs=(
            matrix,
            matrix,
            vector,
            matrix,
            matrix,
            matrix,
            matrix,
            vector,
            matrix,
            matrix,
            matrix,
        ),
        check_vma=False,
    )
```

```python
import functools
import math

import jax
import jax.numpy as jnp
from jax import lax
from jax.experimental import pallas as pl
from jax.experimental.pallas import tpu as pltpu
from jax.sharding import PartitionSpec as P


HEADS = 32
KV_HEADS = 4
HEAD = 64
EPSILON = 1e-05
THETA = 10000.0
SCALE = 0.125
MASKED = -1e30

GROUP = 8
TOK = 128
TOKENS = GROUP * TOK
D = 2048
MY_HEADS = HEADS // GROUP
COLS = D // GROUP
FF_ROWS = 44
FF_PAD = 48
FF_COLS = 16 * FF_PAD
KV_COLS = 2 * HEAD
QKV = COLS + KV_COLS
ATT = QKV + COLS
PACK = ATT + 2 * FF_COLS

MESH = pl.DeviceIdType.MESH
BF16 = jnp.bfloat16
F32 = jnp.float32
ANY = pl.BlockSpec(memory_space=pl.ANY)
VMEM = pl.BlockSpec(memory_space=pltpu.VMEM)


def place():
    me = lax.axis_index("dp")
    return me // 32, (me // 8) % 4, (me // 2) % 4, me % 2


def index(z, y, x, c):
    return ((z * 4 + y) * 4 + x) * 2 + c


def shifted(here, axis, step):
    spot = list(here)
    spot[axis] = (spot[axis] + step) % 4
    return index(*spot)


def group_peers(here):
    z, y, x, c = here
    return [
        ((x + dx) % 4 * 2 + (c + dc) % 2, index(z, y, (x + dx) % 4, (c + dc) % 2))
        for dx in (2, 1, 3, 0)
        for dc in (0, 1)
        if (dx, dc) != (0, 0)
    ]


GROUP_LINKS = [[(2, 1), (2, -1)]] * 2 + [[(2, 1)]] * 2 + [[(2, -1)]] * 2 + [["core"]]


def plane_peers(here):
    z, y, x, c = here
    return [
        (((z + dz) % 4, (y + dy) % 4), index((z + dz) % 4, (y + dy) % 4, x, c))
        for dz in range(4)
        for dy in range(4)
        if (dz, dy) != (0, 0)
    ]


def greet(partners):
    barrier = pltpu.get_barrier_semaphore()
    for partner in partners:
        pl.semaphore_signal(barrier, inc=1, device_id=(partner,), device_id_type=MESH)
    pl.semaphore_wait(barrier, len(partners))


HOP = 3.0
RATE = 40000.0
CORE_RATE = 450000.0
SLACK = 0.0


class Net:
    def __init__(self, send_sem, recv_sem, local_sem):
        self.sems = (send_sem, recv_sem, local_sem)
        self.sent, self.moved = 0, 0
        self.open = []
        self.now = 0.0
        self.free = {}
        self.due = {}
        self.tasks = []
        self.late = []

    def start(self, program, rank=0, slack=0.0):
        task = Task(program, rank, slack)
        self.tasks.append(task)
        self.tasks.sort(key=lambda t: t.rank)
        return task

    def queue(self, copy, ref, links):
        size = math.prod(ref.shape) * jnp.dtype(ref.dtype).itemsize
        done = self.now
        for link in links:
            rate = CORE_RATE if link == "core" else RATE
            self.free[link] = max(self.free.get(link, 0.0), self.now) + size / rate
            done = max(done, self.free[link])
        self.due[id(copy)] = done + HOP
        self.open.append(copy)

    def send(self, src, dst, device, *links):
        copy = pltpu.make_async_remote_copy(
            src_ref=src,
            dst_ref=dst,
            send_sem=self.sems[0].at[self.sent],
            recv_sem=self.sems[1].at[self.sent],
            device_id=(device,),
            device_id_type=MESH,
        )
        copy.start()
        self.sent += 1
        self.queue(copy, src, links)
        return copy

    def move(self, src, dst):
        copy = pltpu.make_async_copy(src, dst, self.sems[2].at[self.moved])
        copy.start()
        self.moved += 1
        self.due[id(copy)] = self.now + 1.0
        return copy

    def spend(self, time):
        self.now += time

    def ready(self, needs):
        times = [0.0]
        for need in needs:
            if isinstance(need, Task):
                times.append(0.0 if need.done else math.inf)
            else:
                times.append(self.due[id(need)])
        return max(times)

    def leave(self, src, dst):
        self.late.append(self.move(src, dst))

    def finish(self):
        for copy in self.open:
            copy.wait_send()
        for copy in self.late:
            copy.wait()


class Task:
    def __init__(self, program, rank, slack):
        self.program, self.rank, self.slack, self.needs, self.done = program, rank, slack, [], False


def run(net, *programs):
    for program in programs:
        net.start(program)
    while net.tasks:
        times = [net.ready(task.needs) + (task.slack if task.needs else 0.0) for task in net.tasks]
        at = next((i for i, time in enumerate(times) if time <= net.now), times.index(min(times)))
        net.now = max(net.now, times[at])
        task = net.tasks[at]
        needs = next(task.program, None)
        if needs is None:
            task.done = True
            net.tasks.remove(task)
        else:
            task.needs = needs


def ring_gather(net, here, axis, at, own=None):
    spot = here[axis]
    before, after = (spot + 3) % 4, (spot + 1) % 4
    up, down = shifted(here, axis, 1), shifted(here, axis, -1)
    source = (lambda part: at(spot, part)) if own is None else own
    one = net.send(source(0), at(spot, 0), up, (axis, 1))
    two = net.send(source(1), at(spot, 1), down, (axis, -1))
    three = net.send(source(1), at(spot, 1), up, (axis, 1))
    four = net.send(source(0), at(spot, 0), down, (axis, -1))
    kept = [] if own is None else [net.move(own(None), at(spot, None))]
    yield [one]
    one.wait_recv()
    five = net.send(at(before, 0), at(before, 0), up, (axis, 1))
    yield [two]
    two.wait_recv()
    six = net.send(at(after, 1), at(after, 1), down, (axis, -1))
    yield [three, four, five, six, *kept]
    for copy in (three, four, five, six):
        copy.wait_recv()
    for copy in kept:
        copy.wait()


def plane_gather(net, here, region, half, own, then=None):
    z, y = here[0], here[1]
    mine = functools.partial(own, half)
    if half == 0:
        yield from ring_gather(net, here, 1, lambda p, s: region(z, p, 0, s), mine)
        second = ring_gather(net, here, 0, lambda p, s: region(p, None, 0, s))
    else:
        yield from ring_gather(net, here, 0, lambda p, s: region(p, y, 1, s), mine)
        second = ring_gather(net, here, 1, lambda p, s: region(None, p, 1, s))
    needs = next(second)
    if then is not None:
        then()
    yield needs
    yield from second


def plane_gather_direct(net, here, region, half, own):
    z, y = here[0], here[1]
    axes = (1, 0) if half == 0 else (0, 1)
    line = region(z, None, 0, None) if half == 0 else region(None, y, 1, None)
    source = own(half, None)
    kept = net.move(source, region(z, y, half, None))
    target = region(z, y, half, None)
    for axis in axes:
        copies = [
            net.send(source, target, shifted(here, axis, 2), (axis, 1), (axis, -1)),
            net.send(source, target, shifted(here, axis, 1), (axis, 1)),
            net.send(source, target, shifted(here, axis, -1), (axis, -1)),
        ]
        yield [*copies, kept]
        for copy in copies:
            copy.wait_recv()
        if axis == axes[0]:
            kept.wait()
        source = target = line


def half_rows(ref, cols):
    def own(half, part):
        size = TOK // 2 if part is None else TOK // 4
        return ref.at[pl.ds(half * (TOK // 2) + (part or 0) * (TOK // 4), size), cols]

    return own


def half_cols(ref, width):
    def own(half, part):
        size = width // 2 if part is None else width // 4
        return ref.at[:, pl.ds(half * (width // 2) + (part or 0) * (width // 4), size)]

    return own


def group_gather(net, here, own, at):
    z, y, x, c = here
    right, left = shifted(here, 2, 1), shifted(here, 2, -1)
    peer = index(z, y, x, 1 - c)
    before, after, far = (x + 3) % 4 * 2 + c, (x + 1) % 4 * 2 + c, (x + 2) % 4 * 2 + c
    mine = x * 2 + c
    one = net.send(own(0), at(mine, 0), right, (2, 1))
    two = net.send(own(1), at(mine, 1), left, (2, -1))
    three = net.send(own(1), at(mine, 1), right, (2, 1))
    four = net.send(own(0), at(mine, 0), left, (2, -1))
    across = [net.send(own(None), at(mine, None), peer, "core")]
    kept = net.move(own(None), at(mine, None))
    yield [one]
    one.wait_recv()
    five = net.send(at(before, 0), at(before, 0), right, (2, 1))
    yield [two]
    two.wait_recv()
    six = net.send(at(after, 1), at(after, 1), left, (2, -1))
    yield [three]
    three.wait_recv()
    across.append(net.send(at(before, None), at(before, None), peer, "core"))
    yield [four]
    four.wait_recv()
    across.append(net.send(at(after, None), at(after, None), peer, "core"))
    yield [five]
    five.wait_recv()
    across.append(net.send(at(far, 0), at(far, 0), peer, "core"))
    yield [six]
    six.wait_recv()
    across.append(net.send(at(far, 1), at(far, 1), peer, "core"))
    yield [*across, kept]
    for copy in across:
        copy.wait_recv()
    kept.wait()


def group_exchange(net, here, src, dst):
    mine = here[2] * 2 + here[3]
    copies = [
        net.send(src(g), dst(mine), device, *links)
        for (g, device), links in zip(group_peers(here), GROUP_LINKS, strict=True)
    ]
    kept = net.move(src(mine), dst(mine))
    yield [*copies, kept]
    for copy in copies:
        copy.wait_recv()
    kept.wait()


def strips(rows, work, step=16, together=1):
    def body(i, carry):
        for j in range(together):
            work(pl.ds(pl.multiple_of((i * together + j) * step, step), step))
        return carry

    lax.fori_loop(0, rows // step // together, body, 0)


def add_into(total, term):
    if len(total.shape) == 3:
        for i in range(total.shape[0]):
            add_into(total.at[i], term.at[i])
        return

    def work(rows):
        total[rows] = (total[rows].astype(F32) + term[rows].astype(F32)).astype(total.dtype)

    strips(total.shape[0], work)


def add_up(out, *terms):
    if len(out.shape) == 3:
        for i in range(out.shape[0]):
            add_up(out.at[i], *[term.at[i] for term in terms])
        return

    def work(rows):
        total = terms[0][rows].astype(F32)
        for term in terms[1:]:
            total = total + term[rows].astype(F32)
        out[rows] = total.astype(out.dtype)

    strips(out.shape[0], work)


def group_reduce_scratch(rows, cols):
    return [
        pltpu.VMEM((4, rows, cols), BF16),
        pltpu.VMEM((2, rows // 2, cols), BF16),
        pltpu.VMEM((2, rows, cols), BF16),
    ]


class GroupReduce:
    ORDER = (2, 1, 3, 0)

    def __init__(self, net, here, src, out, scratch, extra=()):
        self.net, self.here, self.src, self.out, self.extra = net, here, src, out, extra
        self.crossed, self.relay, self.landed = scratch
        self.cross_copies = []

    def cross(self, slot):
        z, y, x, c = self.here
        there = (x + self.ORDER[slot]) % 4
        self.cross_copies.append(
            self.net.send(
                self.src(there * 2 + 1 - c), self.crossed.at[slot], index(z, y, x, 1 - c), "core"
            )
        )

    def steps(self):
        z, y, x, c = self.here
        net, cross = self.net, self.cross_copies
        crossed, relay, landed = self.crossed, self.relay, self.landed
        right, left = shifted(self.here, 2, 1), shifted(self.here, 2, -1)
        held = [self.src((x + step) % 4 * 2 + c) for step in self.ORDER]
        part = [
            [self.src((x + step) % 4 * 2 + c, half) for half in (0, 1)] for step in self.ORDER
        ]
        half = relay.shape[1]
        upper, lower = pl.ds(0, half), pl.ds(half, half)
        yield [cross[0]]
        cross[0].wait_recv()
        add_into(held[0], crossed.at[0])
        net.spend(1.0)
        one = net.send(part[0][0], relay.at[0], right, (2, 1))
        two = net.send(part[0][1], relay.at[1], left, (2, -1))
        yield [cross[1]]
        cross[1].wait_recv()
        add_into(held[1], crossed.at[1])
        net.spend(1.0)
        three = net.send(part[1][1], landed.at[0, lower], right, (2, 1))
        yield [cross[2]]
        cross[2].wait_recv()
        add_into(held[2], crossed.at[2])
        net.spend(1.0)
        four = net.send(part[2][0], landed.at[1, upper], left, (2, -1))
        yield [one]
        one.wait_recv()
        add_into(part[1][0], relay.at[0])
        net.spend(0.5)
        five = net.send(part[1][0], landed.at[0, upper], right, (2, 1))
        yield [two]
        two.wait_recv()
        add_into(part[2][1], relay.at[1])
        net.spend(0.5)
        six = net.send(part[2][1], landed.at[1, lower], left, (2, -1))
        yield [cross[3]]
        cross[3].wait_recv()
        add_into(held[3], crossed.at[3])
        net.spend(1.0)
        yield [three, four, five, six]
        for copy in (three, four, five, six):
            copy.wait_recv()
        add_up(self.out, held[3], landed.at[0], landed.at[1], *self.extra)
        net.spend(1.0)


def plane_reduce_scratch(rows, cols):
    return [
        pltpu.VMEM((2, 4, rows, cols), BF16),
        pltpu.VMEM((2, 4, rows, cols), BF16),
        pltpu.VMEM((2, 2, 4, rows, cols), BF16),
        pltpu.VMEM((2, 4, rows, cols), BF16),
        pltpu.VMEM((2, rows, cols), BF16),
        pltpu.VMEM((2, 2, rows, cols), BF16),
    ]


def plane_reduce(net, here, region, half, out, scratch):
    relay, passing, landed, total, relay_two, landed_two = scratch
    axis, other = (0, 1) if half == 0 else (1, 0)

    def at(position, part):
        return region(position, None, half, part) if half == 0 else region(None, position, half, part)

    spot = here[axis]
    up, down = shifted(here, axis, 1), shifted(here, axis, -1)
    after, before, far = (spot + 1) % 4, (spot + 3) % 4, (spot + 2) % 4
    one = net.send(at(far, 0), relay.at[0], up, (axis, 1))
    two = net.send(at(far, 1), relay.at[1], down, (axis, -1))
    three = net.send(at(after, 1), landed.at[0, 1], up, (axis, 1))
    four = net.send(at(before, 0), landed.at[1, 0], down, (axis, -1))
    moves = [
        net.move(at(after, 0), passing.at[0]),
        net.move(at(before, 1), passing.at[1]),
        net.move(at(spot, 0), total.at[0]),
        net.move(at(spot, 1), total.at[1]),
    ]
    cost = math.prod(relay.shape[1:]) / 250000
    yield [one, moves[0]]
    one.wait_recv()
    moves[0].wait()
    add_into(passing.at[0], relay.at[0])
    net.spend(cost)
    five = net.send(passing.at[0], landed.at[0, 0], up, (axis, 1))
    yield [two, moves[1]]
    two.wait_recv()
    moves[1].wait()
    add_into(passing.at[1], relay.at[1])
    net.spend(cost)
    six = net.send(passing.at[1], landed.at[1, 1], down, (axis, -1))
    yield [four, five, moves[2]]
    moves[2].wait()
    four.wait_recv()
    five.wait_recv()
    add_up(total.at[0], total.at[0], landed.at[0, 0], landed.at[1, 0])
    net.spend(cost)
    spot = here[other]
    up, down = shifted(here, other, 1), shifted(here, other, -1)
    after, before, far = (spot + 1) % 4, (spot + 3) % 4, (spot + 2) % 4
    seven = net.send(total.at[0, far], relay_two.at[0], up, (other, 1))
    eight = net.send(total.at[0, before], landed_two.at[1, 0], down, (other, -1))
    yield [three, six, moves[3]]
    moves[3].wait()
    three.wait_recv()
    six.wait_recv()
    add_up(total.at[1], total.at[1], landed.at[0, 1], landed.at[1, 1])
    net.spend(cost)
    nine = net.send(total.at[1, far], relay_two.at[1], down, (other, -1))
    ten = net.send(total.at[1, after], landed_two.at[0, 1], up, (other, 1))
    yield [seven]
    seven.wait_recv()
    add_into(total.at[0, after], relay_two.at[0])
    net.spend(cost / 4)
    eleven = net.send(total.at[0, after], landed_two.at[0, 0], up, (other, 1))
    yield [nine]
    nine.wait_recv()
    add_into(total.at[1, before], relay_two.at[1])
    net.spend(cost / 4)
    twelve = net.send(total.at[1, before], landed_two.at[1, 1], down, (other, -1))
    yield [eight, eleven]
    eight.wait_recv()
    eleven.wait_recv()
    add_up(out(0), total.at[0, spot], landed_two.at[0, 0], landed_two.at[1, 0])
    net.spend(cost / 4)
    yield [ten, twelve]
    ten.wait_recv()
    twelve.wait_recv()
    add_up(out(1), total.at[1, spot], landed_two.at[0, 1], landed_two.at[1, 1])
    net.spend(cost / 4)


def by_rows(ref, rows, cols):
    def region(z, y, half, part):
        size = rows // 2 if part is None else rows // 4
        start = half * (rows // 2) + (0 if part is None else part * (rows // 4))
        return ref.at[
            slice(None) if z is None else z, slice(None) if y is None else y, pl.ds(start, size), cols
        ]

    return region


def by_cols(ref, cols):
    def region(z, y, half, part):
        size = cols // 2 if part is None else cols // 4
        start = half * (cols // 2) + (0 if part is None else part * (cols // 4))
        return ref.at[
            slice(None) if z is None else z, slice(None) if y is None else y, :, pl.ds(start, size)
        ]

    return region


def row_block(ref, rows):
    def at(g, part=None):
        size = rows if part is None else rows // 2
        start = g * rows + (0 if part is None else part * (rows // 2))
        return ref.at[pl.ds(pl.multiple_of(start, rows // 2), size)]

    return at


def col_block(ref, rows, cols, first=0):
    def at(g, part=None):
        size = rows if part is None else rows // 2
        start = first + (0 if part is None else part * (rows // 2))
        return ref.at[pl.ds(start, size), pl.ds(pl.multiple_of(g * cols, cols), cols)]

    return at


def halves(ref, rows, first=0):
    def own(part):
        size = rows if part is None else rows // 2
        return ref.at[pl.ds(first + (0 if part is None else part * (rows // 2)), size)]

    return own


def ring_partners(here, axes):
    return [shifted(here, axis, step) for axis in axes for step in (1, -1)]


def core_peer(here):
    return index(here[0], here[1], here[2], 1 - here[3])


def communicate(kernel, collective_id, outs, scratch, n_sends, n_moves, name, inside=()):
    def call(*args):
        def body(*refs):
            n_in, n_out = len(args), len(outs)
            send_sem, recv_sem, local_sem = refs[-3:]
            net = Net(send_sem, recv_sem, local_sem)
            kernel(net, place(), refs[:n_in], refs[n_in : n_in + n_out], refs[n_in + n_out : -3])
            net.finish()

        return pl.pallas_call(
            body,
            out_shape=[jax.ShapeDtypeStruct(shape, dtype) for shape, dtype, _ in outs],
            in_specs=[VMEM if i in inside else ANY for i in range(len(args))],
            out_specs=[VMEM if near else ANY for _, _, near in outs],
            scratch_shapes=list(scratch)
            + [
                pltpu.SemaphoreType.DMA((n_sends,)),
                pltpu.SemaphoreType.DMA((n_sends,)),
                pltpu.SemaphoreType.DMA((max(n_moves, 1),)),
            ],
            compiler_params=pltpu.CompilerParams(
                collective_id=collective_id, has_side_effects=True, vmem_limit_bytes=60 << 20
            ),
            name=name,
        )(*args)

    return call


def chunk(i, size):
    return pl.ds(pl.multiple_of(i * size, size), size)


def loop(count, work):
    def body(i, carry):
        work(i)
        return carry

    lax.fori_loop(0, count, body, 0)


def lanes(shape):
    return lax.broadcasted_iota(jnp.int32, shape, 1)


def tables(aux):
    lane = lanes(aux.shape)
    by = [aux] + [pltpu.roll(aux, 32 * k, 1) for k in (1, 2, 3)]
    cosine = jnp.where(lane < 32, by[0], jnp.where(lane < 64, by[1], jnp.where(lane < 96, by[2], by[3])))
    sine = jnp.where(lane < 32, by[3], jnp.where(lane < 64, by[0], jnp.where(lane < 96, by[1], by[2])))
    sine = jnp.where(lane % 64 < 32, -sine, sine)
    begin = jnp.where(lane < 64, by[2], by[0])
    return cosine, sine, begin


def turn(values, cosine, sine):
    width = values.shape[1]
    if width > 128:
        cosine, sine = (jnp.concatenate([t] * (width // 128), axis=1) for t in (cosine, sine))
    partner = jnp.where(
        lanes(values.shape) % 64 < 32,
        pltpu.roll(values, width - 32, 1),
        pltpu.roll(values, 32, 1),
    )
    return values * cosine + partner * sine


def allowed_keys(begin):
    key = lanes(begin.shape).astype(F32)
    query = lax.broadcasted_iota(jnp.int32, begin.shape, 0).astype(F32)
    return (key >= begin) & (key <= query)


def doubled(keyed):
    lane, other = lanes(keyed.shape), pltpu.roll(keyed, 64, 1)
    keys = jnp.where(lane < 64, keyed, other).astype(BF16)
    values = jnp.where(lane < 64, other, keyed).astype(BF16)
    return keys, values


def only_half(pair, side):
    lane = lanes(pair.shape)
    keep = lane < 64 if side == 0 else lane >= 64
    return jnp.where(keep, pair, jnp.zeros_like(pair))


def probabilities(query, keys, allowed):
    scores = jnp.where(allowed, dot_last(query, keys) * SCALE, MASKED)
    powers = jnp.exp(scores - jnp.max(scores, axis=-1, keepdims=True))
    return powers / jnp.sum(powers, axis=-1, keepdims=True)


def rows_of(ref):
    return lambda g: ref.at[pl.ds(pl.multiple_of(g * 16, 16), 16)]


def pack_keyed(w_key, w_value, out):
    for x in range(KV_HEADS):
        tile = pl.ds(x // 2 * 128, 128)
        key, value = w_key[:, tile].astype(F32), w_value[:, tile].astype(F32)
        if x % 2 == 0:
            value = pltpu.roll(value, 64, 1)
        else:
            key = pltpu.roll(key, 64, 1)
        out(x, jnp.where(lanes(key.shape) < 64, key, value).astype(BF16))


def pack_feed(w, out, whole, part):
    whole[...] = w[...].astype(F32)
    part[...] = jnp.zeros_like(part)
    for g in range(GROUP):
        for spot in range(16):
            start = (spot * GROUP + g) * FF_ROWS
            part[:, spot * FF_PAD : spot * FF_PAD + FF_ROWS] = whole[:, start : start + FF_ROWS]
        out(g, part[...].astype(BF16))


def forward(net, here, inputs, outputs, scratch):
    tokens, aux, meta, w_query, w_key, w_value, w_out, w_gate, w_up = inputs
    qkv_w_out, out_w_out, gate_out, up_out, normed_out, qkv_out, attended_out, residual_out = outputs[:8]
    all_aux, all_meta = outputs[8:]
    (
        all_tokens,
        normed,
        packed_one,
        packed_two,
        own_one,
        own_two,
        qkv_w,
        out_w,
        gate,
        up,
        linear,
        qkv,
        mine_attended,
        attended,
        mine_residual,
        residual,
        seen,
        mine_meta,
        gain,
        whole,
        part,
    ) = scratch
    z, y, x, c = here
    mine = x * 2 + c
    greet([device for _, device in group_peers(here)] + [device for _, device in plane_peers(here)])

    def small():
        copies = [net.send(meta, seen.at[mine], device) for _, device in group_peers(here)]
        kept = net.move(meta, seen.at[mine])
        yield [*copies, kept]
        for copy in copies:
            copy.wait_recv()
        kept.wait()
        mine_meta[...] = jnp.sum(seen[...], axis=0)
        spots = all_meta.at[z * 4 + y]
        copies = [net.send(mine_meta, spots, device) for _, device in plane_peers(here)]
        all_meta[z * 4 + y] = mine_meta[...]
        net.spend(1.0)
        yield copies
        for copy in copies:
            copy.wait_recv()
        for spot in range(16):
            gain[:, pl.ds(spot * 128, 128)] = all_meta[spot, 0:1, :]

    parts = [
        (by_rows(out_w, TOK, slice(None)), half_rows(own_two, pl.ds(0, COLS))),
        (by_rows(gate, TOK, slice(None)), half_rows(own_two, pl.ds(COLS, FF_COLS))),
        (by_rows(up, TOK, slice(None)), half_rows(own_two, pl.ds(COLS + FF_COLS, FF_COLS))),
    ]
    tasks = {}

    def gather_part(i):
        region, source = parts[i]
        for half in (0, 1):
            follow = functools.partial(gather_part, i + 1) if half == 1 and i + 1 < len(parts) else None
            tasks[i, half] = net.start(plane_gather(net, here, region, half, source, follow), slack=SLACK)

    def exchange_one():
        def put(x, value):
            packed_one[2 * x, :, COLS:] = value
            packed_one[2 * x + 1, :, COLS:] = value

        pack_keyed(w_key, w_value, put)
        for g in range(GROUP):
            packed_one[g, :, :COLS] = w_query[:, g * COLS : (g + 1) * COLS]
        yield from group_exchange(net, here, lambda g: packed_one.at[g], rows_of(own_one))
        region, source = by_rows(qkv_w, TOK, slice(None)), half_rows(own_one, slice(None))
        for half in (0, 1):
            tasks["qkv", half] = net.start(plane_gather_direct(net, here, region, half, source))

    def exchange_two():
        for g in range(GROUP):
            packed_two[g, :, :COLS] = w_out[:, g * COLS : (g + 1) * COLS]

        def put(start):
            def store(g, value):
                packed_two[g, :, start : start + FF_COLS] = value

            return store

        pack_feed(w_gate, put(COLS), whole, part)
        pack_feed(w_up, put(COLS + FF_COLS), whole, part)
        net.spend(3.0)
        yield [exchanged]
        yield from group_exchange(net, here, lambda g: packed_two.at[g], rows_of(own_two))
        gather_part(0)

    def attend(i):
        rows = chunk(i, TOK)
        cosine, sine, begin = tables(all_aux[rows])
        allowed = allowed_keys(begin)
        turned = turn(linear[rows, :COLS], cosine, sine).astype(BF16)
        keyed = linear[rows, COLS:]
        keyed = jnp.where(lanes(keyed.shape) < 64, turn(keyed, cosine, sine), keyed)
        keys, values = doubled(keyed)
        qkv[rows, :COLS] = turned
        qkv[rows, COLS:] = keyed.astype(BF16)
        for pair in range(MY_HEADS // 2):
            both = turned[:, pair * 128 : pair * 128 + 128]
            sides = []
            for side in (0, 1):
                probs = probabilities(only_half(both, side), keys, allowed)
                sides.append(matmul(probs.astype(BF16), values))
            out = jnp.where(lanes(sides[0].shape) < 64, sides[0], sides[1])
            mine_attended[rows, pair * 128 : pair * 128 + 128] = out.astype(BF16)

    def normalise(strip):
        values = all_tokens[strip].astype(F32)
        scale = lax.rsqrt(jnp.mean(values * values, axis=-1, keepdims=True) + EPSILON)
        normed[strip] = (values * scale * gain[...]).astype(BF16)

    pieces = 4
    size = TOKENS // pieces

    def work():
        yield [gains, took]
        strips(TOKENS, normalise, together=4)
        net.spend(3.0)
        net.leave(normed, normed_out)
        yield [exchanged, placed]
        yield [tasks["qkv", 0], tasks["qkv", 1]]
        net.leave(qkv_w, qkv_w_out)
        sent = []
        for i in range(pieces):
            rows = pl.ds(i * size, size)
            linear[rows] = matmul(normed[rows], qkv_w[...].reshape(D, QKV))
            loop(size // TOK, lambda j, i=i: attend(j + i * (size // TOK)))
            net.spend(2.5)
            at = col_block(attended, size, COLS, i * size)
            sent.append(net.start(group_gather(net, here, halves(mine_attended, size, i * size), at)))
            yield []
        net.leave(qkv, qkv_out)
        my_cols = pl.ds(pl.multiple_of(mine * COLS, COLS), COLS)
        yield [other]
        yield [tasks[0, 0], tasks[0, 1]]
        net.leave(out_w, out_w_out)
        last = []
        for i in range(pieces):
            yield [sent[i]]
            rows = pl.ds(i * size, size)
            out = matmul(attended[rows], out_w[...].reshape(D, COLS))
            mine_residual[rows] = (all_tokens[rows, my_cols].astype(F32) + out).astype(BF16)
            net.spend(0.6)
            at = col_block(residual, size, COLS, i * size)
            last.append(net.start(group_gather(net, here, halves(mine_residual, size, i * size), at)))
            yield []
        net.leave(attended, attended_out)
        for i, (ref, out) in enumerate(((gate, gate_out), (up, up_out))):
            while (i + 1, 1) not in tasks:
                yield [tasks[i, 1]]
            yield [tasks[i + 1, 0], tasks[i + 1, 1]]
            net.leave(ref, out)
        yield last
        net.leave(residual, residual_out)

    exchanged = net.start(exchange_one())
    gains = net.start(small())
    took = net.start(group_gather(net, here, halves(tokens, TOK), row_block(all_tokens, TOK)))
    placed = net.start(group_gather(net, here, halves(aux, TOK), row_block(all_aux, TOK)))
    other = net.start(exchange_two())
    net.start(work(), rank=1)
    run(net)


def forward_call(*args):
    outs = [
        ((4, 4, TOK, QKV), BF16, False),
        ((4, 4, TOK, COLS), BF16, False),
        ((4, 4, TOK, FF_COLS), BF16, False),
        ((4, 4, TOK, FF_COLS), BF16, False),
        ((TOKENS, D), BF16, False),
        ((TOKENS, QKV), BF16, False),
        ((TOKENS, D), BF16, False),
        ((TOKENS, D), BF16, False),
        ((TOKENS, 128), F32, True),
        ((16, 8, 128), F32, True),
    ]
    scratch = [
        pltpu.VMEM((TOKENS, D), BF16),
        pltpu.VMEM((TOKENS, D), BF16),
        pltpu.VMEM((GROUP, 16, QKV), BF16),
        pltpu.VMEM((GROUP, 16, COLS + 2 * FF_COLS), BF16),
        pltpu.VMEM((TOK, QKV), BF16),
        pltpu.VMEM((TOK, COLS + 2 * FF_COLS), BF16),
        pltpu.VMEM((4, 4, TOK, QKV), BF16),
        pltpu.VMEM((4, 4, TOK, COLS), BF16),
        pltpu.VMEM((4, 4, TOK, FF_COLS), BF16),
        pltpu.VMEM((4, 4, TOK, FF_COLS), BF16),
        pltpu.VMEM((TOKENS, QKV), F32),
        pltpu.VMEM((TOKENS, QKV), BF16),
        pltpu.VMEM((TOKENS, COLS), BF16),
        pltpu.VMEM((TOKENS, D), BF16),
        pltpu.VMEM((TOKENS, COLS), BF16),
        pltpu.VMEM((TOKENS, D), BF16),
        pltpu.VMEM((8, 8, 128), F32),
        pltpu.VMEM((8, 128), F32),
        pltpu.VMEM((1, D), F32),
        pltpu.VMEM((16, 16 * GROUP * FF_ROWS), F32),
        pltpu.VMEM((16, FF_COLS), F32),
    ]
    return communicate(forward, 0, outs, scratch, 300, 60, "forward", inside=range(3, 9))(*args)


def feed_forward(net, here, inputs, outputs, scratch):
    residual, gate_w, up_w, w_down, upstream, gain = inputs
    grad_out, mixed_out, down_out, grad_gate, grad_up = outputs
    (
        normed,
        weight,
        narrow,
        all_upstream,
        gate,
        up,
        active,
        grad_gate_lin,
        grad_up_lin,
        mixed_part,
        grad_part,
        grad_down,
        stage,
    ) = scratch[:13]
    own_residual, own_down = scratch[-2:]
    own_down[: FF_ROWS // 16 * 16] = w_down[: FF_ROWS // 16 * 16]
    tail = w_down[FF_ROWS // 16 * 16 :].astype(F32)
    tail = jnp.concatenate([tail, jnp.zeros((FF_PAD - FF_ROWS, D), F32)], axis=0)
    own_down[FF_ROWS // 16 * 16 :] = tail.astype(BF16)
    x = here[2]
    member = x * 2 + here[3]
    loads = [
        net.move(residual, grad_part),
        net.move(gate_w, weight.at[0]),
        net.move(up_w, weight.at[1]),
        net.move(row_block(residual, TOK)(member), own_residual),
    ]
    greet(ring_partners(here, (0, 1, 2)) + [core_peer(here)])
    rows = TOKENS // 4
    gather = net.start(group_gather(net, here, halves(upstream, TOK), row_block(all_upstream, TOK)))
    down_tasks = [
        net.start(plane_gather(net, here, by_cols(narrow, D), half, half_cols(own_down, D)), slack=SLACK)
        for half in (0, 1)
    ]

    def normalise(strip):
        values = grad_part[strip].astype(F32)
        scale = lax.rsqrt(jnp.mean(values * values, axis=-1, keepdims=True) + EPSILON)
        normed[strip] = (values * scale * gain[...]).astype(BF16)

    def expand(i):
        here_rows = chunk(i, rows)
        for j in range(FF_COLS // 256):
            cols = pl.ds(j * 256, 256)
            gate_val = matmul(normed[here_rows], weight[0, :, cols])
            up_val = matmul(normed[here_rows], weight[1, :, cols])
            sigmoid_gate = 1.0 / (1.0 + jnp.exp(-gate_val))
            silu_gate = gate_val * sigmoid_gate
            active[here_rows, cols] = (silu_gate * up_val).astype(BF16)
            gate[here_rows, cols] = silu_gate.astype(BF16)
            up[here_rows, cols] = (
                up_val * sigmoid_gate * (1.0 + gate_val * (1.0 - sigmoid_gate))
            ).astype(BF16)

    def down(j):
        cols = chunk(j, 256)
        for p in range(2):
            part = dot_first(active[:, pl.ds(p * 384, 384)], all_upstream[:, cols])
            grad_down[2 * p : 2 * p + 2, :, :, cols] = part.astype(BF16).reshape(2, 4, FF_PAD, 256)

    def backward(i):
        here_rows = chunk(i, rows)
        for j in range(2):
            cols = pl.ds(j * 384, 384)
            down_rows = narrow[2 * j : 2 * j + 2].reshape(384, D)
            grad_active = dot_last(all_upstream[here_rows], down_rows)
            grad_up_lin[here_rows, cols] = (grad_active * gate[here_rows, cols].astype(F32)).astype(BF16)
            grad_gate_lin[here_rows, cols] = (grad_active * up[here_rows, cols].astype(F32)).astype(BF16)

    quarter = D // 4
    region = by_cols(grad_down, D)

    def narrow_part(half):
        return lambda part: down_out.at[:, pl.ds((half * 2 + part) * quarter, quarter)]

    mix = GroupReduce(net, here, row_block(mixed_part, TOK), mixed_out, scratch[13:16], [own_residual])
    back = GroupReduce(net, here, row_block(grad_part, TOK), grad_out, scratch[16:19])

    def work():
        loads[0].wait()
        strips(TOKENS, normalise, together=4)
        net.spend(3.0)
        loads[1].wait()
        loads[2].wait()
        loop(2, expand)
        net.spend(6.0)
        yield []
        loop(2, lambda i: expand(i + 2))
        net.spend(6.0)
        yield []
        loads[3].wait()
        yield [gather]
        loop(D // 256, down)
        net.spend(4.5)
        for half in (0, 1):
            room = scratch[19 + 6 * half : 25 + 6 * half]
            net.start(plane_reduce(net, here, region, half, narrow_part(half), room), slack=SLACK)
        yield []
        yield down_tasks
        for slot, step in enumerate(GroupReduce.ORDER):
            there = chunk((x + step) % 4, rows)

            def mixed(j):
                cols = chunk(j, 512)
                mixed_part[there, cols] = matmul(active[there], narrow[:, :, :, cols].reshape(FF_COLS, 512)).astype(BF16)

            loop(D // 512, mixed)
            net.spend(1.2)
            mix.cross(slot)
            yield []
        net.start(mix.steps())
        loop(2, backward)
        net.spend(3.0)
        yield []
        loop(2, lambda i: backward(i + 2))
        net.spend(3.0)
        yield []
        for slot, step in enumerate(GroupReduce.ORDER):
            there = chunk((x + step) % 4, rows)

            def to_input(j):
                cols = chunk(j, 512)
                total = dot_last(grad_gate_lin[there], weight[0, cols])
                total = total + dot_last(grad_up_lin[there], weight[1, cols])
                grad_part[there, cols] = total.astype(BF16)

            loop(D // 512, to_input)
            net.spend(2.3)
            back.cross(slot)
            yield []
        net.start(back.steps())
        yield []
        outs = [None, None]
        for m in range(D // 256):
            slot = m % 2
            if outs[slot] is not None:
                for copy in outs[slot]:
                    copy.wait()
            rows_of = normed[:, pl.ds(m * 256, 256)]
            stage[slot, 0] = dot_first(rows_of, grad_gate_lin[...]).astype(BF16)
            stage[slot, 1] = dot_first(rows_of, grad_up_lin[...]).astype(BF16)
            outs[slot] = [
                net.move(stage.at[slot, 0], grad_gate.at[pl.ds(m * 256, 256)]),
                net.move(stage.at[slot, 1], grad_up.at[pl.ds(m * 256, 256)]),
            ]
            net.spend(1.2)
            yield []
        for pair in outs:
            for copy in pair:
                copy.wait()

    net.start(work(), rank=1)
    run(net)


def feed_scratch():
    return (
        [
            pltpu.VMEM((TOKENS, D), BF16),
            pltpu.VMEM((2, D, FF_COLS), BF16),
            pltpu.VMEM((4, 4, FF_PAD, D), BF16),
            pltpu.VMEM((TOKENS, D), BF16),
        ]
        + [pltpu.VMEM((TOKENS, FF_COLS), BF16)] * 5
        + [
            pltpu.VMEM((TOKENS, D), BF16),
            pltpu.VMEM((TOKENS, D), BF16),
            pltpu.VMEM((4, 4, FF_PAD, D), BF16),
            pltpu.VMEM((2, 2, 256, FF_COLS), BF16),
        ]
        + group_reduce_scratch(TOK, D) * 2
        + plane_reduce_scratch(FF_PAD, D // 4) * 2
        + [pltpu.VMEM((TOK, D), BF16), pltpu.VMEM((FF_PAD, D), BF16)]
    )


def quarter_rows(ref):
    return lambda half: lambda part: ref.at[pl.ds((half * 2 + part) * (TOK // 4), TOK // 4)]


def backward(net, here, inputs, outputs, scratch):
    (
        grad_normed_two,
        all_residual,
        upstream,
        tokens,
        all_meta,
        all_aux,
        qkv_in,
        qkv_w_in,
        out_w_in,
        normed_in,
        attended_in,
        gate_in,
        up_in,
        w_query,
        w_key,
        w_value,
        w_gate,
        w_up,
    ) = inputs
    grad_tokens, norms_out, grad_query, grad_key, grad_value, grad_out, grad_gate_out, grad_up_out = outputs
    (
        grad_two,
        residual,
        own_upstream,
        own_tokens,
        grad_residual,
        grad_rounded,
        gains,
        grad_cols,
        qkv_w,
        out_w,
        heads_part,
        heads,
        qkv,
        grad_lin,
        normed,
        attended,
        input_part,
        grad_one,
        grad_gate,
        grad_up,
        grad_qkv_w,
        grad_out_w,
        gate_sum,
        up_sum,
        qkv_sum,
        out_sum,
        gate_rows,
        up_rows,
        qkv_rows,
        out_rows,
        part,
    ) = scratch[:31]
    rest = scratch[31:]
    z, y, x, c = here
    mine = x * 2 + c
    loads = {
        "grad_two": net.move(grad_normed_two, grad_two),
        "residual": net.move(row_block(all_residual, TOK)(mine), residual),
        "upstream": net.move(upstream, own_upstream),
        "gate": net.move(gate_in, grad_gate),
        "out_w": net.move(out_w_in, out_w),
        "qkv_w": net.move(qkv_w_in, qkv_w),
        "up": net.move(up_in, grad_up),
        "qkv": net.move(qkv_in, qkv),
        "attended": net.move(attended_in, attended),
        "normed": net.move(normed_in, normed),
        "tokens": net.move(tokens, own_tokens),
    }
    greet([device for _, device in group_peers(here)] + ring_partners(here, (0, 1)))

    def unpack_feed(rows, out, w, column):
        def finish():
            for g in range(GROUP):
                part[...] = rows[g].astype(F32)
                for spot in range(16):
                    start = (spot * GROUP + g) * FF_ROWS
                    out[:, start : start + FF_ROWS] = part[:, spot * FF_PAD : spot * FF_PAD + FF_ROWS]
            add_norm(column, [(out, w)])
            net.spend(2.0)

        return finish

    def add_norm(column, pairs):
        total = sum(
            jnp.sum(grad[...] * w[...].astype(F32), axis=-1, keepdims=True) for grad, w in pairs
        )
        norms_out[...] += jnp.where(lanes((16, 128)) == column, total, 0.0)

    def unpack_qkv():
        for g in range(GROUP):
            grad_query[:, g * COLS : (g + 1) * COLS] = qkv_rows[g, :, :COLS].astype(F32)
        keyed = [
            qkv_rows[2 * i, :, COLS:].astype(F32) + qkv_rows[2 * i + 1, :, COLS:].astype(F32)
            for i in range(KV_HEADS)
        ]
        lane = lanes(keyed[0].shape)
        for i in range(KV_HEADS // 2):
            first, second = keyed[2 * i], keyed[2 * i + 1]
            cols = pl.ds(i * 128, 128)
            grad_key[:, cols] = jnp.where(lane < 64, first, pltpu.roll(second, 64, 1))
            grad_value[:, cols] = jnp.where(lane < 64, pltpu.roll(first, 64, 1), second)
        add_norm(0, [(grad_query, w_query), (grad_key, w_key), (grad_value, w_value)])

    def unpack_out():
        for g in range(GROUP):
            grad_out[:, g * COLS : (g + 1) * COLS] = out_rows[g].astype(F32)

    def feed_gradients():
        for name, source, total, rows, room, out, w in (
            ("gate", grad_gate, gate_sum, gate_rows, rest[0:12], grad_gate_out, w_gate),
            ("up", grad_up, up_sum, up_rows, rest[12:24], grad_up_out, w_up),
        ):
            yield [loads[name]]
            loads[name].wait()
            yield [give_back(source, total, rows, room, unpack_feed(rows, out, w, 1))]

    def give_back(source, total, rows, room, unpack):
        region, part = by_rows(source, TOK, slice(None)), quarter_rows(total)
        tasks = [
            net.start(plane_reduce(net, here, region, half, part(half), room[6 * half : 6 * half + 6]), slack=SLACK)
            for half in (0, 1)
        ]

        def hand_out():
            yield tasks
            yield from group_exchange(net, here, rows_of(total), lambda g: rows.at[g])
            unpack()

        net.start(hand_out())
        return tasks[1]

    def residual_back(strip):
        values = residual[strip].astype(F32)
        scale = lax.rsqrt(jnp.mean(values * values, axis=-1, keepdims=True) + EPSILON)
        unit = values * scale
        grad = grad_two[strip]
        grad = grad * gains[1:2]
        grad = scale * (grad - unit * jnp.mean(grad * unit, axis=-1, keepdims=True))
        grad = own_upstream[strip].astype(F32) + grad
        grad_residual[strip] = grad
        grad_rounded[strip] = grad.astype(BF16)

    def input_back(strip):
        values = own_tokens[strip].astype(F32)
        scale = lax.rsqrt(jnp.mean(values * values, axis=-1, keepdims=True) + EPSILON)
        unit = values * scale
        grad = grad_one[strip]
        grad = grad * gains[0:1]
        grad = scale * (grad - unit * jnp.mean(grad * unit, axis=-1, keepdims=True))
        grad_tokens[strip] = grad_residual[strip] + grad

    def attend_back(i):
        rows = chunk(i, TOK)
        cosine, sine, begin = tables(all_aux[rows])
        allowed = allowed_keys(begin)
        keys, values = doubled(qkv[rows, COLS:].astype(F32))
        grad_queries = []
        grad_keys = jnp.zeros((TOK, 128), F32)
        grad_values = jnp.zeros((TOK, 128), F32)
        for pair in range(MY_HEADS // 2):
            cols = pl.ds(pair * 128, 128)
            queries, grads = qkv[rows, cols], heads[rows, cols]
            sides = []
            for side in (0, 1):
                query, grad = only_half(queries, side), only_half(grads, side)
                probs = probabilities(query, keys, allowed)
                grad_probs = dot_last(grad, values)
                grad_scores = probs * (grad_probs - jnp.sum(probs * grad_probs, axis=-1, keepdims=True))
                grad_scores = grad_scores.astype(BF16)
                sides.append(matmul(grad_scores, keys))
                grad_keys = grad_keys + dot_first(grad_scores, query)
                grad_values = grad_values + dot_first(probs.astype(BF16), grad)
            grad_queries.append(jnp.where(lanes(sides[0].shape) < 64, sides[0], sides[1]))
        grad_query = jnp.concatenate(grad_queries, axis=1) * SCALE
        grad_lin[rows, :COLS] = turn(grad_query, cosine, -sine).astype(BF16)
        grad_keys = turn((grad_keys + pltpu.roll(grad_keys, 64, 1)) * SCALE, cosine, -sine)
        grad_values = grad_values + pltpu.roll(grad_values, 64, 1)
        grad_lin[rows, COLS:] = jnp.where(lanes(grad_keys.shape) < 64, grad_keys, grad_values).astype(BF16)

    half_tokens = TOKENS // 2

    def work():
        for name in ("grad_two", "residual", "upstream"):
            loads[name].wait()
        for spot in range(16):
            gains[:, pl.ds(spot * 128, 128)] = all_meta[spot]
        norms_out[...] = jnp.zeros_like(norms_out)
        strips(TOK, residual_back, together=2)
        net.spend(2.0)
        spread = net.start(
            group_exchange(net, here, col_block(grad_rounded, TOK, COLS), row_block(grad_cols, TOK))
        )
        yield []
        loads["out_w"].wait()
        yield [spread]
        reduced = []
        for half in (0, 1):
            first = half * half_tokens
            rows = pl.ds(first, half_tokens)
            room = rest[36 + 3 * half : 39 + 3 * half]
            reduce = GroupReduce(
                net, here, col_block(heads_part, half_tokens, COLS, first), heads.at[rows], room
            )
            for slot, step in enumerate(GroupReduce.ORDER):
                cols = chunk((x + step) % 4, 2 * COLS)
                part = dot_last(grad_cols[rows], out_w[cols])
                heads_part[rows, cols] = part.astype(BF16)
                net.spend(0.6)
                reduce.cross(slot)
            reduced.append(net.start(reduce.steps()))
        yield []
        loads["attended"].wait()

        def out_gradient(m):
            part = dot_first(attended[:, chunk(m, 256)], grad_cols[...]).astype(BF16)
            grad_out_w[m // 2, pl.ds(m % 2 * 2, 2)] = part.reshape(2, TOK, COLS)

        for half in (0, 1):
            loop(4, lambda m, half=half: out_gradient(m + 4 * half))
            net.spend(2.3)
            yield []
        give_back(grad_out_w, out_sum, out_rows, rest[45:57], unpack_out)
        loads["qkv"].wait()
        loads["qkv_w"].wait()
        for half in (0, 1):
            yield [reduced[half]]
            loop(4, lambda i, half=half: attend_back(i + 4 * half))
            net.spend(6.0)
        reduce = GroupReduce(net, here, row_block(input_part, TOK), grad_one, rest[42:45])
        for slot, step in enumerate(GroupReduce.ORDER):
            there = chunk((x + step) % 4, 256)

            def to_input(j):
                cols = chunk(j, 512)
                part = dot_last(grad_lin[there], qkv_w[cols])
                input_part[there, cols] = part.astype(BF16)

            loop(D // 512, to_input)
            net.spend(1.3)
            reduce.cross(slot)
            yield []
        reduced = net.start(reduce.steps())
        loads["normed"].wait()

        def in_gradient(m):
            part = dot_first(normed[:, chunk(m, 256)], grad_lin[...]).astype(BF16)
            grad_qkv_w[m // 2, pl.ds(m % 2 * 2, 2)] = part.reshape(2, TOK, QKV)

        loop(8, in_gradient)
        net.spend(3.5)
        give_back(grad_qkv_w, qkv_sum, qkv_rows, rest[24:36], unpack_qkv)
        loads["tokens"].wait()
        yield [reduced]
        strips(TOK, input_back, together=2)
        net.spend(2.0)

    net.start(feed_gradients())
    net.start(work(), rank=1)
    run(net)


def backward_call(*args):
    outs = [
        ((TOK, D), F32, True),
        ((16, 128), F32, True),
        ((16, D), F32, True),
        ((16, KV_HEADS * HEAD), F32, True),
        ((16, KV_HEADS * HEAD), F32, True),
        ((16, D), F32, True),
        ((16, 16 * GROUP * FF_ROWS), F32, True),
        ((16, 16 * GROUP * FF_ROWS), F32, True),
    ]
    scratch = [
        pltpu.VMEM((TOK, D), F32),
        pltpu.VMEM((TOK, D), BF16),
        pltpu.VMEM((TOK, D), BF16),
        pltpu.VMEM((TOK, D), BF16),
        pltpu.VMEM((TOK, D), F32),
        pltpu.VMEM((TOK, D), BF16),
        pltpu.VMEM((8, D), F32),
        pltpu.VMEM((TOKENS, COLS), BF16),
        pltpu.VMEM((D, QKV), BF16),
        pltpu.VMEM((D, COLS), BF16),
        pltpu.VMEM((TOKENS, D), BF16),
        pltpu.VMEM((TOKENS, COLS), BF16),
        pltpu.VMEM((TOKENS, QKV), BF16),
        pltpu.VMEM((TOKENS, QKV), BF16),
        pltpu.VMEM((TOKENS, D), BF16),
        pltpu.VMEM((TOKENS, D), BF16),
        pltpu.VMEM((TOKENS, D), BF16),
        pltpu.VMEM((TOK, D), F32),
        pltpu.VMEM((4, 4, TOK, FF_COLS), BF16),
        pltpu.VMEM((4, 4, TOK, FF_COLS), BF16),
        pltpu.VMEM((4, 4, TOK, QKV), BF16),
        pltpu.VMEM((4, 4, TOK, COLS), BF16),
        pltpu.VMEM((TOK, FF_COLS), BF16),
        pltpu.VMEM((TOK, FF_COLS), BF16),
        pltpu.VMEM((TOK, QKV), BF16),
        pltpu.VMEM((TOK, COLS), BF16),
        pltpu.VMEM((GROUP, 16, FF_COLS), BF16),
        pltpu.VMEM((GROUP, 16, FF_COLS), BF16),
        pltpu.VMEM((GROUP, 16, QKV), BF16),
        pltpu.VMEM((GROUP, 16, COLS), BF16),
        pltpu.VMEM((16, FF_COLS), F32),
    ]
    scratch += plane_reduce_scratch(TOK // 4, FF_COLS) * 4 + plane_reduce_scratch(TOK // 4, QKV) * 2
    scratch += group_reduce_scratch(TOKENS // 2, COLS) * 2 + group_reduce_scratch(TOK, D)
    scratch += plane_reduce_scratch(TOK // 4, COLS) * 2
    return communicate(
        backward, 1, outs, scratch, 180, 60, "backward", inside=(4, 5, 13, 14, 15, 16, 17)
    )(*args)


def sequence_table(lengths):
    ends = jnp.cumsum(lengths)
    places = jnp.arange(TOK, dtype=jnp.int32)
    begins = jnp.max(jnp.where(places[:, None] >= ends[None, :], ends[None, :], 0), axis=-1)
    inverse = jnp.exp(jnp.arange(HEAD // 2, dtype=F32) * (-2.0 * math.log(THETA) / HEAD))
    angle = (places - begins).astype(F32)[:, None] * inverse[None, :]
    start = jnp.broadcast_to(begins.astype(F32)[:, None], (TOK, 64))
    return jnp.concatenate([jnp.cos(angle), jnp.sin(angle), start], axis=1)


def matmul(left, right):
    return jnp.dot(left, right, preferred_element_type=F32)


def dot_last(left, right):
    return lax.dot_general(left, right, (((1,), (1,)), ((), ())), preferred_element_type=F32)


def dot_first(left, right):
    return lax.dot_general(left, right, (((0,), (0,)), ((), ())), preferred_element_type=F32)


def on_device(
    tokens,
    seq_lengths,
    attn_norm,
    w_query,
    w_key,
    w_value,
    w_out,
    mlp_norm,
    w_gate,
    w_up,
    w_down,
    cotangent,
):
    me = lax.axis_index("dp")
    member = me % GROUP
    meta = jnp.stack([attn_norm.astype(F32), mlp_norm.astype(F32)])
    meta = lax.dynamic_update_slice(jnp.zeros((8, 128), F32), meta, (0, member * 16))
    (
        qkv_w,
        out_w,
        gate_w,
        up_w,
        normed,
        qkv,
        all_attended,
        all_residual,
        all_aux,
        all_meta,
    ) = forward_call(
        tokens, sequence_table(seq_lengths[0]), meta, w_query, w_key, w_value, w_out, w_gate, w_up
    )
    mlp_gain = all_meta[:, 1, :].reshape(1, D)

    grad_normed_two, mixed_out, down_sum, grad_gate, grad_up = communicate(
        feed_forward,
        3,
        [
            ((TOK, D), F32, True),
            ((TOK, D), BF16, True),
            ((FF_PAD, D), F32, True),
            ((D, FF_COLS), BF16, False),
            ((D, FF_COLS), BF16, False),
        ],
        feed_scratch(),
        80,
        40,
        "feed_forward",
        inside=(3, 5),
    )(
        all_residual,
        gate_w.reshape(D, FF_COLS),
        up_w.reshape(D, FF_COLS),
        w_down,
        cotangent,
        mlp_gain,
    )

    grad_tokens, norms, grad_query, grad_key, grad_value, grad_out, grad_gate, grad_up = backward_call(
        grad_normed_two,
        all_residual,
        cotangent,
        tokens,
        all_meta,
        all_aux,
        qkv,
        qkv_w.reshape(D, QKV),
        out_w.reshape(D, COLS),
        normed,
        all_attended,
        grad_gate.reshape(4, 4, TOK, FF_COLS),
        grad_up.reshape(4, 4, TOK, FF_COLS),
        w_query,
        w_key,
        w_value,
        w_gate,
        w_up,
    )
    return (
        mixed_out,
        grad_tokens,
        norms[:, 0] / attn_norm.astype(F32),
        grad_query,
        grad_key,
        grad_value,
        grad_out,
        norms[:, 1] / mlp_norm.astype(F32),
        grad_gate,
        grad_up,
        down_sum[:FF_ROWS],
    )


def solution(mesh):
    matrix, vector = P("dp", None), P("dp")
    return jax.shard_map(
        on_device,
        mesh=mesh,
        in_specs=(
            matrix,
            matrix,
            vector,
            matrix,
            matrix,
            matrix,
            matrix,
            vector,
            matrix,
            matrix,
            matrix,
            matrix,
        ),
        out_specs=(
            matrix,
            matrix,
            vector,
            matrix,
            matrix,
            matrix,
            matrix,
            vector,
            matrix,
            matrix,
            matrix,
        ),
        check_vma=False,
    )
```

```python
import functools
import math

import jax
import jax.numpy as jnp
from jax import lax
from jax.experimental import pallas as pl
from jax.experimental.pallas import tpu as pltpu
from jax.sharding import PartitionSpec as P


HEADS = 32
KV_HEADS = 4
HEAD = 64
EPSILON = 1e-05
THETA = 10000.0
SCALE = 0.125
MASKED = -1e30

GROUP = 8
TOK = 128
TOKENS = GROUP * TOK
D = 2048
MY_HEADS = HEADS // GROUP
COLS = D // GROUP
FF_ROWS = 44
FF_PAD = 48
FF_COLS = 16 * FF_PAD
KV_COLS = 2 * HEAD
QKV = COLS + KV_COLS
ATT = QKV + COLS
PACK = ATT + 2 * FF_COLS

MESH = pl.DeviceIdType.MESH
BF16 = jnp.bfloat16
F32 = jnp.float32
ANY = pl.BlockSpec(memory_space=pl.ANY)
VMEM = pl.BlockSpec(memory_space=pltpu.VMEM)


def place():
    me = lax.axis_index("dp")
    return me // 32, (me // 8) % 4, (me // 2) % 4, me % 2


def index(z, y, x, c):
    return ((z * 4 + y) * 4 + x) * 2 + c


def shifted(here, axis, step):
    spot = list(here)
    spot[axis] = (spot[axis] + step) % 4
    return index(*spot)


def group_peers(here):
    z, y, x, c = here
    return [
        ((x + dx) % 4 * 2 + (c + dc) % 2, index(z, y, (x + dx) % 4, (c + dc) % 2))
        for dx in (2, 1, 3, 0)
        for dc in (0, 1)
        if (dx, dc) != (0, 0)
    ]


GROUP_LINKS = [[(2, 1), (2, -1)]] * 2 + [[(2, 1)]] * 2 + [[(2, -1)]] * 2 + [["core"]]


def plane_peers(here):
    z, y, x, c = here
    return [
        (((z + dz) % 4, (y + dy) % 4), index((z + dz) % 4, (y + dy) % 4, x, c))
        for dz in range(4)
        for dy in range(4)
        if (dz, dy) != (0, 0)
    ]


def greet(partners):
    barrier = pltpu.get_barrier_semaphore()
    for partner in partners:
        pl.semaphore_signal(barrier, inc=1, device_id=(partner,), device_id_type=MESH)
    pl.semaphore_wait(barrier, len(partners))


HOP = 3.0
RATE = 34000.0
CORE_RATE = 450000.0
SLACK = 0.0


class Net:
    def __init__(self, send_sem, recv_sem, local_sem):
        self.sems = (send_sem, recv_sem, local_sem)
        self.sent, self.moved = 0, 0
        self.open = []
        self.now = 0.0
        self.free = {}
        self.due = {}
        self.tasks = []
        self.late = []
        self.current = None

    def start(self, program, rank=0, slack=0.0):
        task = Task(program, rank, slack)
        self.tasks.append(task)
        self.tasks.sort(key=lambda t: t.rank)
        return task

    def queue(self, copy, ref, links):
        size = math.prod(ref.shape) * jnp.dtype(ref.dtype).itemsize
        done = self.now
        for link in links:
            rate = CORE_RATE if link == "core" else RATE
            self.free[link] = max(self.free.get(link, 0.0), self.now) + size / rate
            done = max(done, self.free[link])
        self.due[id(copy)] = done + HOP
        self.open.append(copy)

    def send(self, src, dst, device, *links):
        copy = pltpu.make_async_remote_copy(
            src_ref=src,
            dst_ref=dst,
            send_sem=self.sems[0].at[self.sent],
            recv_sem=self.sems[1].at[self.sent],
            device_id=(device,),
            device_id_type=MESH,
        )
        copy.start()
        self.sent += 1
        self.queue(copy, src, links)
        if self.current is not None:
            self.current.copies.append(copy)
        return copy

    def move(self, src, dst):
        copy = pltpu.make_async_copy(src, dst, self.sems[2].at[self.moved])
        copy.start()
        self.moved += 1
        self.due[id(copy)] = self.now + 1.0
        return copy

    def spend(self, time):
        self.now += time

    def ready(self, needs):
        times = [0.0]
        for need in needs:
            if isinstance(need, Task):
                times.append(0.0 if need.done else math.inf)
            else:
                times.append(self.due[id(need)])
        return max(times)

    def leave(self, src, dst):
        self.late.append(self.move(src, dst))

    def flush(self, tasks):
        for task in tasks:
            for copy in task.copies:
                copy.wait_send()
            gone = {id(copy) for copy in task.copies}
            self.open = [copy for copy in self.open if id(copy) not in gone]

    def finish(self):
        for copy in self.open:
            copy.wait_send()
        for copy in self.late:
            copy.wait()


class Task:
    def __init__(self, program, rank, slack):
        self.program, self.rank, self.slack, self.needs, self.done = program, rank, slack, [], False
        self.copies = []


def run(net, *programs):
    for program in programs:
        net.start(program)
    while net.tasks:
        times = [net.ready(task.needs) + (task.slack if task.needs else 0.0) for task in net.tasks]
        at = next((i for i, time in enumerate(times) if time <= net.now), times.index(min(times)))
        net.now = max(net.now, times[at])
        task = net.tasks[at]
        net.current = task
        needs = next(task.program, None)
        net.current = None
        if needs is None:
            task.done = True
            net.tasks.remove(task)
        else:
            task.needs = needs


def ring_gather(net, here, axis, at, own=None):
    spot = here[axis]
    before, after = (spot + 3) % 4, (spot + 1) % 4
    up, down = shifted(here, axis, 1), shifted(here, axis, -1)
    source = (lambda part: at(spot, part)) if own is None else own
    one = net.send(source(0), at(spot, 0), up, (axis, 1))
    two = net.send(source(1), at(spot, 1), down, (axis, -1))
    three = net.send(source(1), at(spot, 1), up, (axis, 1))
    four = net.send(source(0), at(spot, 0), down, (axis, -1))
    kept = [] if own is None else [net.move(own(None), at(spot, None))]
    yield [one]
    one.wait_recv()
    five = net.send(at(before, 0), at(before, 0), up, (axis, 1))
    yield [two]
    two.wait_recv()
    six = net.send(at(after, 1), at(after, 1), down, (axis, -1))
    yield [three, four, five, six, *kept]
    for copy in (three, four, five, six):
        copy.wait_recv()
    for copy in kept:
        copy.wait()


def plane_gather(net, here, region, half, own, then=None):
    z, y = here[0], here[1]
    mine = functools.partial(own, half)
    if half == 0:
        yield from ring_gather(net, here, 1, lambda p, s: region(z, p, 0, s), mine)
        second = ring_gather(net, here, 0, lambda p, s: region(p, None, 0, s))
    else:
        yield from ring_gather(net, here, 0, lambda p, s: region(p, y, 1, s), mine)
        second = ring_gather(net, here, 1, lambda p, s: region(None, p, 1, s))
    needs = next(second)
    if then is not None:
        then()
    yield needs
    yield from second


def plane_gather_direct(net, here, region, half, own):
    z, y = here[0], here[1]
    axes = (1, 0) if half == 0 else (0, 1)
    line = region(z, None, 0, None) if half == 0 else region(None, y, 1, None)
    source = own(half, None)
    kept = net.move(source, region(z, y, half, None))
    target = region(z, y, half, None)
    for axis in axes:
        copies = [
            net.send(source, target, shifted(here, axis, 2), (axis, 1), (axis, -1)),
            net.send(source, target, shifted(here, axis, 1), (axis, 1)),
            net.send(source, target, shifted(here, axis, -1), (axis, -1)),
        ]
        yield [*copies, kept]
        for copy in copies:
            copy.wait_recv()
        if axis == axes[0]:
            kept.wait()
        source = target = line


def half_rows(ref, cols):
    def own(half, part):
        size = TOK // 2 if part is None else TOK // 4
        return ref.at[pl.ds(half * (TOK // 2) + (part or 0) * (TOK // 4), size), cols]

    return own


def half_cols(ref, width):
    def own(half, part):
        size = width // 2 if part is None else width // 4
        return ref.at[:, pl.ds(half * (width // 2) + (part or 0) * (width // 4), size)]

    return own


def group_gather(net, here, own, at):
    z, y, x, c = here
    right, left = shifted(here, 2, 1), shifted(here, 2, -1)
    peer = index(z, y, x, 1 - c)
    before, after, far = (x + 3) % 4 * 2 + c, (x + 1) % 4 * 2 + c, (x + 2) % 4 * 2 + c
    mine = x * 2 + c
    one = net.send(own(0), at(mine, 0), right, (2, 1))
    two = net.send(own(1), at(mine, 1), left, (2, -1))
    three = net.send(own(1), at(mine, 1), right, (2, 1))
    four = net.send(own(0), at(mine, 0), left, (2, -1))
    across = [net.send(own(None), at(mine, None), peer, "core")]
    kept = net.move(own(None), at(mine, None))
    yield [one]
    one.wait_recv()
    five = net.send(at(before, 0), at(before, 0), right, (2, 1))
    yield [two]
    two.wait_recv()
    six = net.send(at(after, 1), at(after, 1), left, (2, -1))
    yield [three]
    three.wait_recv()
    across.append(net.send(at(before, None), at(before, None), peer, "core"))
    yield [four]
    four.wait_recv()
    across.append(net.send(at(after, None), at(after, None), peer, "core"))
    yield [five]
    five.wait_recv()
    across.append(net.send(at(far, 0), at(far, 0), peer, "core"))
    yield [six]
    six.wait_recv()
    across.append(net.send(at(far, 1), at(far, 1), peer, "core"))
    yield [*across, kept]
    for copy in across:
        copy.wait_recv()
    kept.wait()


def group_exchange(net, here, src, dst):
    mine = here[2] * 2 + here[3]
    copies = [
        net.send(src(g), dst(mine), device, *links)
        for (g, device), links in zip(group_peers(here), GROUP_LINKS, strict=True)
    ]
    kept = net.move(src(mine), dst(mine))
    yield [*copies, kept]
    for copy in copies:
        copy.wait_recv()
    kept.wait()


def strips(rows, work, step=16, together=1):
    def body(i, carry):
        for j in range(together):
            work(pl.ds(pl.multiple_of((i * together + j) * step, step), step))
        return carry

    lax.fori_loop(0, rows // step // together, body, 0)


def add_into(total, term):
    if len(total.shape) == 3:
        for i in range(total.shape[0]):
            add_into(total.at[i], term.at[i])
        return

    def work(rows):
        total[rows] = (total[rows].astype(F32) + term[rows].astype(F32)).astype(total.dtype)

    strips(total.shape[0], work)


def add_up(out, *terms):
    if len(out.shape) == 3:
        for i in range(out.shape[0]):
            add_up(out.at[i], *[term.at[i] for term in terms])
        return

    def work(rows):
        total = terms[0][rows].astype(F32)
        for term in terms[1:]:
            total = total + term[rows].astype(F32)
        out[rows] = total.astype(out.dtype)

    strips(out.shape[0], work)


def group_reduce_scratch(rows, cols):
    return [
        pltpu.VMEM((4, rows, cols), BF16),
        pltpu.VMEM((2, rows // 2, cols), BF16),
        pltpu.VMEM((2, rows, cols), BF16),
    ]


class GroupReduce:
    ORDER = (2, 1, 3, 0)

    def __init__(self, net, here, src, out, scratch, extra=()):
        self.net, self.here, self.src, self.out, self.extra = net, here, src, out, extra
        self.crossed, self.relay, self.landed = scratch
        self.cross_copies = []

    def cross(self, slot):
        z, y, x, c = self.here
        there = (x + self.ORDER[slot]) % 4
        self.cross_copies.append(
            self.net.send(
                self.src(there * 2 + 1 - c), self.crossed.at[slot], index(z, y, x, 1 - c), "core"
            )
        )

    def steps(self):
        z, y, x, c = self.here
        net, cross = self.net, self.cross_copies
        crossed, relay, landed = self.crossed, self.relay, self.landed
        right, left = shifted(self.here, 2, 1), shifted(self.here, 2, -1)
        held = [self.src((x + step) % 4 * 2 + c) for step in self.ORDER]
        part = [
            [self.src((x + step) % 4 * 2 + c, half) for half in (0, 1)] for step in self.ORDER
        ]
        half = relay.shape[1]
        upper, lower = pl.ds(0, half), pl.ds(half, half)
        yield [cross[0]]
        cross[0].wait_recv()
        add_into(held[0], crossed.at[0])
        net.spend(1.0)
        one = net.send(part[0][0], relay.at[0], right, (2, 1))
        two = net.send(part[0][1], relay.at[1], left, (2, -1))
        yield [cross[1]]
        cross[1].wait_recv()
        add_into(held[1], crossed.at[1])
        net.spend(1.0)
        three = net.send(part[1][1], landed.at[0, lower], right, (2, 1))
        yield [cross[2]]
        cross[2].wait_recv()
        add_into(held[2], crossed.at[2])
        net.spend(1.0)
        four = net.send(part[2][0], landed.at[1, upper], left, (2, -1))
        yield [one]
        one.wait_recv()
        add_into(part[1][0], relay.at[0])
        net.spend(0.5)
        five = net.send(part[1][0], landed.at[0, upper], right, (2, 1))
        yield [two]
        two.wait_recv()
        add_into(part[2][1], relay.at[1])
        net.spend(0.5)
        six = net.send(part[2][1], landed.at[1, lower], left, (2, -1))
        yield [cross[3]]
        cross[3].wait_recv()
        add_into(held[3], crossed.at[3])
        net.spend(1.0)
        yield [three, four, five, six]
        for copy in (three, four, five, six):
            copy.wait_recv()
        add_up(self.out, held[3], landed.at[0], landed.at[1], *self.extra)
        net.spend(1.0)


def plane_reduce_scratch(rows, cols):
    return [
        pltpu.VMEM((2, 4, rows, cols), BF16),
        pltpu.VMEM((2, 2, 4, rows, cols), BF16),
        pltpu.VMEM((2, rows, cols), BF16),
        pltpu.VMEM((2, 2, rows, cols), BF16),
    ]


def plane_reduce(net, here, region, half, out, scratch):
    relay, landed, relay_two, landed_two = scratch
    axis, other = (0, 1) if half == 0 else (1, 0)

    def at(position, part, second=None):
        spots = (position, second) if half == 0 else (second, position)
        return region(*spots, half, part)

    spot = here[axis]
    up, down = shifted(here, axis, 1), shifted(here, axis, -1)
    after, before, far = (spot + 1) % 4, (spot + 3) % 4, (spot + 2) % 4
    one = net.send(at(far, 0), relay.at[0], up, (axis, 1))
    two = net.send(at(far, 1), relay.at[1], down, (axis, -1))
    three = net.send(at(after, 1), landed.at[0, 1], up, (axis, 1))
    four = net.send(at(before, 0), landed.at[1, 0], down, (axis, -1))
    cost = math.prod(relay.shape[1:]) / 250000
    yield [one]
    one.wait_recv()
    add_into(at(after, 0), relay.at[0])
    net.spend(cost)
    five = net.send(at(after, 0), landed.at[0, 0], up, (axis, 1))
    yield [two]
    two.wait_recv()
    add_into(at(before, 1), relay.at[1])
    net.spend(cost)
    six = net.send(at(before, 1), landed.at[1, 1], down, (axis, -1))
    yield [four, five]
    four.wait_recv()
    five.wait_recv()
    add_up(at(spot, 0), at(spot, 0), landed.at[0, 0], landed.at[1, 0])
    net.spend(cost)
    place_two = here[other]
    up, down = shifted(here, other, 1), shifted(here, other, -1)
    after, before, far = (place_two + 1) % 4, (place_two + 3) % 4, (place_two + 2) % 4
    seven = net.send(at(spot, 0, far), relay_two.at[0], up, (other, 1))
    eight = net.send(at(spot, 0, before), landed_two.at[1, 0], down, (other, -1))
    yield [three, six]
    three.wait_recv()
    six.wait_recv()
    add_up(at(spot, 1), at(spot, 1), landed.at[0, 1], landed.at[1, 1])
    net.spend(cost)
    nine = net.send(at(spot, 1, far), relay_two.at[1], down, (other, -1))
    ten = net.send(at(spot, 1, after), landed_two.at[0, 1], up, (other, 1))
    yield [seven]
    seven.wait_recv()
    add_into(at(spot, 0, after), relay_two.at[0])
    net.spend(cost / 4)
    eleven = net.send(at(spot, 0, after), landed_two.at[0, 0], up, (other, 1))
    yield [nine]
    nine.wait_recv()
    add_into(at(spot, 1, before), relay_two.at[1])
    net.spend(cost / 4)
    twelve = net.send(at(spot, 1, before), landed_two.at[1, 1], down, (other, -1))
    yield [eight, eleven]
    eight.wait_recv()
    eleven.wait_recv()
    add_up(out(0), at(spot, 0, place_two), landed_two.at[0, 0], landed_two.at[1, 0])
    net.spend(cost / 4)
    yield [ten, twelve]
    ten.wait_recv()
    twelve.wait_recv()
    add_up(out(1), at(spot, 1, place_two), landed_two.at[0, 1], landed_two.at[1, 1])
    net.spend(cost / 4)


def by_rows(ref, rows, cols):
    def region(z, y, half, part):
        size = rows // 2 if part is None else rows // 4
        start = half * (rows // 2) + (0 if part is None else part * (rows // 4))
        return ref.at[
            slice(None) if z is None else z, slice(None) if y is None else y, pl.ds(start, size), cols
        ]

    return region


def by_cols(ref, cols):
    def region(z, y, half, part):
        size = cols // 2 if part is None else cols // 4
        start = half * (cols // 2) + (0 if part is None else part * (cols // 4))
        return ref.at[
            slice(None) if z is None else z, slice(None) if y is None else y, :, pl.ds(start, size)
        ]

    return region


def row_block(ref, rows):
    def at(g, part=None):
        size = rows if part is None else rows // 2
        start = g * rows + (0 if part is None else part * (rows // 2))
        return ref.at[pl.ds(pl.multiple_of(start, rows // 2), size)]

    return at


def col_block(ref, rows, cols, first=0):
    def at(g, part=None):
        size = rows if part is None else rows // 2
        start = first + (0 if part is None else part * (rows // 2))
        return ref.at[pl.ds(start, size), pl.ds(pl.multiple_of(g * cols, cols), cols)]

    return at


def halves(ref, rows, first=0):
    def own(part):
        size = rows if part is None else rows // 2
        return ref.at[pl.ds(first + (0 if part is None else part * (rows // 2)), size)]

    return own


def ring_partners(here, axes):
    return [shifted(here, axis, step) for axis in axes for step in (1, -1)]


def core_peer(here):
    return index(here[0], here[1], here[2], 1 - here[3])


def communicate(kernel, collective_id, outs, scratch, n_sends, n_moves, name, inside=()):
    def call(*args):
        def body(*refs):
            n_in, n_out = len(args), len(outs)
            send_sem, recv_sem, local_sem = refs[-3:]
            net = Net(send_sem, recv_sem, local_sem)
            kernel(net, place(), refs[:n_in], refs[n_in : n_in + n_out], refs[n_in + n_out : -3])
            net.finish()

        return pl.pallas_call(
            body,
            out_shape=[jax.ShapeDtypeStruct(shape, dtype) for shape, dtype, _ in outs],
            in_specs=[VMEM if i in inside else ANY for i in range(len(args))],
            out_specs=[VMEM if near else ANY for _, _, near in outs],
            scratch_shapes=list(scratch)
            + [
                pltpu.SemaphoreType.DMA((n_sends,)),
                pltpu.SemaphoreType.DMA((n_sends,)),
                pltpu.SemaphoreType.DMA((max(n_moves, 1),)),
            ],
            compiler_params=pltpu.CompilerParams(
                collective_id=collective_id, has_side_effects=True, vmem_limit_bytes=60 << 20
            ),
            name=name,
        )(*args)

    return call


def chunk(i, size):
    return pl.ds(pl.multiple_of(i * size, size), size)


def loop(count, work):
    def body(i, carry):
        work(i)
        return carry

    lax.fori_loop(0, count, body, 0)


def lanes(shape):
    return lax.broadcasted_iota(jnp.int32, shape, 1)


def tables(aux):
    lane = lanes(aux.shape)
    by = [aux] + [pltpu.roll(aux, 32 * k, 1) for k in (1, 2, 3)]
    cosine = jnp.where(lane < 32, by[0], jnp.where(lane < 64, by[1], jnp.where(lane < 96, by[2], by[3])))
    sine = jnp.where(lane < 32, by[3], jnp.where(lane < 64, by[0], jnp.where(lane < 96, by[1], by[2])))
    sine = jnp.where(lane % 64 < 32, -sine, sine)
    begin = jnp.where(lane < 64, by[2], by[0])
    return cosine, sine, begin


def turn(values, cosine, sine):
    width = values.shape[1]
    if width > 128:
        cosine, sine = (jnp.concatenate([t] * (width // 128), axis=1) for t in (cosine, sine))
    partner = jnp.where(
        lanes(values.shape) % 64 < 32,
        pltpu.roll(values, width - 32, 1),
        pltpu.roll(values, 32, 1),
    )
    return values * cosine + partner * sine


def allowed_keys(begin):
    key = lanes(begin.shape).astype(F32)
    query = lax.broadcasted_iota(jnp.int32, begin.shape, 0).astype(F32)
    return (key >= begin) & (key <= query)


def doubled(keyed):
    lane, other = lanes(keyed.shape), pltpu.roll(keyed, 64, 1)
    keys = jnp.where(lane < 64, keyed, other).astype(BF16)
    values = jnp.where(lane < 64, other, keyed).astype(BF16)
    return keys, values


def only_half(pair, side):
    lane = lanes(pair.shape)
    keep = lane < 64 if side == 0 else lane >= 64
    return jnp.where(keep, pair, jnp.zeros_like(pair))


def probabilities(query, keys, allowed):
    scores = jnp.where(allowed, dot_last(query, keys) * SCALE, MASKED)
    powers = jnp.exp(scores - jnp.max(scores, axis=-1, keepdims=True))
    return powers / jnp.sum(powers, axis=-1, keepdims=True)


def rows_of(ref):
    return lambda g: ref.at[pl.ds(pl.multiple_of(g * 16, 16), 16)]


def pack_keyed(w_key, w_value, out):
    for x in range(KV_HEADS):
        tile = pl.ds(x // 2 * 128, 128)
        key, value = w_key[:, tile].astype(F32), w_value[:, tile].astype(F32)
        if x % 2 == 0:
            value = pltpu.roll(value, 64, 1)
        else:
            key = pltpu.roll(key, 64, 1)
        out(x, jnp.where(lanes(key.shape) < 64, key, value).astype(BF16))


def pack_feed(w, out, whole, part):
    whole[...] = w[...].astype(F32)
    part[...] = jnp.zeros_like(part)
    for g in range(GROUP):
        for spot in range(16):
            start = (spot * GROUP + g) * FF_ROWS
            part[:, spot * FF_PAD : spot * FF_PAD + FF_ROWS] = whole[:, start : start + FF_ROWS]
        out(g, part[...].astype(BF16))


def layer(net, here, inputs, outputs, scratch):
    tokens, aux, meta, upstream, w_query, w_key, w_value, w_out, w_gate, w_up, w_down = inputs
    qkv_w_out, out_w_out, normed_out, qkv_out, attended_out, residual_out, grad_gate, grad_up = outputs[:8]
    all_aux, all_meta, grad_out, mixed_out, down_out = outputs[8:]
    (
        all_tokens,
        normed,
        attended,
        residual,
        all_upstream,
        packed_one,
        packed_two,
        own_one,
        own_two,
        own_down,
        own_residual,
        qkv_w,
        out_w,
        gate_w,
        up_w,
        narrow,
        linear,
        qkv,
        mine_attended,
        mine_residual,
        gate,
        up,
        active,
        grad_down,
        seen,
        mine_meta,
        gain,
        whole,
        part,
    ) = scratch[:29]
    rest = scratch[29:]
    mixed_part, grad_part, normed_two = all_tokens, residual, normed
    z, y, x, c = here
    mine = x * 2 + c
    greet([device for _, device in group_peers(here)] + [device for _, device in plane_peers(here)])

    def small():
        copies = [net.send(meta, seen.at[mine], device) for _, device in group_peers(here)]
        kept = net.move(meta, seen.at[mine])
        yield [*copies, kept]
        for copy in copies:
            copy.wait_recv()
        kept.wait()
        mine_meta[...] = jnp.sum(seen[...], axis=0)
        spots = all_meta.at[z * 4 + y]
        copies = [net.send(mine_meta, spots, device) for _, device in plane_peers(here)]
        all_meta[z * 4 + y] = mine_meta[...]
        net.spend(1.0)
        yield copies
        for copy in copies:
            copy.wait_recv()
        for spot in range(16):
            gain[:, pl.ds(spot * 128, 128)] = all_meta[spot]

    parts = [
        (by_rows(out_w, TOK, slice(None)), half_rows(own_two, pl.ds(0, COLS))),
        (by_rows(gate_w, TOK, slice(None)), half_rows(own_two, pl.ds(COLS, FF_COLS))),
        (by_rows(up_w, TOK, slice(None)), half_rows(own_two, pl.ds(COLS + FF_COLS, FF_COLS))),
        (by_cols(narrow, D), half_cols(own_down, D)),
    ]
    tasks = {}

    def gather_part(i):
        region, source = parts[i]
        for half in (0, 1):
            follow = functools.partial(gather_part, i + 1) if half == 1 and i + 1 < len(parts) else None
            tasks[i, half] = net.start(plane_gather(net, here, region, half, source, follow), slack=SLACK)

    def exchange_one():
        def put(x, value):
            packed_one[2 * x, :, COLS:] = value
            packed_one[2 * x + 1, :, COLS:] = value

        pack_keyed(w_key, w_value, put)
        for g in range(GROUP):
            packed_one[g, :, :COLS] = w_query[:, g * COLS : (g + 1) * COLS]
        yield from group_exchange(net, here, lambda g: packed_one.at[g], rows_of(own_one))
        region, source = by_rows(qkv_w, TOK, slice(None)), half_rows(own_one, slice(None))
        for half in (0, 1):
            tasks["qkv", half] = net.start(plane_gather_direct(net, here, region, half, source))

    def exchange_two():
        for g in range(GROUP):
            packed_two[g, :, :COLS] = w_out[:, g * COLS : (g + 1) * COLS]

        def put(start):
            def store(g, value):
                packed_two[g, :, start : start + FF_COLS] = value

            return store

        full = FF_ROWS // 16 * 16
        own_down[:full] = w_down[:full]
        tail = jnp.concatenate([w_down[full:].astype(F32), jnp.zeros((FF_PAD - FF_ROWS, D), F32)], axis=0)
        own_down[full:] = tail.astype(BF16)
        pack_feed(w_gate, put(COLS), whole, part)
        pack_feed(w_up, put(COLS + FF_COLS), whole, part)
        net.spend(3.0)
        yield [exchanged]
        yield from group_exchange(net, here, lambda g: packed_two.at[g], rows_of(own_two))
        gather_part(0)

    def attend(i):
        rows = chunk(i, TOK)
        cosine, sine, begin = tables(all_aux[rows])
        allowed = allowed_keys(begin)
        local = chunk(i % (size // TOK), TOK)
        turned = turn(linear[local, :COLS], cosine, sine).astype(BF16)
        keyed = linear[local, COLS:]
        keyed = jnp.where(lanes(keyed.shape) < 64, turn(keyed, cosine, sine), keyed)
        keys, values = doubled(keyed)
        qkv[rows, :COLS] = turned
        qkv[rows, COLS:] = keyed.astype(BF16)
        for pair in range(MY_HEADS // 2):
            both = turned[:, pair * 128 : pair * 128 + 128]
            sides = []
            for side in (0, 1):
                probs = probabilities(only_half(both, side), keys, allowed)
                sides.append(matmul(probs.astype(BF16), values))
            out = jnp.where(lanes(sides[0].shape) < 64, sides[0], sides[1])
            mine_attended[rows, pair * 128 : pair * 128 + 128] = out.astype(BF16)

    def normalise(source, target, row, strip):
        values = source[strip].astype(F32)
        scale = lax.rsqrt(jnp.mean(values * values, axis=-1, keepdims=True) + EPSILON)
        target[strip] = (values * scale * gain[row : row + 1]).astype(BF16)

    def expand(i):
        rows = chunk(i, size)
        for j in range(FF_COLS // 256):
            cols = pl.ds(j * 256, 256)
            gate_val = matmul(normed_two[rows], gate_w[:, :, :, cols].reshape(D, 256))
            up_val = matmul(normed_two[rows], up_w[:, :, :, cols].reshape(D, 256))
            sigmoid_gate = 1.0 / (1.0 + jnp.exp(-gate_val))
            silu_gate = gate_val * sigmoid_gate
            active[rows, cols] = (silu_gate * up_val).astype(BF16)
            gate[rows, cols] = silu_gate.astype(BF16)
            up[rows, cols] = (
                up_val * sigmoid_gate * (1.0 + gate_val * (1.0 - sigmoid_gate))
            ).astype(BF16)

    def shrink_back(i):
        rows = chunk(i, size)
        for j in range(2):
            cols = pl.ds(j * 384, 384)
            down_rows = narrow[2 * j : 2 * j + 2].reshape(384, D)
            grad_active = dot_last(all_upstream[rows], down_rows)
            gate[rows, cols] = (grad_active * gate[rows, cols].astype(F32)).astype(BF16)
            up[rows, cols] = (grad_active * up[rows, cols].astype(F32)).astype(BF16)

    def down_gradient(j):
        cols = chunk(j, 256)
        for p in range(2):
            grad = dot_first(active[:, pl.ds(p * 384, 384)], all_upstream[:, cols])
            grad_down[2 * p : 2 * p + 2, :, :, cols] = grad.astype(BF16).reshape(2, 4, FF_PAD, 256)

    def feed_gradient(m):
        columns = normed_two[:, chunk(m, 256)]
        spots = pl.ds(m % 2 * 2, 2)
        gate_w[m // 2, spots] = dot_first(columns, up[...]).astype(BF16).reshape(2, TOK, FF_COLS)
        up_w[m // 2, spots] = dot_first(columns, gate[...]).astype(BF16).reshape(2, TOK, FF_COLS)

    pieces = 4
    size = TOKENS // pieces
    quarter = D // 4

    def narrow_part(half):
        return lambda part: down_out.at[:, pl.ds((half * 2 + part) * quarter, quarter)]

    def gathered(i):
        while (i, 1) not in tasks:
            yield [tasks[i - 1, 1]]
        yield [tasks[i, 0], tasks[i, 1]]

    def work():
        yield [gains, took]
        strips(TOKENS, functools.partial(normalise, all_tokens, normed, 0), together=4)
        net.spend(4.0)
        normed_copy = net.move(normed, normed_out)
        yield [exchanged, placed]
        yield [tasks["qkv", 0], tasks["qkv", 1]]
        net.leave(qkv_w, qkv_w_out)
        sent = []
        for i in range(pieces):
            rows = pl.ds(i * size, size)
            linear[...] = matmul(normed[rows], qkv_w[...].reshape(D, QKV))
            loop(size // TOK, lambda j, i=i: attend(j + i * (size // TOK)))
            net.spend(3.0)
            at = col_block(attended, size, COLS, i * size)
            sent.append(net.start(group_gather(net, here, halves(mine_attended, size, i * size), at)))
            yield []
        net.leave(qkv, qkv_out)
        my_cols = pl.ds(pl.multiple_of(mine * COLS, COLS), COLS)
        yield [other]
        yield from gathered(0)
        net.leave(out_w, out_w_out)
        last = []
        for i in range(pieces):
            yield [sent[i]]
            rows = pl.ds(i * size, size)
            out = matmul(attended[rows], out_w[...].reshape(D, COLS))
            mine_residual[rows] = (all_tokens[rows, my_cols].astype(F32) + out).astype(BF16)
            net.spend(0.8)
            at = col_block(residual, size, COLS, i * size)
            last.append(net.start(group_gather(net, here, halves(mine_residual, size, i * size), at)))
            yield []
        late = net.start(group_gather(net, here, halves(upstream, TOK), row_block(all_upstream, TOK)))
        yield []
        net.leave(attended, attended_out)
        normed_copy.wait()
        for i in (1, 2):
            yield from gathered(i)
        for i in range(pieces):
            yield [last[i]]

            def norm(strip, i=i):
                start = pl.multiple_of(i * size + strip.start, 16)
                normalise(residual, normed_two, 1, pl.ds(start, 16))

            strips(size, norm, together=4)
            expand(i)
            net.spend(4.3)
            yield []
        own_copy = net.move(row_block(residual, TOK)(mine), own_residual)
        net.flush([took])
        yield from gathered(3)
        own_copy.wait()
        net.leave(own_residual, residual_out)
        mix = GroupReduce(net, here, row_block(mixed_part, TOK), mixed_out, rest[0:3], [own_residual])
        for slot, step in enumerate(GroupReduce.ORDER):
            there = chunk((x + step) % 4, size)

            def mixed(j):
                cols = chunk(j, 512)
                out = matmul(active[there], narrow[:, :, :, cols].reshape(FF_COLS, 512))
                mixed_part[there, cols] = out.astype(BF16)

            loop(D // 512, mixed)
            net.spend(1.3)
            mix.cross(slot)
            yield []
        net.start(mix.steps())
        yield [late]
        for i in range(pieces):
            shrink_back(i)
            net.spend(2.0)
            yield []
        net.flush(last)
        back = GroupReduce(net, here, row_block(grad_part, TOK), grad_out, rest[3:6])
        for slot, step in enumerate(GroupReduce.ORDER):
            there = chunk((x + step) % 4, size)

            def to_input(j):
                total = dot_last(up[there], gate_w[j].reshape(512, FF_COLS))
                total = total + dot_last(gate[there], up_w[j].reshape(512, FF_COLS))
                grad_part[there, chunk(j, 512)] = total.astype(BF16)

            loop(D // 512, to_input)
            net.spend(2.3)
            back.cross(slot)
            yield []
        net.start(back.steps())
        loop(4, down_gradient)
        net.spend(2.3)
        yield []
        loop(4, lambda j: down_gradient(j + 4))
        net.spend(2.3)
        region = by_cols(grad_down, D)
        for half in (0, 1):
            room = rest[6 + 4 * half : 10 + 4 * half]
            net.start(plane_reduce(net, here, region, half, narrow_part(half), room), slack=SLACK)
        yield []
        net.flush([tasks[i, half] for i in (1, 2) for half in (0, 1)])
        for m in range(8):
            feed_gradient(m)
            net.spend(1.3)
            yield []
            if m % 2 == 1:
                net.leave(gate_w.at[m // 2], grad_gate.at[m // 2])
                net.leave(up_w.at[m // 2], grad_up.at[m // 2])

    exchanged = net.start(exchange_one())
    gains = net.start(small())
    took = net.start(group_gather(net, here, halves(tokens, TOK), row_block(all_tokens, TOK)))
    placed = net.start(group_gather(net, here, halves(aux, TOK), row_block(all_aux, TOK)))
    other = net.start(exchange_two())
    net.start(work(), rank=1)
    run(net)


def layer_call(*args):
    outs = [
        ((4, 4, TOK, QKV), BF16, False),
        ((4, 4, TOK, COLS), BF16, False),
        ((TOKENS, D), BF16, False),
        ((TOKENS, QKV), BF16, False),
        ((TOKENS, D), BF16, False),
        ((TOK, D), BF16, False),
        ((4, 4, TOK, FF_COLS), BF16, False),
        ((4, 4, TOK, FF_COLS), BF16, False),
        ((TOKENS, 128), F32, True),
        ((16, 8, 128), F32, True),
        ((TOK, D), F32, True),
        ((TOK, D), BF16, True),
        ((FF_PAD, D), F32, True),
    ]
    scratch = [pltpu.VMEM((TOKENS, D), BF16)] * 5 + [
        pltpu.VMEM((GROUP, 16, QKV), BF16),
        pltpu.VMEM((GROUP, 16, COLS + 2 * FF_COLS), BF16),
        pltpu.VMEM((TOK, QKV), BF16),
        pltpu.VMEM((TOK, COLS + 2 * FF_COLS), BF16),
        pltpu.VMEM((FF_PAD, D), BF16),
        pltpu.VMEM((TOK, D), BF16),
        pltpu.VMEM((4, 4, TOK, QKV), BF16),
        pltpu.VMEM((4, 4, TOK, COLS), BF16),
        pltpu.VMEM((4, 4, TOK, FF_COLS), BF16),
        pltpu.VMEM((4, 4, TOK, FF_COLS), BF16),
        pltpu.VMEM((4, 4, FF_PAD, D), BF16),
        pltpu.VMEM((TOKENS // 4, QKV), F32),
        pltpu.VMEM((TOKENS, QKV), BF16),
        pltpu.VMEM((TOKENS, COLS), BF16),
        pltpu.VMEM((TOKENS, COLS), BF16),
        pltpu.VMEM((TOKENS, FF_COLS), BF16),
        pltpu.VMEM((TOKENS, FF_COLS), BF16),
        pltpu.VMEM((TOKENS, FF_COLS), BF16),
        pltpu.VMEM((4, 4, FF_PAD, D), BF16),
        pltpu.VMEM((8, 8, 128), F32),
        pltpu.VMEM((8, 128), F32),
        pltpu.VMEM((8, D), F32),
        pltpu.VMEM((16, 16 * GROUP * FF_ROWS), F32),
        pltpu.VMEM((16, FF_COLS), F32),
    ]
    scratch += group_reduce_scratch(TOK, D) * 2 + plane_reduce_scratch(FF_PAD, D // 4) * 2
    return communicate(layer, 0, outs, scratch, 400, 60, "layer", inside=range(4, 11))(*args)


def quarter_rows(ref):
    return lambda half: lambda part: ref.at[pl.ds((half * 2 + part) * (TOK // 4), TOK // 4)]


def backward(net, here, inputs, outputs, scratch):
    (
        grad_normed_two,
        all_residual,
        upstream,
        tokens,
        all_meta,
        all_aux,
        qkv_in,
        qkv_w_in,
        out_w_in,
        normed_in,
        attended_in,
        gate_in,
        up_in,
        w_query,
        w_key,
        w_value,
        w_gate,
        w_up,
    ) = inputs
    grad_tokens, norms_out, grad_query, grad_key, grad_value, grad_out, grad_gate_out, grad_up_out = outputs
    (
        grad_two,
        residual,
        own_upstream,
        own_tokens,
        grad_residual,
        grad_rounded,
        gains,
        grad_cols,
        qkv_w,
        out_w,
        heads_part,
        heads,
        qkv,
        grad_lin,
        normed,
        attended,
        input_part,
        grad_one,
        grad_gate,
        grad_up,
        grad_qkv_w,
        grad_out_w,
        gate_sum,
        up_sum,
        qkv_sum,
        out_sum,
        gate_rows,
        up_rows,
        qkv_rows,
        out_rows,
        part,
    ) = scratch[:31]
    rest = scratch[31:]
    z, y, x, c = here
    mine = x * 2 + c
    loads = {
        "grad_two": net.move(grad_normed_two, grad_two),
        "residual": net.move(all_residual, residual),
        "upstream": net.move(upstream, own_upstream),
        "gate": net.move(gate_in, grad_gate),
        "out_w": net.move(out_w_in, out_w),
        "qkv_w": net.move(qkv_w_in, qkv_w),
        "up": net.move(up_in, grad_up),
        "qkv": net.move(qkv_in, qkv),
        "attended": net.move(attended_in, attended),
        "normed": net.move(normed_in, normed),
        "tokens": net.move(tokens, own_tokens),
    }
    greet([device for _, device in group_peers(here)] + ring_partners(here, (0, 1)))

    def unpack_feed(rows, out, w, column):
        def finish():
            for g in range(GROUP):
                part[...] = rows[g].astype(F32)
                for spot in range(16):
                    start = (spot * GROUP + g) * FF_ROWS
                    out[:, start : start + FF_ROWS] = part[:, spot * FF_PAD : spot * FF_PAD + FF_ROWS]
            add_norm(column, [(out, w)])
            net.spend(2.0)

        return finish

    def add_norm(column, pairs):
        total = sum(
            jnp.sum(grad[...] * w[...].astype(F32), axis=-1, keepdims=True) for grad, w in pairs
        )
        norms_out[...] += jnp.where(lanes((16, 128)) == column, total, 0.0)

    def unpack_qkv():
        for g in range(GROUP):
            grad_query[:, g * COLS : (g + 1) * COLS] = qkv_rows[g, :, :COLS].astype(F32)
        keyed = [
            qkv_rows[2 * i, :, COLS:].astype(F32) + qkv_rows[2 * i + 1, :, COLS:].astype(F32)
            for i in range(KV_HEADS)
        ]
        lane = lanes(keyed[0].shape)
        for i in range(KV_HEADS // 2):
            first, second = keyed[2 * i], keyed[2 * i + 1]
            cols = pl.ds(i * 128, 128)
            grad_key[:, cols] = jnp.where(lane < 64, first, pltpu.roll(second, 64, 1))
            grad_value[:, cols] = jnp.where(lane < 64, pltpu.roll(first, 64, 1), second)
        add_norm(0, [(grad_query, w_query), (grad_key, w_key), (grad_value, w_value)])

    def unpack_out():
        for g in range(GROUP):
            grad_out[:, g * COLS : (g + 1) * COLS] = out_rows[g].astype(F32)

    def feed_gradients():
        for name, source, total, rows, room, out, w in (
            ("gate", grad_gate, gate_sum, gate_rows, rest[0:8], grad_gate_out, w_gate),
            ("up", grad_up, up_sum, up_rows, rest[8:16], grad_up_out, w_up),
        ):
            yield [loads[name]]
            loads[name].wait()
            yield [give_back(source, total, rows, room, unpack_feed(rows, out, w, 1))]

    def give_back(source, total, rows, room, unpack):
        region, part = by_rows(source, TOK, slice(None)), quarter_rows(total)
        tasks = [
            net.start(plane_reduce(net, here, region, half, part(half), room[4 * half : 4 * half + 4]), slack=SLACK)
            for half in (0, 1)
        ]

        def hand_out():
            yield tasks
            yield from group_exchange(net, here, rows_of(total), lambda g: rows.at[g])
            unpack()

        net.start(hand_out())
        return tasks[1]

    def residual_back(strip):
        values = residual[strip].astype(F32)
        scale = lax.rsqrt(jnp.mean(values * values, axis=-1, keepdims=True) + EPSILON)
        unit = values * scale
        grad = grad_two[strip]
        grad = grad * gains[1:2]
        grad = scale * (grad - unit * jnp.mean(grad * unit, axis=-1, keepdims=True))
        grad = own_upstream[strip].astype(F32) + grad
        grad_residual[strip] = grad
        grad_rounded[strip] = grad.astype(BF16)

    def input_back(strip):
        values = own_tokens[strip].astype(F32)
        scale = lax.rsqrt(jnp.mean(values * values, axis=-1, keepdims=True) + EPSILON)
        unit = values * scale
        grad = grad_one[strip]
        grad = grad * gains[0:1]
        grad = scale * (grad - unit * jnp.mean(grad * unit, axis=-1, keepdims=True))
        grad_tokens[strip] = grad_residual[strip] + grad

    def attend_back(i):
        rows = chunk(i, TOK)
        cosine, sine, begin = tables(all_aux[rows])
        allowed = allowed_keys(begin)
        keys, values = doubled(qkv[rows, COLS:].astype(F32))
        grad_queries = []
        grad_keys = jnp.zeros((TOK, 128), F32)
        grad_values = jnp.zeros((TOK, 128), F32)
        for pair in range(MY_HEADS // 2):
            cols = pl.ds(pair * 128, 128)
            queries, grads = qkv[rows, cols], heads[rows, cols]
            sides = []
            for side in (0, 1):
                query, grad = only_half(queries, side), only_half(grads, side)
                probs = probabilities(query, keys, allowed)
                grad_probs = dot_last(grad, values)
                grad_scores = probs * (grad_probs - jnp.sum(probs * grad_probs, axis=-1, keepdims=True))
                grad_scores = grad_scores.astype(BF16)
                sides.append(matmul(grad_scores, keys))
                grad_keys = grad_keys + dot_first(grad_scores, query)
                grad_values = grad_values + dot_first(probs.astype(BF16), grad)
            grad_queries.append(jnp.where(lanes(sides[0].shape) < 64, sides[0], sides[1]))
        grad_query = jnp.concatenate(grad_queries, axis=1) * SCALE
        grad_lin[rows, :COLS] = turn(grad_query, cosine, -sine).astype(BF16)
        grad_keys = turn((grad_keys + pltpu.roll(grad_keys, 64, 1)) * SCALE, cosine, -sine)
        grad_values = grad_values + pltpu.roll(grad_values, 64, 1)
        grad_lin[rows, COLS:] = jnp.where(lanes(grad_keys.shape) < 64, grad_keys, grad_values).astype(BF16)

    half_tokens = TOKENS // 2

    def work():
        for name in ("grad_two", "residual", "upstream"):
            loads[name].wait()
        for spot in range(16):
            gains[:, pl.ds(spot * 128, 128)] = all_meta[spot]
        norms_out[...] = jnp.zeros_like(norms_out)
        strips(TOK, residual_back, together=2)
        net.spend(2.0)
        spread = net.start(
            group_exchange(net, here, col_block(grad_rounded, TOK, COLS), row_block(grad_cols, TOK))
        )
        yield []
        loads["out_w"].wait()
        yield [spread]
        reduced = []
        for half in (0, 1):
            first = half * half_tokens
            rows = pl.ds(first, half_tokens)
            room = rest[24 + 3 * half : 27 + 3 * half]
            reduce = GroupReduce(
                net, here, col_block(heads_part, half_tokens, COLS, first), heads.at[rows], room
            )
            for slot, step in enumerate(GroupReduce.ORDER):
                cols = chunk((x + step) % 4, 2 * COLS)
                part = dot_last(grad_cols[rows], out_w[cols])
                heads_part[rows, cols] = part.astype(BF16)
                net.spend(0.6)
                reduce.cross(slot)
            reduced.append(net.start(reduce.steps()))
        yield []
        loads["attended"].wait()

        def out_gradient(m):
            part = dot_first(attended[:, chunk(m, 256)], grad_cols[...]).astype(BF16)
            grad_out_w[m // 2, pl.ds(m % 2 * 2, 2)] = part.reshape(2, TOK, COLS)

        for half in (0, 1):
            loop(4, lambda m, half=half: out_gradient(m + 4 * half))
            net.spend(2.3)
            yield []
        give_back(grad_out_w, out_sum, out_rows, rest[33:41], unpack_out)
        loads["qkv"].wait()
        loads["qkv_w"].wait()
        for half in (0, 1):
            yield [reduced[half]]
            loop(4, lambda i, half=half: attend_back(i + 4 * half))
            net.spend(6.0)
        reduce = GroupReduce(net, here, row_block(input_part, TOK), grad_one, rest[30:33])
        for slot, step in enumerate(GroupReduce.ORDER):
            there = chunk((x + step) % 4, 256)

            def to_input(j):
                cols = chunk(j, 512)
                part = dot_last(grad_lin[there], qkv_w[cols])
                input_part[there, cols] = part.astype(BF16)

            loop(D // 512, to_input)
            net.spend(1.3)
            reduce.cross(slot)
            yield []
        reduced = net.start(reduce.steps())
        loads["normed"].wait()

        def in_gradient(m):
            part = dot_first(normed[:, chunk(m, 256)], grad_lin[...]).astype(BF16)
            grad_qkv_w[m // 2, pl.ds(m % 2 * 2, 2)] = part.reshape(2, TOK, QKV)

        loop(8, in_gradient)
        net.spend(3.5)
        give_back(grad_qkv_w, qkv_sum, qkv_rows, rest[16:24], unpack_qkv)
        loads["tokens"].wait()
        yield [reduced]
        strips(TOK, input_back, together=2)
        net.spend(2.0)

    net.start(feed_gradients())
    net.start(work(), rank=1)
    run(net)


def backward_call(*args):
    outs = [
        ((TOK, D), F32, True),
        ((16, 128), F32, True),
        ((16, D), F32, True),
        ((16, KV_HEADS * HEAD), F32, True),
        ((16, KV_HEADS * HEAD), F32, True),
        ((16, D), F32, True),
        ((16, 16 * GROUP * FF_ROWS), F32, True),
        ((16, 16 * GROUP * FF_ROWS), F32, True),
    ]
    scratch = [
        pltpu.VMEM((TOK, D), F32),
        pltpu.VMEM((TOK, D), BF16),
        pltpu.VMEM((TOK, D), BF16),
        pltpu.VMEM((TOK, D), BF16),
        pltpu.VMEM((TOK, D), F32),
        pltpu.VMEM((TOK, D), BF16),
        pltpu.VMEM((8, D), F32),
        pltpu.VMEM((TOKENS, COLS), BF16),
        pltpu.VMEM((D, QKV), BF16),
        pltpu.VMEM((D, COLS), BF16),
        pltpu.VMEM((TOKENS, D), BF16),
        pltpu.VMEM((TOKENS, COLS), BF16),
        pltpu.VMEM((TOKENS, QKV), BF16),
        pltpu.VMEM((TOKENS, QKV), BF16),
        pltpu.VMEM((TOKENS, D), BF16),
        pltpu.VMEM((TOKENS, D), BF16),
        pltpu.VMEM((TOKENS, D), BF16),
        pltpu.VMEM((TOK, D), F32),
        pltpu.VMEM((4, 4, TOK, FF_COLS), BF16),
        pltpu.VMEM((4, 4, TOK, FF_COLS), BF16),
        pltpu.VMEM((4, 4, TOK, QKV), BF16),
        pltpu.VMEM((4, 4, TOK, COLS), BF16),
        pltpu.VMEM((TOK, FF_COLS), BF16),
        pltpu.VMEM((TOK, FF_COLS), BF16),
        pltpu.VMEM((TOK, QKV), BF16),
        pltpu.VMEM((TOK, COLS), BF16),
        pltpu.VMEM((GROUP, 16, FF_COLS), BF16),
        pltpu.VMEM((GROUP, 16, FF_COLS), BF16),
        pltpu.VMEM((GROUP, 16, QKV), BF16),
        pltpu.VMEM((GROUP, 16, COLS), BF16),
        pltpu.VMEM((16, FF_COLS), F32),
    ]
    scratch += plane_reduce_scratch(TOK // 4, FF_COLS) * 4 + plane_reduce_scratch(TOK // 4, QKV) * 2
    scratch += group_reduce_scratch(TOKENS // 2, COLS) * 2 + group_reduce_scratch(TOK, D)
    scratch += plane_reduce_scratch(TOK // 4, COLS) * 2
    return communicate(
        backward, 1, outs, scratch, 180, 60, "backward", inside=(4, 5, 13, 14, 15, 16, 17)
    )(*args)


def sequence_table(lengths):
    ends = jnp.cumsum(lengths)
    places = jnp.arange(TOK, dtype=jnp.int32)
    begins = jnp.max(jnp.where(places[:, None] >= ends[None, :], ends[None, :], 0), axis=-1)
    inverse = jnp.exp(jnp.arange(HEAD // 2, dtype=F32) * (-2.0 * math.log(THETA) / HEAD))
    angle = (places - begins).astype(F32)[:, None] * inverse[None, :]
    start = jnp.broadcast_to(begins.astype(F32)[:, None], (TOK, 64))
    return jnp.concatenate([jnp.cos(angle), jnp.sin(angle), start], axis=1)


def matmul(left, right):
    return jnp.dot(left, right, preferred_element_type=F32)


def dot_last(left, right):
    return lax.dot_general(left, right, (((1,), (1,)), ((), ())), preferred_element_type=F32)


def dot_first(left, right):
    return lax.dot_general(left, right, (((0,), (0,)), ((), ())), preferred_element_type=F32)


def on_device(
    tokens,
    seq_lengths,
    attn_norm,
    w_query,
    w_key,
    w_value,
    w_out,
    mlp_norm,
    w_gate,
    w_up,
    w_down,
    cotangent,
):
    me = lax.axis_index("dp")
    member = me % GROUP
    meta = jnp.stack([attn_norm.astype(F32), mlp_norm.astype(F32)])
    meta = lax.dynamic_update_slice(jnp.zeros((8, 128), F32), meta, (0, member * 16))
    (
        qkv_w,
        out_w,
        normed,
        qkv,
        all_attended,
        own_residual,
        grad_gate,
        grad_up,
        all_aux,
        all_meta,
        grad_normed_two,
        mixed_out,
        down_sum,
    ) = layer_call(
        tokens,
        sequence_table(seq_lengths[0]),
        meta,
        cotangent,
        w_query,
        w_key,
        w_value,
        w_out,
        w_gate,
        w_up,
        w_down,
    )
    grad_tokens, norms, grad_query, grad_key, grad_value, grad_out, grad_gate, grad_up = backward_call(
        grad_normed_two,
        own_residual,
        cotangent,
        tokens,
        all_meta,
        all_aux,
        qkv,
        qkv_w.reshape(D, QKV),
        out_w.reshape(D, COLS),
        normed,
        all_attended,
        grad_gate,
        grad_up,
        w_query,
        w_key,
        w_value,
        w_gate,
        w_up,
    )
    return (
        mixed_out,
        grad_tokens,
        norms[:, 0] / attn_norm.astype(F32),
        grad_query,
        grad_key,
        grad_value,
        grad_out,
        norms[:, 1] / mlp_norm.astype(F32),
        grad_gate,
        grad_up,
        down_sum[:FF_ROWS],
    )


def solution(mesh):
    matrix, vector = P("dp", None), P("dp")
    return jax.shard_map(
        on_device,
        mesh=mesh,
        in_specs=(
            matrix,
            matrix,
            vector,
            matrix,
            matrix,
            matrix,
            matrix,
            vector,
            matrix,
            matrix,
            matrix,
            matrix,
        ),
        out_specs=(
            matrix,
            matrix,
            vector,
            matrix,
            matrix,
            matrix,
            matrix,
            vector,
            matrix,
            matrix,
            matrix,
        ),
        check_vma=False,
    )
```

```python
import functools
import math

import jax
import jax.numpy as jnp
from jax import lax
from jax.experimental import pallas as pl
from jax.experimental.pallas import tpu as pltpu
from jax.sharding import PartitionSpec as P


HEADS = 32
KV_HEADS = 4
HEAD = 64
EPSILON = 1e-05
THETA = 10000.0
SCALE = 0.125
MASKED = -1e30

GROUP = 8
TOK = 128
TOKENS = GROUP * TOK
D = 2048
MY_HEADS = HEADS // GROUP
COLS = D // GROUP
FF_ROWS = 44
FF_PAD = 48
FF_COLS = 16 * FF_PAD
KV_COLS = 2 * HEAD
QKV = COLS + KV_COLS
ATT = QKV + COLS
PACK = ATT + 2 * FF_COLS

MESH = pl.DeviceIdType.MESH
BF16 = jnp.bfloat16
F32 = jnp.float32
ANY = pl.BlockSpec(memory_space=pl.ANY)
VMEM = pl.BlockSpec(memory_space=pltpu.VMEM)


def place():
    me = lax.axis_index("dp")
    return me // 32, (me // 8) % 4, (me // 2) % 4, me % 2


def index(z, y, x, c):
    return ((z * 4 + y) * 4 + x) * 2 + c


def shifted(here, axis, step):
    spot = list(here)
    spot[axis] = (spot[axis] + step) % 4
    return index(*spot)


def group_peers(here):
    z, y, x, c = here
    return [
        ((x + dx) % 4 * 2 + (c + dc) % 2, index(z, y, (x + dx) % 4, (c + dc) % 2))
        for dx in (2, 1, 3, 0)
        for dc in (0, 1)
        if (dx, dc) != (0, 0)
    ]


GROUP_LINKS = [[(2, 1), (2, -1)]] * 2 + [[(2, 1)]] * 2 + [[(2, -1)]] * 2 + [["core"]]


def plane_peers(here):
    z, y, x, c = here
    return [
        (((z + dz) % 4, (y + dy) % 4), index((z + dz) % 4, (y + dy) % 4, x, c))
        for dz in range(4)
        for dy in range(4)
        if (dz, dy) != (0, 0)
    ]


def greet(partners):
    barrier = pltpu.get_barrier_semaphore()
    for partner in partners:
        pl.semaphore_signal(barrier, inc=1, device_id=(partner,), device_id_type=MESH)
    pl.semaphore_wait(barrier, len(partners))


HOP = 3.0
RATE = 34000.0
CORE_RATE = 450000.0
SLACK = 0.0


class Net:
    def __init__(self, send_sem, recv_sem, local_sem):
        self.sems = (send_sem, recv_sem, local_sem)
        self.sent, self.moved = 0, 0
        self.open = []
        self.now = 0.0
        self.free = {}
        self.due = {}
        self.tasks = []
        self.late = []
        self.current = None

    def start(self, program, rank=0, slack=0.0):
        task = Task(program, rank, slack)
        self.tasks.append(task)
        self.tasks.sort(key=lambda t: t.rank)
        return task

    def queue(self, copy, ref, links):
        size = math.prod(ref.shape) * jnp.dtype(ref.dtype).itemsize
        done = self.now
        for link in links:
            rate = CORE_RATE if link == "core" else RATE
            self.free[link] = max(self.free.get(link, 0.0), self.now) + size / rate
            done = max(done, self.free[link])
        self.due[id(copy)] = done + HOP
        self.open.append(copy)

    def send(self, src, dst, device, *links):
        copy = pltpu.make_async_remote_copy(
            src_ref=src,
            dst_ref=dst,
            send_sem=self.sems[0].at[self.sent],
            recv_sem=self.sems[1].at[self.sent],
            device_id=(device,),
            device_id_type=MESH,
        )
        copy.start()
        self.sent += 1
        self.queue(copy, src, links)
        if self.current is not None:
            self.current.copies.append(copy)
        return copy

    def move(self, src, dst):
        copy = pltpu.make_async_copy(src, dst, self.sems[2].at[self.moved])
        copy.start()
        self.moved += 1
        self.due[id(copy)] = self.now + 1.0
        return copy

    def spend(self, time):
        self.now += time

    def ready(self, needs):
        times = [0.0]
        for need in needs:
            if isinstance(need, Task):
                times.append(0.0 if need.done else math.inf)
            else:
                times.append(self.due[id(need)])
        return max(times)

    def leave(self, src, dst):
        self.late.append(self.move(src, dst))

    def flush(self, tasks):
        for task in tasks:
            for copy in task.copies:
                copy.wait_send()
            gone = {id(copy) for copy in task.copies}
            self.open = [copy for copy in self.open if id(copy) not in gone]

    def finish(self):
        for copy in self.open:
            copy.wait_send()
        for copy in self.late:
            copy.wait()


class Task:
    def __init__(self, program, rank, slack):
        self.program, self.rank, self.slack, self.needs, self.done = program, rank, slack, [], False
        self.copies = []


def run(net, *programs):
    for program in programs:
        net.start(program)
    while net.tasks:
        times = [net.ready(task.needs) + (task.slack if task.needs else 0.0) for task in net.tasks]
        at = next((i for i, time in enumerate(times) if time <= net.now), times.index(min(times)))
        net.now = max(net.now, times[at])
        task = net.tasks[at]
        net.current = task
        needs = next(task.program, None)
        net.current = None
        if needs is None:
            task.done = True
            net.tasks.remove(task)
        else:
            task.needs = needs


def ring_gather(net, here, axis, at, own=None):
    spot = here[axis]
    before, after = (spot + 3) % 4, (spot + 1) % 4
    up, down = shifted(here, axis, 1), shifted(here, axis, -1)
    source = (lambda part: at(spot, part)) if own is None else own
    one = net.send(source(0), at(spot, 0), up, (axis, 1))
    two = net.send(source(1), at(spot, 1), down, (axis, -1))
    three = net.send(source(1), at(spot, 1), up, (axis, 1))
    four = net.send(source(0), at(spot, 0), down, (axis, -1))
    kept = [] if own is None else [net.move(own(None), at(spot, None))]
    yield [one]
    one.wait_recv()
    five = net.send(at(before, 0), at(before, 0), up, (axis, 1))
    yield [two]
    two.wait_recv()
    six = net.send(at(after, 1), at(after, 1), down, (axis, -1))
    yield [three, four, five, six, *kept]
    for copy in (three, four, five, six):
        copy.wait_recv()
    for copy in kept:
        copy.wait()


def plane_gather(net, here, region, half, own, then=None):
    z, y = here[0], here[1]
    mine = functools.partial(own, half)
    if half == 0:
        yield from ring_gather(net, here, 1, lambda p, s: region(z, p, 0, s), mine)
        second = ring_gather(net, here, 0, lambda p, s: region(p, None, 0, s))
    else:
        yield from ring_gather(net, here, 0, lambda p, s: region(p, y, 1, s), mine)
        second = ring_gather(net, here, 1, lambda p, s: region(None, p, 1, s))
    needs = next(second)
    if then is not None:
        then()
    yield needs
    yield from second


def plane_gather_direct(net, here, region, half, own):
    z, y = here[0], here[1]
    axes = (1, 0) if half == 0 else (0, 1)
    line = region(z, None, 0, None) if half == 0 else region(None, y, 1, None)
    source = own(half, None)
    kept = net.move(source, region(z, y, half, None))
    target = region(z, y, half, None)
    for axis in axes:
        copies = [
            net.send(source, target, shifted(here, axis, 2), (axis, 1), (axis, -1)),
            net.send(source, target, shifted(here, axis, 1), (axis, 1)),
            net.send(source, target, shifted(here, axis, -1), (axis, -1)),
        ]
        yield [*copies, kept]
        for copy in copies:
            copy.wait_recv()
        if axis == axes[0]:
            kept.wait()
        source = target = line


def half_rows(ref, cols):
    def own(half, part):
        size = TOK // 2 if part is None else TOK // 4
        return ref.at[pl.ds(half * (TOK // 2) + (part or 0) * (TOK // 4), size), cols]

    return own


def half_cols(ref, width):
    def own(half, part):
        size = width // 2 if part is None else width // 4
        return ref.at[:, pl.ds(half * (width // 2) + (part or 0) * (width // 4), size)]

    return own


def group_gather(net, here, own, at):
    z, y, x, c = here
    right, left = shifted(here, 2, 1), shifted(here, 2, -1)
    peer = index(z, y, x, 1 - c)
    before, after, far = (x + 3) % 4 * 2 + c, (x + 1) % 4 * 2 + c, (x + 2) % 4 * 2 + c
    mine = x * 2 + c
    one = net.send(own(0), at(mine, 0), right, (2, 1))
    two = net.send(own(1), at(mine, 1), left, (2, -1))
    three = net.send(own(1), at(mine, 1), right, (2, 1))
    four = net.send(own(0), at(mine, 0), left, (2, -1))
    across = [net.send(own(None), at(mine, None), peer, "core")]
    kept = net.move(own(None), at(mine, None))
    yield [one]
    one.wait_recv()
    five = net.send(at(before, 0), at(before, 0), right, (2, 1))
    yield [two]
    two.wait_recv()
    six = net.send(at(after, 1), at(after, 1), left, (2, -1))
    yield [three]
    three.wait_recv()
    across.append(net.send(at(before, None), at(before, None), peer, "core"))
    yield [four]
    four.wait_recv()
    across.append(net.send(at(after, None), at(after, None), peer, "core"))
    yield [five]
    five.wait_recv()
    across.append(net.send(at(far, 0), at(far, 0), peer, "core"))
    yield [six]
    six.wait_recv()
    across.append(net.send(at(far, 1), at(far, 1), peer, "core"))
    yield [*across, kept]
    for copy in across:
        copy.wait_recv()
    kept.wait()


def group_exchange(net, here, src, dst):
    mine = here[2] * 2 + here[3]
    copies = [
        net.send(src(g), dst(mine), device, *links)
        for (g, device), links in zip(group_peers(here), GROUP_LINKS, strict=True)
    ]
    kept = net.move(src(mine), dst(mine))
    yield [*copies, kept]
    for copy in copies:
        copy.wait_recv()
    kept.wait()


def strips(rows, work, step=16, together=1):
    def body(i, carry):
        for j in range(together):
            work(pl.ds(pl.multiple_of((i * together + j) * step, step), step))
        return carry

    lax.fori_loop(0, rows // step // together, body, 0)


def add_into(total, term):
    if len(total.shape) == 3:
        for i in range(total.shape[0]):
            add_into(total.at[i], term.at[i])
        return

    def work(rows):
        total[rows] = (total[rows].astype(F32) + term[rows].astype(F32)).astype(total.dtype)

    strips(total.shape[0], work)


def add_up(out, *terms):
    if len(out.shape) == 3:
        for i in range(out.shape[0]):
            add_up(out.at[i], *[term.at[i] for term in terms])
        return

    def work(rows):
        total = terms[0][rows].astype(F32)
        for term in terms[1:]:
            total = total + term[rows].astype(F32)
        out[rows] = total.astype(out.dtype)

    strips(out.shape[0], work)


def group_reduce_scratch(rows, cols):
    return [
        pltpu.VMEM((4, rows, cols), BF16),
        pltpu.VMEM((2, rows // 2, cols), BF16),
        pltpu.VMEM((2, rows, cols), BF16),
    ]


class GroupReduce:
    ORDER = (2, 1, 3, 0)

    def __init__(self, net, here, src, out, scratch, extra=()):
        self.net, self.here, self.src, self.out, self.extra = net, here, src, out, extra
        self.crossed, self.relay, self.landed = scratch
        self.cross_copies = []

    def cross(self, slot):
        z, y, x, c = self.here
        there = (x + self.ORDER[slot]) % 4
        self.cross_copies.append(
            self.net.send(
                self.src(there * 2 + 1 - c), self.crossed.at[slot], index(z, y, x, 1 - c), "core"
            )
        )

    def steps(self):
        z, y, x, c = self.here
        net, cross = self.net, self.cross_copies
        crossed, relay, landed = self.crossed, self.relay, self.landed
        right, left = shifted(self.here, 2, 1), shifted(self.here, 2, -1)
        held = [self.src((x + step) % 4 * 2 + c) for step in self.ORDER]
        part = [
            [self.src((x + step) % 4 * 2 + c, half) for half in (0, 1)] for step in self.ORDER
        ]
        half = relay.shape[1]
        upper, lower = pl.ds(0, half), pl.ds(half, half)
        yield [cross[0]]
        cross[0].wait_recv()
        add_into(held[0], crossed.at[0])
        net.spend(1.0)
        one = net.send(part[0][0], relay.at[0], right, (2, 1))
        two = net.send(part[0][1], relay.at[1], left, (2, -1))
        yield [cross[1]]
        cross[1].wait_recv()
        add_into(held[1], crossed.at[1])
        net.spend(1.0)
        three = net.send(part[1][1], landed.at[0, lower], right, (2, 1))
        yield [cross[2]]
        cross[2].wait_recv()
        add_into(held[2], crossed.at[2])
        net.spend(1.0)
        four = net.send(part[2][0], landed.at[1, upper], left, (2, -1))
        yield [one]
        one.wait_recv()
        add_into(part[1][0], relay.at[0])
        net.spend(0.5)
        five = net.send(part[1][0], landed.at[0, upper], right, (2, 1))
        yield [two]
        two.wait_recv()
        add_into(part[2][1], relay.at[1])
        net.spend(0.5)
        six = net.send(part[2][1], landed.at[1, lower], left, (2, -1))
        yield [cross[3]]
        cross[3].wait_recv()
        add_into(held[3], crossed.at[3])
        net.spend(1.0)
        yield [three, four, five, six]
        for copy in (three, four, five, six):
            copy.wait_recv()
        add_up(self.out, held[3], landed.at[0], landed.at[1], *self.extra)
        net.spend(1.0)


def plane_reduce_scratch(rows, cols):
    return [
        pltpu.VMEM((2, 4, rows, cols), BF16),
        pltpu.VMEM((2, 2, 4, rows, cols), BF16),
        pltpu.VMEM((2, rows, cols), BF16),
        pltpu.VMEM((2, 2, rows, cols), BF16),
    ]


def plane_reduce(net, here, region, half, out, scratch):
    relay, landed, relay_two, landed_two = scratch
    axis, other = (0, 1) if half == 0 else (1, 0)

    def at(position, part, second=None):
        spots = (position, second) if half == 0 else (second, position)
        return region(*spots, half, part)

    spot = here[axis]
    up, down = shifted(here, axis, 1), shifted(here, axis, -1)
    after, before, far = (spot + 1) % 4, (spot + 3) % 4, (spot + 2) % 4
    one = net.send(at(far, 0), relay.at[0], up, (axis, 1))
    two = net.send(at(far, 1), relay.at[1], down, (axis, -1))
    three = net.send(at(after, 1), landed.at[0, 1], up, (axis, 1))
    four = net.send(at(before, 0), landed.at[1, 0], down, (axis, -1))
    cost = math.prod(relay.shape[1:]) / 250000
    yield [one]
    one.wait_recv()
    add_into(at(after, 0), relay.at[0])
    net.spend(cost)
    five = net.send(at(after, 0), landed.at[0, 0], up, (axis, 1))
    yield [two]
    two.wait_recv()
    add_into(at(before, 1), relay.at[1])
    net.spend(cost)
    six = net.send(at(before, 1), landed.at[1, 1], down, (axis, -1))
    yield [four, five]
    four.wait_recv()
    five.wait_recv()
    add_up(at(spot, 0), at(spot, 0), landed.at[0, 0], landed.at[1, 0])
    net.spend(cost)
    place_two = here[other]
    up, down = shifted(here, other, 1), shifted(here, other, -1)
    after, before, far = (place_two + 1) % 4, (place_two + 3) % 4, (place_two + 2) % 4
    seven = net.send(at(spot, 0, far), relay_two.at[0], up, (other, 1))
    eight = net.send(at(spot, 0, before), landed_two.at[1, 0], down, (other, -1))
    yield [three, six]
    three.wait_recv()
    six.wait_recv()
    add_up(at(spot, 1), at(spot, 1), landed.at[0, 1], landed.at[1, 1])
    net.spend(cost)
    nine = net.send(at(spot, 1, far), relay_two.at[1], down, (other, -1))
    ten = net.send(at(spot, 1, after), landed_two.at[0, 1], up, (other, 1))
    yield [seven]
    seven.wait_recv()
    add_into(at(spot, 0, after), relay_two.at[0])
    net.spend(cost / 4)
    eleven = net.send(at(spot, 0, after), landed_two.at[0, 0], up, (other, 1))
    yield [nine]
    nine.wait_recv()
    add_into(at(spot, 1, before), relay_two.at[1])
    net.spend(cost / 4)
    twelve = net.send(at(spot, 1, before), landed_two.at[1, 1], down, (other, -1))
    yield [eight, eleven]
    eight.wait_recv()
    eleven.wait_recv()
    add_up(out(0), at(spot, 0, place_two), landed_two.at[0, 0], landed_two.at[1, 0])
    net.spend(cost / 4)
    yield [ten, twelve]
    ten.wait_recv()
    twelve.wait_recv()
    add_up(out(1), at(spot, 1, place_two), landed_two.at[0, 1], landed_two.at[1, 1])
    net.spend(cost / 4)


def by_rows(ref, rows, cols):
    def region(z, y, half, part):
        size = rows // 2 if part is None else rows // 4
        start = half * (rows // 2) + (0 if part is None else part * (rows // 4))
        return ref.at[
            slice(None) if z is None else z, slice(None) if y is None else y, pl.ds(start, size), cols
        ]

    return region


def by_cols(ref, cols):
    def region(z, y, half, part):
        size = cols // 2 if part is None else cols // 4
        start = half * (cols // 2) + (0 if part is None else part * (cols // 4))
        return ref.at[
            slice(None) if z is None else z, slice(None) if y is None else y, :, pl.ds(start, size)
        ]

    return region


def row_block(ref, rows):
    def at(g, part=None):
        size = rows if part is None else rows // 2
        start = g * rows + (0 if part is None else part * (rows // 2))
        return ref.at[pl.ds(pl.multiple_of(start, rows // 2), size)]

    return at


def col_block(ref, rows, cols, first=0):
    def at(g, part=None):
        size = rows if part is None else rows // 2
        start = first + (0 if part is None else part * (rows // 2))
        return ref.at[pl.ds(start, size), pl.ds(pl.multiple_of(g * cols, cols), cols)]

    return at


def halves(ref, rows, first=0):
    def own(part):
        size = rows if part is None else rows // 2
        return ref.at[pl.ds(first + (0 if part is None else part * (rows // 2)), size)]

    return own


def ring_partners(here, axes):
    return [shifted(here, axis, step) for axis in axes for step in (1, -1)]


def core_peer(here):
    return index(here[0], here[1], here[2], 1 - here[3])


def communicate(kernel, collective_id, outs, scratch, n_sends, n_moves, name, inside=()):
    def call(*args):
        def body(*refs):
            n_in, n_out = len(args), len(outs)
            send_sem, recv_sem, local_sem = refs[-3:]
            net = Net(send_sem, recv_sem, local_sem)
            kernel(net, place(), refs[:n_in], refs[n_in : n_in + n_out], refs[n_in + n_out : -3])
            net.finish()

        return pl.pallas_call(
            body,
            out_shape=[jax.ShapeDtypeStruct(shape, dtype) for shape, dtype, _ in outs],
            in_specs=[VMEM if i in inside else ANY for i in range(len(args))],
            out_specs=[VMEM if near else ANY for _, _, near in outs],
            scratch_shapes=list(scratch)
            + [
                pltpu.SemaphoreType.DMA((n_sends,)),
                pltpu.SemaphoreType.DMA((n_sends,)),
                pltpu.SemaphoreType.DMA((max(n_moves, 1),)),
            ],
            compiler_params=pltpu.CompilerParams(
                collective_id=collective_id, has_side_effects=True, vmem_limit_bytes=60 << 20
            ),
            name=name,
        )(*args)

    return call


def chunk(i, size):
    return pl.ds(pl.multiple_of(i * size, size), size)


def loop(count, work):
    def body(i, carry):
        work(i)
        return carry

    lax.fori_loop(0, count, body, 0)


def lanes(shape):
    return lax.broadcasted_iota(jnp.int32, shape, 1)


def tables(aux):
    lane = lanes(aux.shape)
    by = [aux] + [pltpu.roll(aux, 32 * k, 1) for k in (1, 2, 3)]
    cosine = jnp.where(lane < 32, by[0], jnp.where(lane < 64, by[1], jnp.where(lane < 96, by[2], by[3])))
    sine = jnp.where(lane < 32, by[3], jnp.where(lane < 64, by[0], jnp.where(lane < 96, by[1], by[2])))
    sine = jnp.where(lane % 64 < 32, -sine, sine)
    begin = jnp.where(lane < 64, by[2], by[0])
    return cosine, sine, begin


def turn(values, cosine, sine):
    width = values.shape[1]
    if width > 128:
        cosine, sine = (jnp.concatenate([t] * (width // 128), axis=1) for t in (cosine, sine))
    partner = jnp.where(
        lanes(values.shape) % 64 < 32,
        pltpu.roll(values, width - 32, 1),
        pltpu.roll(values, 32, 1),
    )
    return values * cosine + partner * sine


def allowed_keys(begin):
    key = lanes(begin.shape).astype(F32)
    query = lax.broadcasted_iota(jnp.int32, begin.shape, 0).astype(F32)
    return (key >= begin) & (key <= query)


def doubled(keyed):
    lane, other = lanes(keyed.shape), pltpu.roll(keyed, 64, 1)
    keys = jnp.where(lane < 64, keyed, other).astype(BF16)
    values = jnp.where(lane < 64, other, keyed).astype(BF16)
    return keys, values


def only_half(pair, side):
    lane = lanes(pair.shape)
    keep = lane < 64 if side == 0 else lane >= 64
    return jnp.where(keep, pair, jnp.zeros_like(pair))


def probabilities(query, keys, allowed):
    scores = jnp.where(allowed, dot_last(query, keys) * SCALE, MASKED)
    powers = jnp.exp(scores - jnp.max(scores, axis=-1, keepdims=True))
    return powers / jnp.sum(powers, axis=-1, keepdims=True)


def rows_of(ref):
    return lambda g: ref.at[pl.ds(pl.multiple_of(g * 16, 16), 16)]


def pack_keyed(w_key, w_value, out):
    for x in range(KV_HEADS):
        tile = pl.ds(x // 2 * 128, 128)
        key, value = w_key[:, tile].astype(F32), w_value[:, tile].astype(F32)
        if x % 2 == 0:
            value = pltpu.roll(value, 64, 1)
        else:
            key = pltpu.roll(key, 64, 1)
        out(x, jnp.where(lanes(key.shape) < 64, key, value).astype(BF16))


def pack_feed(w, out, whole, part):
    whole[...] = w[...].astype(F32)
    part[...] = jnp.zeros_like(part)
    for g in range(GROUP):
        for spot in range(16):
            start = (spot * GROUP + g) * FF_ROWS
            part[:, spot * FF_PAD : spot * FF_PAD + FF_ROWS] = whole[:, start : start + FF_ROWS]
        out(g, part[...].astype(BF16))


def layer(net, here, inputs, outputs, scratch):
    tokens, aux, meta, upstream, w_query, w_key, w_value, w_out, w_gate, w_up, w_down = inputs
    qkv_w_out, out_w_out, normed_out, qkv_out, attended_out, residual_out, grad_gate, grad_up = outputs[:8]
    all_aux, all_meta, grad_out, mixed_out, down_out = outputs[8:]
    (
        all_tokens,
        normed,
        attended,
        residual,
        all_upstream,
        packed_one,
        packed_two,
        own_one,
        own_two,
        own_down,
        own_residual,
        qkv_w,
        out_w,
        gate_w,
        up_w,
        narrow,
        linear,
        qkv,
        mine_attended,
        mine_residual,
        gate,
        up,
        active,
        grad_down,
        seen,
        mine_meta,
        gain,
        whole,
        part,
    ) = scratch[:29]
    rest = scratch[29:]
    mixed_part, grad_part, normed_two = all_tokens, residual, normed
    z, y, x, c = here
    mine = x * 2 + c
    greet([device for _, device in group_peers(here)] + [device for _, device in plane_peers(here)])

    def small():
        copies = [net.send(meta, seen.at[mine], device) for _, device in group_peers(here)]
        kept = net.move(meta, seen.at[mine])
        yield [*copies, kept]
        for copy in copies:
            copy.wait_recv()
        kept.wait()
        mine_meta[...] = jnp.sum(seen[...], axis=0)
        spots = all_meta.at[z * 4 + y]
        copies = [net.send(mine_meta, spots, device) for _, device in plane_peers(here)]
        all_meta[z * 4 + y] = mine_meta[...]
        net.spend(1.0)
        yield copies
        for copy in copies:
            copy.wait_recv()
        for spot in range(16):
            gain[:, pl.ds(spot * 128, 128)] = all_meta[spot]

    parts = [
        (by_rows(out_w, TOK, slice(None)), half_rows(own_two, pl.ds(0, COLS))),
        (by_rows(gate_w, TOK, slice(None)), half_rows(own_two, pl.ds(COLS, FF_COLS))),
        (by_rows(up_w, TOK, slice(None)), half_rows(own_two, pl.ds(COLS + FF_COLS, FF_COLS))),
        (by_cols(narrow, D), half_cols(own_down, D)),
    ]
    tasks = {}

    def gather_part(i):
        region, source = parts[i]
        for half in (0, 1):
            follow = functools.partial(gather_part, i + 1) if half == 1 and i + 1 < len(parts) else None
            tasks[i, half] = net.start(plane_gather(net, here, region, half, source, follow), slack=SLACK)

    def exchange_one():
        def put(x, value):
            packed_one[2 * x, :, COLS:] = value
            packed_one[2 * x + 1, :, COLS:] = value

        pack_keyed(w_key, w_value, put)
        for g in range(GROUP):
            packed_one[g, :, :COLS] = w_query[:, g * COLS : (g + 1) * COLS]
        yield from group_exchange(net, here, lambda g: packed_one.at[g], rows_of(own_one))
        region, source = by_rows(qkv_w, TOK, slice(None)), half_rows(own_one, slice(None))
        for half in (0, 1):
            tasks["qkv", half] = net.start(plane_gather_direct(net, here, region, half, source))

    def exchange_two():
        for g in range(GROUP):
            packed_two[g, :, :COLS] = w_out[:, g * COLS : (g + 1) * COLS]

        def put(start):
            def store(g, value):
                packed_two[g, :, start : start + FF_COLS] = value

            return store

        full = FF_ROWS // 16 * 16
        own_down[:full] = w_down[:full]
        tail = jnp.concatenate([w_down[full:].astype(F32), jnp.zeros((FF_PAD - FF_ROWS, D), F32)], axis=0)
        own_down[full:] = tail.astype(BF16)
        pack_feed(w_gate, put(COLS), whole, part)
        pack_feed(w_up, put(COLS + FF_COLS), whole, part)
        net.spend(3.0)
        yield [exchanged]
        yield from group_exchange(net, here, lambda g: packed_two.at[g], rows_of(own_two))
        gather_part(0)

    def attend(i):
        rows = chunk(i, TOK)
        cosine, sine, begin = tables(all_aux[rows])
        allowed = allowed_keys(begin)
        local = chunk(i % (size // TOK), TOK)
        turned = turn(linear[local, :COLS], cosine, sine).astype(BF16)
        keyed = linear[local, COLS:]
        keyed = jnp.where(lanes(keyed.shape) < 64, turn(keyed, cosine, sine), keyed)
        keys, values = doubled(keyed)
        qkv[rows, :COLS] = turned
        qkv[rows, COLS:] = keyed.astype(BF16)
        for pair in range(MY_HEADS // 2):
            both = turned[:, pair * 128 : pair * 128 + 128]
            sides = []
            for side in (0, 1):
                probs = probabilities(only_half(both, side), keys, allowed)
                sides.append(matmul(probs.astype(BF16), values))
            out = jnp.where(lanes(sides[0].shape) < 64, sides[0], sides[1])
            mine_attended[rows, pair * 128 : pair * 128 + 128] = out.astype(BF16)

    def normalise(source, target, row, strip):
        values = source[strip].astype(F32)
        scale = lax.rsqrt(jnp.mean(values * values, axis=-1, keepdims=True) + EPSILON)
        target[strip] = (values * scale * gain[row : row + 1]).astype(BF16)

    def expand(i):
        rows = chunk(i, size)
        for j in range(FF_COLS // 256):
            cols = pl.ds(j * 256, 256)
            gate_val = matmul(normed_two[rows], gate_w[:, :, :, cols].reshape(D, 256))
            up_val = matmul(normed_two[rows], up_w[:, :, :, cols].reshape(D, 256))
            sigmoid_gate = 1.0 / (1.0 + jnp.exp(-gate_val))
            silu_gate = gate_val * sigmoid_gate
            active[rows, cols] = (silu_gate * up_val).astype(BF16)
            gate[rows, cols] = silu_gate.astype(BF16)
            up[rows, cols] = (
                up_val * sigmoid_gate * (1.0 + gate_val * (1.0 - sigmoid_gate))
            ).astype(BF16)

    def shrink_back(i):
        rows = chunk(i, size)
        for j in range(2):
            cols = pl.ds(j * 384, 384)
            down_rows = narrow[2 * j : 2 * j + 2].reshape(384, D)
            grad_active = dot_last(all_upstream[rows], down_rows)
            gate[rows, cols] = (grad_active * gate[rows, cols].astype(F32)).astype(BF16)
            up[rows, cols] = (grad_active * up[rows, cols].astype(F32)).astype(BF16)

    def down_gradient(j):
        cols = chunk(j, 256)
        for p in range(2):
            grad = dot_first(active[:, pl.ds(p * 384, 384)], all_upstream[:, cols])
            grad_down[2 * p : 2 * p + 2, :, :, cols] = grad.astype(BF16).reshape(2, 4, FF_PAD, 256)

    def feed_gradient(m):
        columns = normed_two[:, chunk(m, 256)]
        spots = pl.ds(m % 2 * 2, 2)
        gate_w[m // 2, spots] = dot_first(columns, up[...]).astype(BF16).reshape(2, TOK, FF_COLS)
        up_w[m // 2, spots] = dot_first(columns, gate[...]).astype(BF16).reshape(2, TOK, FF_COLS)

    pieces = 4
    size = TOKENS // pieces
    quarter = D // 4

    def narrow_part(half):
        return lambda part: down_out.at[:, pl.ds((half * 2 + part) * quarter, quarter)]

    def gathered(i):
        while (i, 1) not in tasks:
            yield [tasks[i - 1, 1]]
        yield [tasks[i, 0], tasks[i, 1]]

    def work():
        yield [gains, took]
        strips(TOKENS, functools.partial(normalise, all_tokens, normed, 0), together=4)
        net.spend(4.0)
        normed_copy = net.move(normed, normed_out)
        yield [exchanged, placed]
        yield [tasks["qkv", 0], tasks["qkv", 1]]
        net.leave(qkv_w, qkv_w_out)
        sent = []
        for i in range(pieces):
            rows = pl.ds(i * size, size)
            linear[...] = matmul(normed[rows], qkv_w[...].reshape(D, QKV))
            loop(size // TOK, lambda j, i=i: attend(j + i * (size // TOK)))
            net.spend(3.0)
            at = col_block(attended, size, COLS, i * size)
            sent.append(net.start(group_gather(net, here, halves(mine_attended, size, i * size), at)))
            yield []
        net.leave(qkv, qkv_out)
        my_cols = pl.ds(pl.multiple_of(mine * COLS, COLS), COLS)
        yield [other]
        yield from gathered(0)
        net.leave(out_w, out_w_out)
        last = []
        for i in range(pieces):
            yield [sent[i]]
            rows = pl.ds(i * size, size)
            out = matmul(attended[rows], out_w[...].reshape(D, COLS))
            mine_residual[rows] = (all_tokens[rows, my_cols].astype(F32) + out).astype(BF16)
            net.spend(0.8)
            at = col_block(residual, size, COLS, i * size)
            last.append(net.start(group_gather(net, here, halves(mine_residual, size, i * size), at)))
            yield []
        late = net.start(group_gather(net, here, halves(upstream, TOK), row_block(all_upstream, TOK)))
        yield []
        net.leave(attended, attended_out)
        normed_copy.wait()
        for i in (1, 2):
            yield from gathered(i)
        for i in range(pieces):
            yield [last[i]]

            def norm(strip, i=i):
                start = pl.multiple_of(i * size + strip.start, 16)
                normalise(residual, normed_two, 1, pl.ds(start, 16))

            strips(size, norm, together=4)
            expand(i)
            net.spend(4.3)
            yield []
        own_copy = net.move(row_block(residual, TOK)(mine), own_residual)
        net.flush([took])
        yield from gathered(3)
        own_copy.wait()
        net.leave(own_residual, residual_out)
        mix = GroupReduce(net, here, row_block(mixed_part, TOK), mixed_out, rest[0:3], [own_residual])
        for slot, step in enumerate(GroupReduce.ORDER):
            there = chunk((x + step) % 4, size)

            def mixed(j):
                cols = chunk(j, 512)
                out = matmul(active[there], narrow[:, :, :, cols].reshape(FF_COLS, 512))
                mixed_part[there, cols] = out.astype(BF16)

            loop(D // 512, mixed)
            net.spend(1.3)
            mix.cross(slot)
            yield []
        net.start(mix.steps())
        yield [late]
        for i in range(pieces):
            shrink_back(i)
            net.spend(2.0)
            yield []
        net.flush(last)
        back = GroupReduce(net, here, row_block(grad_part, TOK), grad_out, rest[3:6])
        for slot, step in enumerate(GroupReduce.ORDER):
            there = chunk((x + step) % 4, size)

            def to_input(j):
                total = dot_last(up[there], gate_w[j].reshape(512, FF_COLS))
                total = total + dot_last(gate[there], up_w[j].reshape(512, FF_COLS))
                grad_part[there, chunk(j, 512)] = total.astype(BF16)

            loop(D // 512, to_input)
            net.spend(2.3)
            back.cross(slot)
            yield []
        net.start(back.steps())
        loop(4, down_gradient)
        net.spend(2.3)
        yield []
        loop(4, lambda j: down_gradient(j + 4))
        net.spend(2.3)
        region = by_cols(grad_down, D)
        for half in (0, 1):
            room = rest[6 + 4 * half : 10 + 4 * half]
            net.start(plane_reduce(net, here, region, half, narrow_part(half), room), slack=SLACK)
        yield []
        net.flush([tasks[i, half] for i in (1, 2) for half in (0, 1)])
        for m in range(8):
            feed_gradient(m)
            net.spend(1.3)
            yield []
            if m % 2 == 1:
                net.leave(gate_w.at[m // 2], grad_gate.at[m // 2])
                net.leave(up_w.at[m // 2], grad_up.at[m // 2])

    exchanged = net.start(exchange_one())
    gains = net.start(small())
    took = net.start(group_gather(net, here, halves(tokens, TOK), row_block(all_tokens, TOK)))
    placed = net.start(group_gather(net, here, halves(aux, TOK), row_block(all_aux, TOK)))
    other = net.start(exchange_two())
    net.start(work(), rank=1)
    run(net)


def layer_call(*args):
    outs = [
        ((4, 4, TOK, QKV), BF16, False),
        ((4, 4, TOK, COLS), BF16, False),
        ((TOKENS, D), BF16, False),
        ((TOKENS, QKV), BF16, False),
        ((TOKENS, D), BF16, False),
        ((TOK, D), BF16, False),
        ((4, 4, TOK, FF_COLS), BF16, False),
        ((4, 4, TOK, FF_COLS), BF16, False),
        ((TOKENS, 128), F32, True),
        ((16, 8, 128), F32, True),
        ((TOK, D), F32, True),
        ((TOK, D), BF16, True),
        ((FF_PAD, D), F32, True),
    ]
    scratch = [pltpu.VMEM((TOKENS, D), BF16)] * 5 + [
        pltpu.VMEM((GROUP, 16, QKV), BF16),
        pltpu.VMEM((GROUP, 16, COLS + 2 * FF_COLS), BF16),
        pltpu.VMEM((TOK, QKV), BF16),
        pltpu.VMEM((TOK, COLS + 2 * FF_COLS), BF16),
        pltpu.VMEM((FF_PAD, D), BF16),
        pltpu.VMEM((TOK, D), BF16),
        pltpu.VMEM((4, 4, TOK, QKV), BF16),
        pltpu.VMEM((4, 4, TOK, COLS), BF16),
        pltpu.VMEM((4, 4, TOK, FF_COLS), BF16),
        pltpu.VMEM((4, 4, TOK, FF_COLS), BF16),
        pltpu.VMEM((4, 4, FF_PAD, D), BF16),
        pltpu.VMEM((TOKENS // 4, QKV), F32),
        pltpu.VMEM((TOKENS, QKV), BF16),
        pltpu.VMEM((TOKENS, COLS), BF16),
        pltpu.VMEM((TOKENS, COLS), BF16),
        pltpu.VMEM((TOKENS, FF_COLS), BF16),
        pltpu.VMEM((TOKENS, FF_COLS), BF16),
        pltpu.VMEM((TOKENS, FF_COLS), BF16),
        pltpu.VMEM((4, 4, FF_PAD, D), BF16),
        pltpu.VMEM((8, 8, 128), F32),
        pltpu.VMEM((8, 128), F32),
        pltpu.VMEM((8, D), F32),
        pltpu.VMEM((16, 16 * GROUP * FF_ROWS), F32),
        pltpu.VMEM((16, FF_COLS), F32),
    ]
    scratch += group_reduce_scratch(TOK, D) * 2 + plane_reduce_scratch(FF_PAD, D // 4) * 2
    return communicate(layer, 0, outs, scratch, 400, 60, "layer", inside=range(4, 11))(*args)


def quarter_rows(ref):
    return lambda half: lambda part: ref.at[pl.ds((half * 2 + part) * (TOK // 4), TOK // 4)]


def backward(net, here, inputs, outputs, scratch):
    (
        grad_normed_two,
        all_residual,
        upstream,
        tokens,
        all_meta,
        all_aux,
        qkv_in,
        qkv_w_in,
        out_w_in,
        normed_in,
        attended_in,
        gate_in,
        up_in,
        w_query,
        w_key,
        w_value,
        w_gate,
        w_up,
    ) = inputs
    grad_tokens, norms_out, grad_query, grad_key, grad_value, grad_out, grad_gate_out, grad_up_out = outputs
    (
        grad_two,
        residual,
        own_upstream,
        own_tokens,
        grad_residual,
        grad_rounded,
        gains,
        grad_cols,
        qkv_w,
        out_w,
        heads_part,
        heads,
        qkv,
        grad_lin,
        normed,
        attended,
        input_part,
        grad_one,
        grad_gate,
        grad_up,
        grad_qkv_w,
        grad_out_w,
        gate_sum,
        up_sum,
        qkv_sum,
        out_sum,
        gate_rows,
        up_rows,
        qkv_rows,
        out_rows,
        part,
    ) = scratch[:31]
    rest = scratch[31:]
    z, y, x, c = here
    mine = x * 2 + c
    loads = {
        "grad_two": net.move(grad_normed_two, grad_two),
        "residual": net.move(all_residual, residual),
        "upstream": net.move(upstream, own_upstream),
        "gate": net.move(gate_in, grad_gate),
        "out_w": net.move(out_w_in, out_w),
        "qkv_w": net.move(qkv_w_in, qkv_w),
        "up": net.move(up_in, grad_up),
        "qkv": net.move(qkv_in, qkv),
        "attended": net.move(attended_in, attended),
        "normed": net.move(normed_in, normed),
        "tokens": net.move(tokens, own_tokens),
    }
    greet([device for _, device in group_peers(here)] + ring_partners(here, (0, 1)))

    def unpack_feed(rows, out, w, column):
        def finish():
            for g in range(GROUP):
                part[...] = rows[g].astype(F32)
                for spot in range(16):
                    start = (spot * GROUP + g) * FF_ROWS
                    out[:, start : start + FF_ROWS] = part[:, spot * FF_PAD : spot * FF_PAD + FF_ROWS]
            add_norm(column, [(out, w)])
            net.spend(2.0)

        return finish

    def add_norm(column, pairs):
        total = sum(
            jnp.sum(grad[...] * w[...].astype(F32), axis=-1, keepdims=True) for grad, w in pairs
        )
        norms_out[...] += jnp.where(lanes((16, 128)) == column, total, 0.0)

    def unpack_qkv():
        for g in range(GROUP):
            grad_query[:, g * COLS : (g + 1) * COLS] = qkv_rows[g, :, :COLS].astype(F32)
        keyed = [
            qkv_rows[2 * i, :, COLS:].astype(F32) + qkv_rows[2 * i + 1, :, COLS:].astype(F32)
            for i in range(KV_HEADS)
        ]
        lane = lanes(keyed[0].shape)
        for i in range(KV_HEADS // 2):
            first, second = keyed[2 * i], keyed[2 * i + 1]
            cols = pl.ds(i * 128, 128)
            grad_key[:, cols] = jnp.where(lane < 64, first, pltpu.roll(second, 64, 1))
            grad_value[:, cols] = jnp.where(lane < 64, pltpu.roll(first, 64, 1), second)
        add_norm(0, [(grad_query, w_query), (grad_key, w_key), (grad_value, w_value)])

    def unpack_out():
        for g in range(GROUP):
            grad_out[:, g * COLS : (g + 1) * COLS] = out_rows[g].astype(F32)

    def feed_gradients():
        for name, source, total, rows, room, out, w in (
            ("gate", grad_gate, gate_sum, gate_rows, rest[0:8], grad_gate_out, w_gate),
            ("up", grad_up, up_sum, up_rows, rest[8:16], grad_up_out, w_up),
        ):
            yield [loads[name]]
            loads[name].wait()
            yield [give_back(source, total, rows, room, unpack_feed(rows, out, w, 1))]

    def give_back(source, total, rows, room, unpack):
        region, part = by_rows(source, TOK, slice(None)), quarter_rows(total)
        tasks = [
            net.start(plane_reduce(net, here, region, half, part(half), room[4 * half : 4 * half + 4]), slack=SLACK)
            for half in (0, 1)
        ]

        def hand_out():
            yield tasks
            yield from group_exchange(net, here, rows_of(total), lambda g: rows.at[g])
            unpack()

        net.start(hand_out())
        return tasks[1]

    def residual_back(strip):
        values = residual[strip].astype(F32)
        scale = lax.rsqrt(jnp.mean(values * values, axis=-1, keepdims=True) + EPSILON)
        unit = values * scale
        grad = grad_two[strip]
        grad = grad * gains[1:2]
        grad = scale * (grad - unit * jnp.mean(grad * unit, axis=-1, keepdims=True))
        grad = own_upstream[strip].astype(F32) + grad
        grad_residual[strip] = grad
        grad_rounded[strip] = grad.astype(BF16)

    def input_back(strip):
        values = own_tokens[strip].astype(F32)
        scale = lax.rsqrt(jnp.mean(values * values, axis=-1, keepdims=True) + EPSILON)
        unit = values * scale
        grad = grad_one[strip]
        grad = grad * gains[0:1]
        grad = scale * (grad - unit * jnp.mean(grad * unit, axis=-1, keepdims=True))
        grad_tokens[strip] = grad_residual[strip] + grad

    def attend_back(i):
        rows = chunk(i, TOK)
        cosine, sine, begin = tables(all_aux[rows])
        allowed = allowed_keys(begin)
        keys, values = doubled(qkv[rows, COLS:].astype(F32))
        grad_queries = []
        grad_keys = jnp.zeros((TOK, 128), F32)
        grad_values = jnp.zeros((TOK, 128), F32)
        for pair in range(MY_HEADS // 2):
            cols = pl.ds(pair * 128, 128)
            queries, grads = qkv[rows, cols], heads[rows, cols]
            sides = []
            for side in (0, 1):
                query, grad = only_half(queries, side), only_half(grads, side)
                probs = probabilities(query, keys, allowed)
                grad_probs = dot_last(grad, values)
                grad_scores = probs * (grad_probs - jnp.sum(probs * grad_probs, axis=-1, keepdims=True))
                grad_scores = grad_scores.astype(BF16)
                sides.append(matmul(grad_scores, keys))
                grad_keys = grad_keys + dot_first(grad_scores, query)
                grad_values = grad_values + dot_first(probs.astype(BF16), grad)
            grad_queries.append(jnp.where(lanes(sides[0].shape) < 64, sides[0], sides[1]))
        grad_query = jnp.concatenate(grad_queries, axis=1) * SCALE
        grad_lin[rows, :COLS] = turn(grad_query, cosine, -sine).astype(BF16)
        grad_keys = turn((grad_keys + pltpu.roll(grad_keys, 64, 1)) * SCALE, cosine, -sine)
        grad_values = grad_values + pltpu.roll(grad_values, 64, 1)
        grad_lin[rows, COLS:] = jnp.where(lanes(grad_keys.shape) < 64, grad_keys, grad_values).astype(BF16)

    half_tokens = TOKENS // 2

    def work():
        for name in ("grad_two", "residual", "upstream"):
            loads[name].wait()
        for spot in range(16):
            gains[:, pl.ds(spot * 128, 128)] = all_meta[spot]
        norms_out[...] = jnp.zeros_like(norms_out)
        strips(TOK, residual_back, together=2)
        net.spend(2.0)
        spread = net.start(
            group_exchange(net, here, col_block(grad_rounded, TOK, COLS), row_block(grad_cols, TOK))
        )
        yield []
        loads["out_w"].wait()
        yield [spread]
        reduced = []
        for half in (0, 1):
            first = half * half_tokens
            rows = pl.ds(first, half_tokens)
            room = rest[24 + 3 * half : 27 + 3 * half]
            reduce = GroupReduce(
                net, here, col_block(heads_part, half_tokens, COLS, first), heads.at[rows], room
            )
            for slot, step in enumerate(GroupReduce.ORDER):
                cols = chunk((x + step) % 4, 2 * COLS)
                part = dot_last(grad_cols[rows], out_w[cols])
                heads_part[rows, cols] = part.astype(BF16)
                net.spend(0.6)
                reduce.cross(slot)
            reduced.append(net.start(reduce.steps()))
        yield []
        loads["attended"].wait()

        def out_gradient(m):
            part = dot_first(attended[:, chunk(m, 256)], grad_cols[...]).astype(BF16)
            grad_out_w[m // 2, pl.ds(m % 2 * 2, 2)] = part.reshape(2, TOK, COLS)

        for half in (0, 1):
            loop(4, lambda m, half=half: out_gradient(m + 4 * half))
            net.spend(2.3)
            yield []
        give_back(grad_out_w, out_sum, out_rows, rest[33:41], unpack_out)
        loads["qkv"].wait()
        loads["qkv_w"].wait()
        for half in (0, 1):
            yield [reduced[half]]
            loop(4, lambda i, half=half: attend_back(i + 4 * half))
            net.spend(6.0)
        reduce = GroupReduce(net, here, row_block(input_part, TOK), grad_one, rest[30:33])
        for slot, step in enumerate(GroupReduce.ORDER):
            there = chunk((x + step) % 4, 256)

            def to_input(j):
                cols = chunk(j, 512)
                part = dot_last(grad_lin[there], qkv_w[cols])
                input_part[there, cols] = part.astype(BF16)

            loop(D // 512, to_input)
            net.spend(1.3)
            reduce.cross(slot)
            yield []
        reduced = net.start(reduce.steps())
        loads["normed"].wait()

        def in_gradient(m):
            part = dot_first(normed[:, chunk(m, 256)], grad_lin[...]).astype(BF16)
            grad_qkv_w[m // 2, pl.ds(m % 2 * 2, 2)] = part.reshape(2, TOK, QKV)

        loop(8, in_gradient)
        net.spend(3.5)
        give_back(grad_qkv_w, qkv_sum, qkv_rows, rest[16:24], unpack_qkv)
        loads["tokens"].wait()
        yield [reduced]
        strips(TOK, input_back, together=2)
        net.spend(2.0)

    net.start(feed_gradients())
    net.start(work(), rank=1)
    run(net)


def backward_call(*args):
    outs = [
        ((TOK, D), F32, True),
        ((16, 128), F32, True),
        ((16, D), F32, True),
        ((16, KV_HEADS * HEAD), F32, True),
        ((16, KV_HEADS * HEAD), F32, True),
        ((16, D), F32, True),
        ((16, 16 * GROUP * FF_ROWS), F32, True),
        ((16, 16 * GROUP * FF_ROWS), F32, True),
    ]
    scratch = [
        pltpu.VMEM((TOK, D), F32),
        pltpu.VMEM((TOK, D), BF16),
        pltpu.VMEM((TOK, D), BF16),
        pltpu.VMEM((TOK, D), BF16),
        pltpu.VMEM((TOK, D), F32),
        pltpu.VMEM((TOK, D), BF16),
        pltpu.VMEM((8, D), F32),
        pltpu.VMEM((TOKENS, COLS), BF16),
        pltpu.VMEM((D, QKV), BF16),
        pltpu.VMEM((D, COLS), BF16),
        pltpu.VMEM((TOKENS, D), BF16),
        pltpu.VMEM((TOKENS, COLS), BF16),
        pltpu.VMEM((TOKENS, QKV), BF16),
        pltpu.VMEM((TOKENS, QKV), BF16),
        pltpu.VMEM((TOKENS, D), BF16),
        pltpu.VMEM((TOKENS, D), BF16),
        pltpu.VMEM((TOKENS, D), BF16),
        pltpu.VMEM((TOK, D), F32),
        pltpu.VMEM((4, 4, TOK, FF_COLS), BF16),
        pltpu.VMEM((4, 4, TOK, FF_COLS), BF16),
        pltpu.VMEM((4, 4, TOK, QKV), BF16),
        pltpu.VMEM((4, 4, TOK, COLS), BF16),
        pltpu.VMEM((TOK, FF_COLS), BF16),
        pltpu.VMEM((TOK, FF_COLS), BF16),
        pltpu.VMEM((TOK, QKV), BF16),
        pltpu.VMEM((TOK, COLS), BF16),
        pltpu.VMEM((GROUP, 16, FF_COLS), BF16),
        pltpu.VMEM((GROUP, 16, FF_COLS), BF16),
        pltpu.VMEM((GROUP, 16, QKV), BF16),
        pltpu.VMEM((GROUP, 16, COLS), BF16),
        pltpu.VMEM((16, FF_COLS), F32),
    ]
    scratch += plane_reduce_scratch(TOK // 4, FF_COLS) * 4 + plane_reduce_scratch(TOK // 4, QKV) * 2
    scratch += group_reduce_scratch(TOKENS // 2, COLS) * 2 + group_reduce_scratch(TOK, D)
    scratch += plane_reduce_scratch(TOK // 4, COLS) * 2
    return communicate(
        backward, 1, outs, scratch, 180, 60, "backward", inside=(4, 5, 13, 14, 15, 16, 17)
    )(*args)


def sequence_table(lengths):
    ends = jnp.cumsum(lengths)
    places = jnp.arange(TOK, dtype=jnp.int32)
    begins = jnp.max(jnp.where(places[:, None] >= ends[None, :], ends[None, :], 0), axis=-1)
    inverse = jnp.exp(jnp.arange(HEAD // 2, dtype=F32) * (-2.0 * math.log(THETA) / HEAD))
    angle = (places - begins).astype(F32)[:, None] * inverse[None, :]
    start = jnp.broadcast_to(begins.astype(F32)[:, None], (TOK, 64))
    return jnp.concatenate([jnp.cos(angle), jnp.sin(angle), start], axis=1)


def matmul(left, right):
    return jnp.dot(left, right, preferred_element_type=F32)


def dot_last(left, right):
    return lax.dot_general(left, right, (((1,), (1,)), ((), ())), preferred_element_type=F32)


def dot_first(left, right):
    return lax.dot_general(left, right, (((0,), (0,)), ((), ())), preferred_element_type=F32)


def hand_over(down_sum, *results):
    count = len(results)

    def body(*refs):
        sums, sources, down, targets, sem = refs[0], refs[1 : 1 + count], refs[1 + count], refs[2 + count : -1], refs[-1]
        copies = [
            pltpu.make_async_copy(source, target, sem.at[i])
            for i, (source, target) in enumerate(zip(sources, targets, strict=True))
        ]
        for copy in copies:
            copy.start()
        down[...] = sums[:FF_ROWS]
        for copy in copies:
            copy.wait()

    return pl.pallas_call(
        body,
        out_shape=[jax.ShapeDtypeStruct((FF_ROWS, D), F32)]
        + [jax.ShapeDtypeStruct(result.shape, result.dtype) for result in results],
        in_specs=[VMEM] + [ANY] * count,
        out_specs=[VMEM] + [ANY] * count,
        scratch_shapes=[pltpu.SemaphoreType.DMA((count,))],
        name="hand_over",
    )(down_sum, *results)


def on_device(
    tokens,
    seq_lengths,
    attn_norm,
    w_query,
    w_key,
    w_value,
    w_out,
    mlp_norm,
    w_gate,
    w_up,
    w_down,
    cotangent,
):
    me = lax.axis_index("dp")
    member = me % GROUP
    meta = jnp.stack([attn_norm.astype(F32), mlp_norm.astype(F32)])
    meta = lax.dynamic_update_slice(jnp.zeros((8, 128), F32), meta, (0, member * 16))
    (
        qkv_w,
        out_w,
        normed,
        qkv,
        all_attended,
        own_residual,
        grad_gate,
        grad_up,
        all_aux,
        all_meta,
        grad_normed_two,
        mixed_out,
        down_sum,
    ) = layer_call(
        tokens,
        sequence_table(seq_lengths[0]),
        meta,
        cotangent,
        w_query,
        w_key,
        w_value,
        w_out,
        w_gate,
        w_up,
        w_down,
    )
    grad_tokens, norms, grad_query, grad_key, grad_value, grad_out, grad_gate, grad_up = backward_call(
        grad_normed_two,
        own_residual,
        cotangent,
        tokens,
        all_meta,
        all_aux,
        qkv,
        qkv_w.reshape(D, QKV),
        out_w.reshape(D, COLS),
        normed,
        all_attended,
        grad_gate,
        grad_up,
        w_query,
        w_key,
        w_value,
        w_gate,
        w_up,
    )
    grad_down, mixed_out, grad_tokens, grad_query, grad_key, grad_value, grad_out, grad_gate, grad_up = hand_over(
        down_sum, mixed_out, grad_tokens, grad_query, grad_key, grad_value, grad_out, grad_gate, grad_up
    )
    return (
        mixed_out,
        grad_tokens,
        norms[:, 0] / attn_norm.astype(F32),
        grad_query,
        grad_key,
        grad_value,
        grad_out,
        norms[:, 1] / mlp_norm.astype(F32),
        grad_gate,
        grad_up,
        grad_down,
    )


def solution(mesh):
    matrix, vector = P("dp", None), P("dp")
    return jax.shard_map(
        on_device,
        mesh=mesh,
        in_specs=(
            matrix,
            matrix,
            vector,
            matrix,
            matrix,
            matrix,
            matrix,
            vector,
            matrix,
            matrix,
            matrix,
            matrix,
        ),
        out_specs=(
            matrix,
            matrix,
            vector,
            matrix,
            matrix,
            matrix,
            matrix,
            vector,
            matrix,
            matrix,
            matrix,
        ),
        check_vma=False,
    )
```
